32 devices in a mesh: shard: 2 (over x), ctx: 4 (over y, core), tp: 4 (over z).
Axes of the slice: x: 2, y: 2, z: 4, core: 2. Of those that a mesh axis runs over, the one named last changes fastest.
Arguments:
- inputs: bfloat16 [2, 2048, 2048], P('shard', 'ctx'), may hold values from -6 to 6
- lengths: int32 [2], P('shard'), may hold values from 1024 to 2048, as said below
- cotangent: bfloat16 [2, 2048, 2048], P('shard', 'ctx'), may hold values from -6 to 6
- norm1_gain: bfloat16 [2048], P(('shard', 'ctx')), may hold values from 0.099609375 to 1.8984375
- branch_weight: bfloat16 [2048, 2560], P(('shard', 'ctx'), 'tp'), may hold values from -0.125 to 0.125
- rec_in_weight: bfloat16 [2048, 2560], P(('shard', 'ctx'), 'tp'), may hold values from -0.125 to 0.125
- conv_weight: bfloat16 [4, 16, 160], P(None, 'tp', ('shard', 'ctx')), may hold values from -3 to 3
- conv_bias: bfloat16 [16, 160], P('tp', ('shard', 'ctx')), may hold values from -3 to 3
- rgate_weight: bfloat16 [16, 160, 160], P('tp', ('shard', 'ctx')), may hold values from -0.5 to 0.5
- rgate_bias: bfloat16 [16, 160], P('tp', ('shard', 'ctx')), may hold values from -3 to 3
- igate_weight: bfloat16 [16, 160, 160], P('tp', ('shard', 'ctx')), may hold values from -0.5 to 0.5
- igate_bias: bfloat16 [16, 160], P('tp', ('shard', 'ctx')), may hold values from -3 to 3
- decay_param: bfloat16 [16, 160], P('tp', ('shard', 'ctx')), may hold values from 4.5 to 8.5
- out_weight: bfloat16 [2048, 2560], P(('shard', 'ctx'), 'tp'), may hold values from -0.5 to 0.5
- norm2_gain: bfloat16 [2048], P(('shard', 'ctx')), may hold values from 0.099609375 to 1.8984375
- mlp_gate_weight: bfloat16 [2048, 6144], P(('shard', 'ctx'), 'tp'), may hold values from -0.125 to 0.125
- mlp_up_weight: bfloat16 [2048, 6144], P(('shard', 'ctx'), 'tp'), may hold values from -0.125 to 0.125
- mlp_down_weight: bfloat16 [2048, 6144], P(('shard', 'ctx'), 'tp'), may hold values from -0.109375 to 0.109375
Outputs:
- output: bfloat16 [2, 2048, 2048], P('shard', 'ctx')
- input_grad: bfloat16 [2, 2048, 2048], P('shard', 'ctx')
- grad_norm1_gain: float32 [2048], P(('shard', 'ctx'))
- grad_branch_weight: float32 [2048, 2560], P(('shard', 'ctx'), 'tp')
- grad_rec_in_weight: float32 [2048, 2560], P(('shard', 'ctx'), 'tp')
- grad_conv_weight: float32 [4, 16, 160], P(None, 'tp', ('shard', 'ctx'))
- grad_conv_bias: float32 [16, 160], P('tp', ('shard', 'ctx'))
- grad_rgate_weight: float32 [16, 160, 160], P('tp', ('shard', 'ctx'))
- grad_rgate_bias: float32 [16, 160], P('tp', ('shard', 'ctx'))
- grad_igate_weight: float32 [16, 160, 160], P('tp', ('shard', 'ctx'))
- grad_igate_bias: float32 [16, 160], P('tp', ('shard', 'ctx'))
- grad_decay_param: float32 [16, 160], P('tp', ('shard', 'ctx'))
- grad_out_weight: float32 [2048, 2560], P(('shard', 'ctx'), 'tp')
- grad_norm2_gain: float32 [2048], P(('shard', 'ctx'))
- grad_mlp_gate_weight: float32 [2048, 6144], P(('shard', 'ctx'), 'tp')
- grad_mlp_up_weight: float32 [2048, 6144], P(('shard', 'ctx'), 'tp')
- grad_mlp_down_weight: float32 [2048, 6144], P(('shard', 'ctx'), 'tp')
The draws below stay inside these ranges and needn't reach their ends.
Inputs may be any that keep to these rules, and one draw needn't show every extreme that they name: `lengths`: some slot holds exactly 2048 tokens and another exactly 1024.
All inputs are finite; a program needn't handle non-finite values.
Results may differ from the reference program's by a relative error of at most 0.008.
The reference program's roundings to bfloat16 on the way count: a program that leaves them out, or rounds other values in their place, can miss the bound.
Values may be sent and summed in bfloat16 or wider, within the bound.
A program may use at most 192 MiB of HBM per device.

```python
import jax
import jax.numpy as jnp
from jax import lax

D = 2048
W = 2560
H = 16
FF = 6144
CONV = 4
BW = 160
SLOTS = 2
SLOT_LEN = 2048
MIN_LEN = 1024


def draw_lengths(key, part):
    drawn = jax.random.randint(jax.random.fold_in(key, 11), (SLOTS,), MIN_LEN, SLOT_LEN + 1)
    order = jax.random.permutation(jax.random.fold_in(key, 12), SLOTS)
    slot_ids = jnp.arange(SLOTS)
    drawn = jnp.where(slot_ids == order[0], SLOT_LEN, drawn)
    drawn = jnp.where(slot_ids == order[1], MIN_LEN, drawn)
    return drawn.astype(jnp.int32)


def shard_levels(rng, extent, shards, low, largest):
    level = 1.0
    for position, blocks in shards:
        heights = jax.random.uniform(jax.random.fold_in(jax.random.fold_in(rng, 6), position), (blocks,), jnp.float32, low / len(shards), largest / len(shards))
        level = level * jnp.repeat(jnp.exp(heights), extent[position] // blocks).reshape((-1,) + (1,) * (len(extent) - 1 - position))
    return level


def gaussian(stream_key, shape, scale, limit, shards=(), kind=jnp.bfloat16):
    loudness = shard_levels(stream_key, shape, shards, -0.22, 0.18) if shards else 1.0
    values = jax.random.normal(stream_key, shape, jnp.float32) * scale * loudness
    return jnp.minimum(jnp.maximum(values, -limit), limit).astype(kind)


def setup_inputs(seed: int = 0) -> dict:
    seeds = jax.random.split(jax.random.key(seed), 19)
    return {
        "inputs": gaussian(seeds[0], (SLOTS, SLOT_LEN, D), 1.0, 6.0, ((0, 2), (1, 4))),
        "lengths": draw_lengths(jax.random.fold_in(seeds[18], 71), 0),
        "cotangent": gaussian(seeds[2], (SLOTS, SLOT_LEN, D), 1.0, 6.0, ((0, 2), (1, 4))),
        "norm1_gain": jnp.clip(1.0 + 0.18 * jax.random.normal(seeds[3], (D,), jnp.float32), 0.099609375, 1.8984375).astype(jnp.bfloat16),
        "branch_weight": gaussian(seeds[4], (D, W), D ** -0.5, 0.125, ((0, 8), (1, 4))),
        "rec_in_weight": gaussian(seeds[5], (D, W), D ** -0.5, 0.125, ((0, 8), (1, 4))),
        "conv_weight": gaussian(seeds[6], (CONV, H, BW), CONV ** -0.5, 3.0, ((1, 4), (2, 8))),
        "conv_bias": gaussian(seeds[7], (H, BW), 0.5, 3.0, ((0, 4), (1, 8))),
        "rgate_weight": gaussian(seeds[8], (H, BW, BW), BW ** -0.5, 0.5, ((0, 4), (1, 8))),
        "rgate_bias": gaussian(seeds[9], (H, BW), 0.5, 3.0, ((0, 4), (1, 8))),
        "igate_weight": gaussian(seeds[10], (H, BW, BW), BW ** -0.5, 0.5, ((0, 4), (1, 8))),
        "igate_bias": gaussian(seeds[11], (H, BW), 0.5, 3.0, ((0, 4), (1, 8))),
        "decay_param": jnp.clip(4.5 + 4.0 * jax.random.uniform(seeds[12], (H, BW), jnp.float32) ** shard_levels(seeds[12], (H, BW), ((0, 4), (1, 8)), -0.2, 0.2), 4.5, 8.5).astype(jnp.bfloat16),
        "out_weight": gaussian(seeds[13], (D, W), (W // 16) ** -0.5, 0.5, ((0, 8), (1, 4))),
        "norm2_gain": jnp.clip(1.0 + 0.18 * jax.random.normal(seeds[14], (D,), jnp.float32), 0.099609375, 1.8984375).astype(jnp.bfloat16),
        "mlp_gate_weight": gaussian(seeds[15], (D, FF), D ** -0.5, 0.125, ((0, 8), (1, 4))),
        "mlp_up_weight": gaussian(seeds[16], (D, FF), D ** -0.5, 0.125, ((0, 8), (1, 4))),
        "mlp_down_weight": gaussian(seeds[17], (D, FF), (FF // 2) ** -0.5, 0.109375, ((0, 8), (1, 4))),
    }


EPS = 1e-06
DECAY_SCALE = 8.0
HIGHEST = lax.Precision.HIGHEST

@jax.custom_vjp
def low(v):
    return lax.optimization_barrier(v.astype(jnp.bfloat16)).astype(jnp.float32)

@jax.custom_vjp
def low_back(v):
    return v

def low_keep(v):
    return (low(v), None)

def low_pass(kept, grad):
    return (grad,)

def back_keep(v):
    return (v, None)

def back_low(kept, grad):
    return (low(grad),)
low.defvjp(low_keep, low_pass)
low_back.defvjp(back_keep, back_low)

def affine_join(earlier, later):
    return (earlier[0] * later[0], later[0] * earlier[1] + later[1])

def norm_apply(tok_rows, gain_row):
    return tok_rows * lax.rsqrt(lax.optimization_barrier(jnp.mean(tok_rows * tok_rows, axis=-1, keepdims=True)) + EPS) * gain_row

def matmul(left_side, right_side):
    return jnp.dot(left_side, right_side, precision=HIGHEST, preferred_element_type=jnp.float32)

def slot_forward(slot_rows, live_mask, params):
    gain_one, w_branch, w_rec, conv_taps, conv_shift, w_rate, b_rate, w_entry, b_entry, decay_param, w_out, gain_two, w_gate, w_up, w_down = params
    seq_len = slot_rows.shape[0]
    normed_one = low(norm_apply(slot_rows, gain_one))
    branch_pre = low_back(matmul(normed_one, w_branch))
    rec_pre = low_back(matmul(normed_one, w_rec))
    edge_count = conv_taps.shape[0] - 1
    padded = jnp.concatenate([jnp.zeros((edge_count, rec_pre.shape[1]), jnp.float32), rec_pre], axis=0)
    flat_taps = conv_taps.reshape(conv_taps.shape[0], -1)
    conv_out = conv_shift.reshape(-1) + jnp.zeros_like(rec_pre)
    for tap_index in range(conv_taps.shape[0]):
        start_row = edge_count - tap_index
        conv_out = conv_out + flat_taps[tap_index] * padded[start_row:start_row + seq_len]
    blocks_in = conv_out.reshape(seq_len, w_rate.shape[0], w_rate.shape[1])
    gate_rate = jax.nn.sigmoid(jnp.einsum('lhi,hij->lhj', blocks_in, w_rate, precision=HIGHEST) + b_rate)
    gate_entry = jax.nn.sigmoid(jnp.einsum('lhi,hij->lhj', blocks_in, w_entry, precision=HIGHEST) + b_entry)
    log_decay = -DECAY_SCALE * gate_rate * jax.nn.softplus(-decay_param)
    decay_rows = jnp.exp(log_decay).reshape(seq_len, -1)
    drive_rows = (jnp.sqrt(-jnp.expm1(2.0 * log_decay)) * gate_entry * blocks_in).reshape(seq_len, -1)
    run_decay, run_state = lax.associative_scan(affine_join, (decay_rows, drive_rows), axis=0)
    mixed = low(jax.nn.gelu(branch_pre) * run_state)
    mixer_out = low_back(matmul(mixed, w_out.T))
    middle = slot_rows + mixer_out
    normed_two = low(norm_apply(middle, gain_two))
    gate_pre = low_back(matmul(normed_two, w_gate))
    up_pre = low_back(matmul(normed_two, w_up))
    hidden = low(jax.nn.gelu(gate_pre) * up_pre)
    mlp_out = low_back(matmul(hidden, w_down.T))
    return (middle + mlp_out) * live_mask[:, None]

def reference(inputs, lengths, cotangent, norm1_gain, branch_weight, rec_in_weight, conv_weight, conv_bias, rgate_weight, rgate_bias, igate_weight, igate_bias, decay_param, out_weight, norm2_gain, mlp_gate_weight, mlp_up_weight, mlp_down_weight):
    params = (norm1_gain.astype(jnp.float32), branch_weight.astype(jnp.float32), rec_in_weight.astype(jnp.float32), conv_weight.astype(jnp.float32), conv_bias.astype(jnp.float32), rgate_weight.astype(jnp.float32), rgate_bias.astype(jnp.float32), igate_weight.astype(jnp.float32), igate_bias.astype(jnp.float32), decay_param.astype(jnp.float32), out_weight.astype(jnp.float32), norm2_gain.astype(jnp.float32), mlp_gate_weight.astype(jnp.float32), mlp_up_weight.astype(jnp.float32), mlp_down_weight.astype(jnp.float32))
    all_rows = inputs.astype(jnp.float32)
    positions = jnp.arange(SLOT_LEN, dtype=jnp.int32)
    live_masks = (positions[None, :] < lengths.astype(jnp.int32)[:, None]).astype(jnp.float32)
    slot_step = jax.checkpoint(slot_forward)

    def whole_block(slot_data, weights):
        return lax.map(lambda pair_items: slot_step(pair_items[0], pair_items[1], weights), (slot_data, live_masks))
    result, pullback = jax.vjp(whole_block, all_rows, params)
    grad_input, grads = pullback(cotangent.astype(jnp.float32))
    return (result.astype(jnp.bfloat16), grad_input.astype(jnp.bfloat16), grads[0], grads[1], grads[2], grads[3], grads[4], grads[5], grads[6], grads[7], grads[8], grads[9], grads[10], grads[11], grads[12], grads[13], grads[14])
```

```python
import functools

import jax
import jax.numpy as jnp
from jax import lax
from jax.experimental import pallas as pl
from jax.experimental.pallas import tpu as pltpu
from jax.sharding import PartitionSpec as P

EPS = 1e-06
DECAY_SCALE = 8.0
F32 = jnp.float32
BF16 = jnp.bfloat16
MESH = pl.DeviceIdType.MESH
ANY = pl.BlockSpec(memory_space=pl.ANY)
VM = pl.BlockSpec(memory_space=pltpu.VMEM)
VMEM_LIMIT = 60 * 1024 * 1024


def dot(a, b):
    return jnp.dot(a, b, preferred_element_type=F32)


def dot_rows(a, b):
    return lax.dot_general(a, b, (((1,), (1,)), ((), ())), preferred_element_type=F32)


def dot_tokens(a, b):
    return lax.dot_general(a, b, (((0,), (0,)), ((), ())), preferred_element_type=F32)


def halves(v):
    hi = v.astype(BF16)
    return hi, (v - hi.astype(F32)).astype(BF16)


def gelu(v):
    return jax.nn.gelu(v)


def gelu_both(v):
    c = 0.7978845608028654
    th = jnp.tanh(c * (v + 0.044715 * v * v * v))
    half = 0.5 * (1.0 + th)
    return v * half, half + 0.5 * v * (1.0 - th * th) * c * (1.0 + 3 * 0.044715 * v * v)


def sigmoid(v):
    return 1.0 / (1.0 + jnp.exp(-v))


def minus_expm1(v):
    near = -v * (1.0 + v / 2 * (1.0 + v / 3 * (1.0 + v / 4 * (1.0 + v / 5 * (1.0 + v / 6)))))
    return jnp.where(v > -0.25, near, 1.0 - jnp.exp(v))


class Grid:
    def __init__(self, mesh):
        self.S, self.Q, self.T = (mesh.shape[n] for n in ("shard", "ctx", "tp"))
        dev = mesh.devices

        def chip(d):
            return tuple(getattr(d, "coords", None) or ())

        def paired(one, two):
            return bool(chip(one)) and chip(one) == chip(two)

        self.core_in = None
        if self.Q % 2 == 0 and paired(dev[0, 0, 0], dev[0, 1, 0]):
            self.core_in = "ctx"
        elif self.S % 2 == 0 and paired(dev[0, 0, 0], dev[1, 0, 0]):
            self.core_in = "shard"
        self.C = 1 if self.core_in is None else 2
        self.A = self.S // 2 if self.core_in == "shard" else self.S
        self.B = self.Q // 2 if self.core_in == "ctx" else self.Q
        self.N = self.S * self.Q

    def me(self):
        s, q = lax.axis_index("shard"), lax.axis_index("ctx")
        if self.core_in == "ctx":
            return s, q // 2, q % 2
        if self.core_in == "shard":
            return s // 2, q, s % 2
        return s, q, 0

    def shard_ctx(self, a, b, c):
        if self.core_in == "ctx":
            return a, b * 2 + c
        if self.core_in == "shard":
            return a * 2 + c, b
        return a, b

    def block(self, a, b, c):
        s, q = self.shard_ctx(a, b, c)
        return s * self.Q + q

    def dev(self, a, b, c):
        s, q = self.shard_ctx(a, b, c)
        return {"shard": s, "ctx": q}


class Wire:
    def __init__(self, send, recv, base=0):
        self.send, self.recv, self.used = send, recv, base

    def copy(self, src, dst, dev):
        self.used += 1
        return self.at(self.used - 1, src, dst, dev)

    def at(self, k, src, dst, dev):
        return pltpu.make_async_remote_copy(
            src_ref=src,
            dst_ref=dst,
            send_sem=self.send.at[k],
            recv_sem=self.recv.at[k],
            device_id=dev,
            device_id_type=MESH,
        )


def greet(devs):
    bar = pltpu.get_barrier_semaphore()
    for d in devs:
        pl.semaphore_signal(bar, inc=1, device_id=d, device_id_type=MESH)
    pl.semaphore_wait(bar, len(devs))


def ring_peers(size, at, place):
    if size == 1:
        return []
    if size == 2:
        return [place((at + 1) % 2)]
    return [place((at + 1) % size), place((at + size - 1) % size)]


def plane_peers(g):
    a, b, c = g.me()
    out = ring_peers(g.A, a, lambda k: g.dev(k, b, c))
    out += ring_peers(g.B, b, lambda k: g.dev(a, k, c))
    if g.C == 2:
        out.append(g.dev(a, b, 1 - c))
    return out


def gather_count(g):
    ring = 0
    for nf, ng in ((g.A, g.B), (g.B, g.A)):
        ring += (nf - 1) + (ng - 1) * nf
    return ring + (g.C - 1) * (1 + ring)


def gather_steps(g, wire, srcs, dsts):
    a, b, c = g.me()
    sib = None if g.C == 1 else g.dev(a, b, 1 - c)
    sends, sib_copies = [], []

    def ring(h):
        if h == 0:
            return g.A, a, (lambda k: g.dev(k, b, c)), g.B, b, (lambda k: g.dev(a, k, c)), (lambda f, s: g.block(f, s, c))
        return g.B, b, (lambda k: g.dev(a, k, c)), g.A, a, (lambda k: g.dev(k, b, c)), (lambda f, s: g.block(s, f, c))

    def start(src, dst, dev):
        cp = wire.copy(src, dst, dev)
        cp.start()
        sends.append(cp)
        return cp

    def rows_of(dst, blk, h, rows):
        half = rows // 2
        return dst.at[pl.ds(pl.multiple_of(blk * rows + h * half, half), half)]

    state = []
    mine = g.block(a, b, c)
    for src, dst in zip(srcs, dsts):
        rows = src.shape[0]
        half = rows // 2
        per = []
        for h in (0, 1):
            nf, f, fdev, ng, s, sdev, blk = ring(h)
            own = src.at[pl.ds(h * half, half)]
            land = rows_of(dst, mine, h, rows)
            first = start(own, land, fdev((f + 1) % nf)) if nf > 1 else None
            per.append([first, None, own, land])
        for h in (0, 1):
            nf, f, fdev, ng, s, sdev, blk = ring(h)
            _, _, own, land = per[h]
            second = {}
            if ng > 1:
                second[(0, 0)] = start(own, land, sdev((s + 1) % ng))
            per[h][1] = second
        if sib is not None:
            whole = dst.at[pl.ds(pl.multiple_of(mine * rows, rows), rows)]
            sib_copies.append(start(src, whole, sib))
        state.append(per)
        yield
    for (src, dst), per in zip(zip(srcs, dsts), state):
        rows = src.shape[0]
        for h in (0, 1):
            nf, f, fdev, ng, s, sdev, blk = ring(h)
            cp = per[h][0]
            for i in range(1, nf):
                cp.wait_recv()
                at = rows_of(dst, blk((f - i) % nf, s), h, rows)
                if i < nf - 1:
                    cp = start(at, at, fdev((f + 1) % nf))
                if ng > 1:
                    per[h][1][(0, i)] = start(at, at, sdev((s + 1) % ng))
                if sib is not None:
                    sib_copies.append(start(at, at, sib))
        yield
    for (src, dst), per in zip(zip(srcs, dsts), state):
        rows = src.shape[0]
        for h in (0, 1):
            nf, f, fdev, ng, s, sdev, blk = ring(h)
            second = per[h][1]
            for j in range(1, ng):
                for i in range(nf):
                    second[(j - 1, i)].wait_recv()
                    at = rows_of(dst, blk((f - i) % nf, (s - j) % ng), h, rows)
                    if j < ng - 1:
                        second[(j, i)] = start(at, at, sdev((s + 1) % ng))
                    if sib is not None:
                        sib_copies.append(start(at, at, sib))
        yield
    for cp in sib_copies:
        cp.wait_recv()
    for cp in sends:
        cp.wait_send()


def gather_kernel(g, n, *refs):
    srcs, dsts = refs[:n], refs[n : 2 * n]
    send, recv, here = refs[2 * n :]
    greet(plane_peers(g))
    mine = g.block(*g.me())
    locals_ = []
    for k, (src, dst) in enumerate(zip(srcs, dsts)):
        rows = src.shape[0]
        cp = pltpu.make_async_copy(src, dst.at[pl.ds(pl.multiple_of(mine * rows, rows), rows)], here.at[k])
        cp.start()
        locals_.append(cp)
    for _ in gather_steps(g, Wire(send, recv), srcs, dsts):
        pass
    for cp in locals_:
        cp.wait()


def gather_call(g, srcs, cid):
    n = len(srcs)
    count = n * gather_count(g)
    return pl.pallas_call(
        functools.partial(gather_kernel, g, n),
        out_shape=[jax.ShapeDtypeStruct((g.N * s.shape[0], s.shape[1]), s.dtype) for s in srcs],
        in_specs=[ANY] * n,
        out_specs=[ANY] * n,
        scratch_shapes=[
            pltpu.SemaphoreType.DMA((count,)),
            pltpu.SemaphoreType.DMA((count,)),
            pltpu.SemaphoreType.DMA((n,)),
        ],
        compiler_params=pltpu.CompilerParams(collective_id=cid, has_side_effects=True),
        name="gather",
    )(*srcs)


def tp_peers(g):
    t = lax.axis_index("tp")
    return ring_peers(g.T, t, lambda k: {"tp": k})


def tp_count(g, subs):
    return 2 * (g.T - 1) * subs


def tp_sum_steps(g, wire, subs, rows, partial, finish, term, sendbuf, recvbuf, out):
    T = g.T
    t = lax.axis_index("tp")
    right = {"tp": (t + 1) % T}
    sub = rows // subs
    sends = []
    last = [None] * subs
    for i in range(T):
        k = (t + 2 * T - 1 - i) % T
        partial(pl.multiple_of(k * rows, rows), rows, term)
        for u in range(subs):
            part = term[u * sub : (u + 1) * sub]
            if i > 0:
                last[u].wait_recv()
                part = part + recvbuf[i - 1, u * sub : (u + 1) * sub].astype(F32)
            if i < T - 1:
                sendbuf[i, u * sub : (u + 1) * sub] = part.astype(BF16)
                cp = wire.copy(
                    sendbuf.at[i, pl.ds(u * sub, sub)], recvbuf.at[i, pl.ds(u * sub, sub)], right
                )
                cp.start()
                sends.append(cp)
                last[u] = cp
            else:
                at = pl.multiple_of(k * rows + u * sub, sub)
                out[pl.ds(at, sub)] = finish(part, u * sub, at, sub)
                if T > 1:
                    cp = wire.copy(out.at[pl.ds(at, sub)], out.at[pl.ds(at, sub)], right)
                    cp.start()
                    sends.append(cp)
                    last[u] = cp
        yield
    for i in range(1, T):
        k = (t + T - i) % T
        for u in range(subs):
            last[u].wait_recv()
            if i < T - 1:
                at = pl.multiple_of(k * rows + u * sub, sub)
                cp = wire.copy(out.at[pl.ds(at, sub)], out.at[pl.ds(at, sub)], right)
                cp.start()
                sends.append(cp)
                last[u] = cp
        yield
    for cp in sends:
        cp.wait_send()


def tp_scratch(g, rows, width, subs):
    n = max(1, g.T - 1)
    return [
        pltpu.VMEM((rows, width), F32),
        pltpu.VMEM((n, rows, width), BF16),
        pltpu.VMEM((n, rows, width), BF16),
        pltpu.SemaphoreType.DMA((max(1, tp_count(g, subs)),)),
        pltpu.SemaphoreType.DMA((max(1, tp_count(g, subs)),)),
    ]


SUBS = 4


def tp_call(g, body, operands, out_shape, rows, width, cid, name):
    n_in, n_out = len(operands), len(out_shape)

    def kernel(*refs):
        ins, outs = refs[:n_in], refs[n_in : n_in + n_out]
        term, sendbuf, recvbuf, send, recv = refs[n_in + n_out :]
        greet(tp_peers(g))
        partial, finish = body(ins, outs)
        for _ in tp_sum_steps(g, Wire(send, recv), SUBS, rows, partial, finish, term, sendbuf, recvbuf, outs[0]):
            pass

    return pl.pallas_call(
        kernel,
        out_shape=out_shape,
        in_specs=[VM] * n_in,
        out_specs=[VM] * n_out,
        scratch_shapes=tp_scratch(g, rows, width, SUBS),
        compiler_params=pltpu.CompilerParams(
            collective_id=cid, has_side_effects=True, vmem_limit_bytes=VMEM_LIMIT
        ),
        name=name,
    )(*operands)


def tile_of(width):
    return 512 if width % 512 == 0 else width


def rows_product(term, at, n, pairs):
    width = term.shape[1]
    tile = tile_of(width)

    def body(j, _):
        c0 = pl.multiple_of(j * tile, tile)
        total = None
        for l, r in pairs:
            p = dot_rows(l[pl.ds(at, n)], r[pl.ds(c0, tile)])
            total = p if total is None else total + p
        term[:, pl.ds(c0, tile)] = total
        return 0

    lax.fori_loop(0, width // tile, body, 0)


def mean_square(v):
    return jnp.mean(v * v, axis=-1, keepdims=True)


def mix_out_body(ins, outs):
    mixed, w_out, x, gain = ins
    _, middle = outs

    def partial(at, n, term):
        rows_product(term, at, n, [(mixed, w_out)])

    def finish(total, near, at, n):
        m = x[pl.ds(at, n)].astype(F32) + total
        middle[near : near + n] = m
        return (m * lax.rsqrt(mean_square(m) + EPS) * gain[...]).astype(BF16)

    return partial, finish


def mlp_out_body(ins, outs):
    hidden, w_down, middle, live = ins

    def partial(at, n, term):
        rows_product(term, at, n, [(hidden, w_down)])

    def finish(total, near, at, n):
        return ((middle[near : near + n] + total) * live[pl.ds(at, n)]).astype(BF16)

    return partial, finish


def norm_back(grad_normed, rows, gain):
    inv = lax.rsqrt(mean_square(rows) + EPS)
    gg = grad_normed * gain
    back = inv * gg - rows * (inv * inv * inv) * jnp.mean(gg * rows, axis=-1, keepdims=True)
    return back, jnp.sum(grad_normed * rows * inv, axis=0, keepdims=True)


def mlp_back_body(ins, outs):
    gate_low, up_low, w_gate, w_up, middle, cot, live, gain = ins
    _, grad_middle, grad_gain = outs

    def partial(at, n, term):
        rows_product(term, at, n, [(gate_low, w_gate), (up_low, w_up)])

    def finish(total, near, at, n):
        back, gain_sum = norm_back(total, middle[near : near + n], gain[...])
        gm = cot[pl.ds(at, n)].astype(F32) * live[pl.ds(at, n)] + back
        grad_middle[near : near + n] = gm
        grad_gain[...] = gain_sum if near == 0 else grad_gain[...] + gain_sum
        return gm.astype(BF16)

    return partial, finish


def rec_back_body(ins, outs):
    branch_low, rec_low, w_branch, w_rec, x, grad_middle, gain = ins
    _, grad_gain = outs

    def partial(at, n, term):
        rows_product(term, at, n, [(branch_low, w_branch), (rec_low, w_rec)])

    def finish(total, near, at, n):
        back, gain_sum = norm_back(total, x[pl.ds(at, n)].astype(F32), gain[...])
        grad_gain[...] = gain_sum if near == 0 else grad_gain[...] + gain_sum
        return (grad_middle[near : near + n] + back).astype(BF16)

    return partial, finish


TAPS, SHIFT, RBIAS, EBIAS, SOFT = 0, 4, 5, 6, 7
ROWS = 64
GROUP = 8


def ctx_peers(g):
    q = lax.axis_index("ctx")
    return [{"ctx": (q + k) % g.Q} for k in range(1, g.Q)]


def swap_edges(g, wire, src, land):
    q = lax.axis_index("ctx")
    cps = []
    for k in range(1, g.Q):
        cp = wire.copy(src, land.at[q], {"ctx": (q + k) % g.Q})
        cp.start()
        cps.append(cp)
    for cp in cps:
        cp.wait_recv()
    for cp in cps:
        cp.wait_send()


def row_shift(v, n):
    return pltpu.roll(v, n % v.shape[0], 0)


def forward_kernel(g, rec, branch, w_rate, w_entry, vecs, mixed, conv, rate, entry, state, edge,
                   ext, acum, bcum, tot, halo, gath, send, recv):
    L, CH = rec.shape
    q = lax.axis_index("ctx")
    greet(ctx_peers(g))
    wire = Wire(send, recv)
    ext[8:] = rec[...]
    if g.Q > 1:
        cp = wire.copy(ext.at[pl.ds(L, 8)], halo, {"ctx": (q + 1) % g.Q})
        cp.start()
        cp.wait()
        ext[0:8] = jnp.where(q > 0, halo[...], 0.0)
    else:
        ext[0:8] = jnp.zeros((8, CH), F32)
    sub = lax.broadcasted_iota(jnp.int32, (GROUP, 1), 0)

    def chunk(i, carry):
        ca, cb = carry
        r0 = pl.multiple_of(i * ROWS, ROWS)
        wide = ext[pl.ds(r0, ROWS + 8)]
        c = vecs[SHIFT : SHIFT + 1] + vecs[TAPS : TAPS + 1] * wide[8:]
        for k in range(1, 4):
            c = c + vecs[TAPS + k : TAPS + k + 1] * row_shift(wide, k)[8:]
        conv[pl.ds(r0, ROWS)] = c
        hi, lo = halves(c)
        gr = sigmoid(dot(hi, w_rate[...]) + dot(lo, w_rate[...]) + vecs[RBIAS : RBIAS + 1])
        ge = sigmoid(dot(hi, w_entry[...]) + dot(lo, w_entry[...]) + vecs[EBIAS : EBIAS + 1])
        rate[pl.ds(r0, ROWS)] = gr
        entry[pl.ds(r0, ROWS)] = ge
        log = -DECAY_SCALE * gr * vecs[SOFT : SOFT + 1]
        dec = jnp.exp(log)
        drive = jnp.sqrt(minus_expm1(2.0 * log)) * ge * c
        for n in range(ROWS // GROUP):
            A = dec[n * GROUP : (n + 1) * GROUP]
            B = drive[n * GROUP : (n + 1) * GROUP]
            for step in (1, 2, 4):
                keep = sub >= step
                As = jnp.where(keep, row_shift(A, step), 1.0)
                Bs = jnp.where(keep, row_shift(B, step), 0.0)
                B = B + A * Bs
                A = A * As
            B = B + A * cb
            A = A * ca
            acum[pl.ds(r0 + n * GROUP, GROUP)] = A
            bcum[pl.ds(r0 + n * GROUP, GROUP)] = B
            ca = A[GROUP - 1 : GROUP]
            cb = B[GROUP - 1 : GROUP]
        return ca, cb

    ca, cb = lax.fori_loop(0, L // ROWS, chunk, (jnp.ones((1, CH), F32), jnp.zeros((1, CH), F32)))
    tot[0:1] = ca
    tot[1:2] = cb
    start = jnp.zeros((1, CH), F32)
    if g.Q > 1:
        swap_edges(g, wire, tot, gath)
        for d in range(g.Q - 1):
            new = gath[d, 0:1] * start + gath[d, 1:2]
            start = jnp.where(d < q, new, start)
    edge[...] = jnp.broadcast_to(start, (8, CH))

    def fix(i, _):
        r0 = pl.multiple_of(i * ROWS, ROWS)
        s = bcum[pl.ds(r0, ROWS)] + acum[pl.ds(r0, ROWS)] * start
        state[pl.ds(r0, ROWS)] = s
        mixed[pl.ds(r0, ROWS)] = (gelu_both(branch[pl.ds(r0, ROWS)])[0] * s).astype(BF16)
        return 0

    lax.fori_loop(0, L // ROWS, fix, 0)


def forward_call(g, rec, branch, w_rate, w_entry, vecs, cid):
    L, CH = rec.shape
    wide = jax.ShapeDtypeStruct((L, CH), F32)
    return pl.pallas_call(
        functools.partial(forward_kernel, g),
        out_shape=[jax.ShapeDtypeStruct((L, CH), BF16), wide, wide, wide, wide, jax.ShapeDtypeStruct((8, CH), F32)],
        in_specs=[VM] * 5,
        out_specs=[VM] * 6,
        scratch_shapes=[
            pltpu.VMEM((L + 8, CH), F32),
            pltpu.VMEM((L, CH), F32),
            pltpu.VMEM((L, CH), F32),
            pltpu.VMEM((8, CH), F32),
            pltpu.VMEM((8, CH), F32),
            pltpu.VMEM((g.Q, 8, CH), F32),
            pltpu.SemaphoreType.DMA((g.Q,)),
            pltpu.SemaphoreType.DMA((g.Q,)),
        ],
        compiler_params=pltpu.CompilerParams(
            collective_id=cid, has_side_effects=True, vmem_limit_bytes=VMEM_LIMIT
        ),
        name="rec_forward",
    )(rec, branch, w_rate, w_entry, vecs)


def backward_kernel(g, mid_low, w_out, branch, rec, conv, rate, entry, state, edge, w_rate, w_entry, vecs,
                    branch_low, rec_low, g_rate, g_entry, g_vecs,
                    sgrad, acum, bcum, gconv, conv_h, conv_l, rb_h, rb_l, eb_h, eb_l, tot, gath, halo, prevx, send, recv):
    L, CH = rec.shape
    q = lax.axis_index("ctx")
    greet(ctx_peers(g))
    wire = Wire(send, recv)
    tail = None
    if g.Q > 1:
        tail = wire.copy(rec.at[pl.ds(L - 8, 8)], prevx, {"ctx": (q + 1) % g.Q})
        tail.start()
    sub = lax.broadcasted_iota(jnp.int32, (GROUP, 1), 0)
    chunks = L // ROWS

    def chunk(j, carry):
        ua, ub = carry
        r0 = pl.multiple_of((chunks - 1 - j) * ROWS, ROWS)
        gm = dot(mid_low[pl.ds(r0, ROWS)], w_out[...])
        act, slope = gelu_both(branch[pl.ds(r0, ROWS)])
        branch_low[pl.ds(r0, ROWS)] = (gm * state[pl.ds(r0, ROWS)] * slope).astype(BF16)
        sg = gm * act
        sgrad[pl.ds(r0, ROWS)] = sg
        dec = jnp.exp(-DECAY_SCALE * rate[pl.ds(r0, ROWS)] * vecs[SOFT : SOFT + 1])
        sg = dec * sg
        for n in reversed(range(ROWS // GROUP)):
            A = dec[n * GROUP : (n + 1) * GROUP]
            B = sg[n * GROUP : (n + 1) * GROUP]
            for step in (1, 2, 4):
                keep = sub < GROUP - step
                As = jnp.where(keep, row_shift(A, -step), 1.0)
                Bs = jnp.where(keep, row_shift(B, -step), 0.0)
                B = B + A * Bs
                A = A * As
            B = B + A * ub
            A = A * ua
            acum[pl.ds(r0 + n * GROUP, GROUP)] = A
            bcum[pl.ds(r0 + n * GROUP, GROUP)] = B
            ua = A[0:1]
            ub = B[0:1]
        return ua, ub

    ua, ub = lax.fori_loop(0, chunks, chunk, (jnp.ones((1, CH), F32), jnp.zeros((1, CH), F32)))
    tot[0:1] = ua
    tot[1:2] = ub
    arriving = jnp.zeros((1, CH), F32)
    if g.Q > 1:
        swap_edges(g, wire, tot, gath)
        for d in reversed(range(1, g.Q)):
            new = gath[d, 0:1] * arriving + gath[d, 1:2]
            arriving = jnp.where(d > q, new, arriving)
        tail.wait()
    acum[L:] = jnp.ones((8, CH), F32)
    bcum[L:] = jnp.zeros((8, CH), F32)
    zero = jnp.zeros((1, CH), F32)
    if g.Q > 1:
        prev_rows = jnp.where(q > 0, prevx[...], 0.0)
    else:
        prev_rows = jnp.zeros((8, CH), F32)

    def back(i, carry):
        gdec, gbr, gbe, gshift, gt0, gt1, gt2, gt3, last_state, last_rec = carry
        r0 = pl.multiple_of(i * ROWS, ROWS)
        aw = row_shift(acum[pl.ds(r0, ROWS + 8)], -1)[:ROWS]
        bw = row_shift(bcum[pl.ds(r0, ROWS + 8)], -1)[:ROWS]
        car = sgrad[pl.ds(r0, ROWS)] + bw + aw * arriving
        st = state[pl.ds(r0, ROWS)]
        prev = row_shift(jnp.concatenate([last_state, st], axis=0), 1)[8:]
        gr = rate[pl.ds(r0, ROWS)]
        ge = entry[pl.ds(r0, ROWS)]
        c = conv[pl.ds(r0, ROWS)]
        soft = vecs[SOFT : SOFT + 1]
        log = -DECAY_SCALE * gr * soft
        dec = jnp.exp(log)
        scale = jnp.sqrt(minus_expm1(2.0 * log))
        ec = ge * c
        glog = car * prev * dec - car * ec * dec * dec / scale
        glr = 8.0 * glog * gr
        gdec = gdec + jnp.sum(glr, axis=0, keepdims=True)
        rb = -glr * soft * (1.0 - gr)
        cs = car * scale
        eb = cs * ec * (1.0 - ge)
        gbr = gbr + jnp.sum(rb, axis=0, keepdims=True)
        gbe = gbe + jnp.sum(eb, axis=0, keepdims=True)
        rh, rl = halves(rb)
        eh, el = halves(eb)
        ch, cl = halves(c)
        rb_h[pl.ds(r0, ROWS)] = rh
        rb_l[pl.ds(r0, ROWS)] = rl
        eb_h[pl.ds(r0, ROWS)] = eh
        eb_l[pl.ds(r0, ROWS)] = el
        conv_h[pl.ds(r0, ROWS)] = ch
        conv_l[pl.ds(r0, ROWS)] = cl
        wr, we = w_rate[...], w_entry[...]
        gc = cs * ge + dot_rows(rh, wr) + dot_rows(rl, wr) + dot_rows(eh, we) + dot_rows(el, we)
        gconv[pl.ds(r0, ROWS)] = gc
        gshift = gshift + jnp.sum(gc, axis=0, keepdims=True)
        x = rec[pl.ds(r0, ROWS)]
        wide = jnp.concatenate([last_rec, x], axis=0)
        gts = [gt0, gt1, gt2, gt3]
        for k in range(4):
            xk = x if k == 0 else row_shift(wide, k)[8:]
            gts[k] = gts[k] + jnp.sum(gc * xk, axis=0, keepdims=True)
        return (gdec, gbr, gbe, gshift, *gts, st[ROWS - 8 :], x[ROWS - 8 :])

    carry = lax.fori_loop(0, chunks, back, (zero,) * 8 + (edge[...], prev_rows))
    gdec, gbr, gbe, gshift, gt0, gt1, gt2, gt3 = carry[:8]
    if g.Q > 1:
        cp = wire.copy(gconv.at[pl.ds(0, 8)], halo, {"ctx": (q + g.Q - 1) % g.Q})
        cp.start()
    for k, v in enumerate((gt0, gt1, gt2, gt3, gshift, gbr, gbe, gdec)):
        g_vecs[k : k + 1] = v

    def product(h, l):
        return dot_tokens(conv_h[...], h[...]) + dot_tokens(conv_l[...], h[...]) + dot_tokens(conv_h[...], l[...])

    g_rate[...] = product(rb_h, rb_l)
    g_entry[...] = product(eb_h, eb_l)
    if g.Q > 1:
        cp.wait()
        gconv[L:] = jnp.where(q < g.Q - 1, halo[...], 0.0)
    else:
        gconv[L:] = jnp.zeros((8, CH), F32)

    def last(i, _):
        r0 = pl.multiple_of(i * ROWS, ROWS)
        wide = gconv[pl.ds(r0, ROWS + 8)]
        total = vecs[TAPS : TAPS + 1] * wide[:ROWS]
        for k in range(1, 4):
            total = total + vecs[TAPS + k : TAPS + k + 1] * row_shift(wide, -k)[:ROWS]
        rec_low[pl.ds(r0, ROWS)] = total.astype(BF16)
        return 0

    lax.fori_loop(0, chunks, last, 0)


def backward_call(g, mid_low, w_out, branch, rec, conv, rate, entry, state, edge, w_rate, w_entry, vecs, cid):
    L, CH = rec.shape
    low = jax.ShapeDtypeStruct((L, CH), BF16)
    dense = jax.ShapeDtypeStruct((CH, CH), F32)
    return pl.pallas_call(
        functools.partial(backward_kernel, g),
        out_shape=[low, low, dense, dense, jax.ShapeDtypeStruct((8, CH), F32)],
        in_specs=[VM] * 12,
        out_specs=[VM] * 5,
        scratch_shapes=[
            pltpu.VMEM((L, CH), F32),
            pltpu.VMEM((L + 8, CH), F32),
            pltpu.VMEM((L + 8, CH), F32),
            pltpu.VMEM((L + 8, CH), F32),
        ]
        + [pltpu.VMEM((L, CH), BF16)] * 6
        + [
            pltpu.VMEM((8, CH), F32),
            pltpu.VMEM((g.Q, 8, CH), F32),
            pltpu.VMEM((8, CH), F32),
            pltpu.VMEM((8, CH), F32),
            pltpu.SemaphoreType.DMA((g.Q + 1,)),
            pltpu.SemaphoreType.DMA((g.Q + 1,)),
        ],
        compiler_params=pltpu.CompilerParams(
            collective_id=cid, has_side_effects=True, vmem_limit_bytes=VMEM_LIMIT
        ),
        name="rec_backward",
    )(mid_low, w_out, branch, rec, conv, rate, entry, state, edge, w_rate, w_entry, vecs)


def reduce_count(g):
    ring = 0
    for nf, ng in ((g.A, g.B), (g.B, g.A)):
        ring += (nf - 1) * ng + (ng - 1)
    return ring + (g.C - 1) * g.A * g.B


def reduce_bufs(g, rows, width):
    nb = g.A * g.B
    arrivals = reduce_count(g) - (g.C - 1) * nb
    return [
        pltpu.VMEM((nb, rows, width), BF16),
        pltpu.VMEM((nb, rows, width), BF16),
        pltpu.VMEM((max(1, arrivals), rows // 2, width), BF16),
    ]


def reduce_steps(g, wire, items):
    a, b, c = g.me()
    sends = []

    def start(src, dst, dev):
        cp = wire.copy(src, dst, dev)
        cp.start()
        sends.append(cp)
        return cp

    nb = g.A * g.B

    def owner(k, core):
        return g.block((a + g.A - k // g.B) % g.A, (b + g.B - k % g.B) % g.B, core)

    def each_tile(width, fn):
        tile = tile_of(width)
        lax.fori_loop(0, width // tile, lambda j, _: fn(pl.ds(pl.multiple_of(j * tile, tile), tile)) or 0, 0)

    bases = []
    for term, out, (to_sib, sums, land) in items:
        base = wire.used
        bases.append(base)
        if g.C == 2:
            wire.used += nb

            def one(i, _):
                k = (i + 1) % nb

                def tile(cols):
                    to_sib[k, :, cols] = term(owner(k, 1 - c), cols).astype(BF16)

                each_tile(out.shape[1], tile)
                wire.at(base + k, to_sib.at[k], sums.at[k], g.dev(a, b, 1 - c)).start()
                return 0

            lax.fori_loop(0, nb, one, 0)
        yield

    rings = [(g.A, g.B), (g.B, g.A)]
    devs = [
        (g.dev((a + 1) % g.A, b, c), g.dev(a, (b + 1) % g.B, c)),
        (g.dev(a, (b + 1) % g.B, c), g.dev((a + 1) % g.A, b, c)),
    ]

    def slot(h, df, dg):
        return df * g.B + dg if h == 0 else dg * g.B + df

    state = []
    for (term, out, (to_sib, sums, land)), base in zip(items, bases):
        half = out.shape[0] // 2

        def got(k):
            if g.C == 2:
                wire.at(base + k, to_sib.at[k], sums.at[k], g.dev(a, b, 1 - c)).wait_recv()

        def one(k, _):
            got(k)

            def tile(cols):
                s = term(owner(k, c), cols)
                if g.C == 2:
                    s = s + sums[k, :, cols].astype(F32)
                sums[k, :, cols] = s.astype(BF16)

            each_tile(out.shape[1], tile)
            return 0

        lax.fori_loop(1, nb, one, 0)
        used = 0
        first = ({}, {})
        for h in (0, 1):
            nf, ng = rings[h]
            if nf > 1:
                for dg in [d % ng for d in range(1, ng + 1)]:
                    k = slot(h, 1, dg)
                    first[h][dg] = (start(sums.at[k, pl.ds(h * half, half)], land.at[used], devs[h][0]), used)
                    used += 1
        got(0)

        def tile(cols):
            s = term(owner(0, c), cols)
            if g.C == 2:
                s = s + sums[0, :, cols].astype(F32)
            out[:, cols] = s

        each_tile(out.shape[1], tile)
        state.append([first, used])
        yield

    def add(out, sums, k, h, half, arrived):
        at = slice(h * half, (h + 1) * half)
        if k == 0:
            out[at] = out[at] + arrived.astype(F32)
        else:
            sums[k, at] = (sums[k, at].astype(F32) + arrived.astype(F32)).astype(BF16)

    seconds = []
    for (term, out, (to_sib, sums, land)), st in zip(items, state):
        half = out.shape[0] // 2
        first, used = st
        second = [None, None]
        for h in (0, 1):
            nf, ng = rings[h]
            for i in range(1, nf):
                df = (i + 1) % nf
                for dg in [d % ng for d in range(1, ng + 1)]:
                    cp, at = first[h][dg]
                    cp.wait_recv()
                    k = slot(h, df, dg)
                    add(out, sums, k, h, half, land[at])
                    if i < nf - 1:
                        first[h][dg] = (start(sums.at[k, pl.ds(h * half, half)], land.at[used], devs[h][0]), used)
                        used += 1
                    elif dg == 1 and ng > 1:
                        second[h] = (start(sums.at[k, pl.ds(h * half, half)], land.at[used], devs[h][1]), used)
                        used += 1
            if nf == 1 and ng > 1:
                k = slot(h, 0, 1)
                second[h] = (start(sums.at[k, pl.ds(h * half, half)], land.at[used], devs[h][1]), used)
                used += 1
        seconds.append([second, used])
        yield
    for (term, out, (to_sib, sums, land)), (second, used) in zip(items, seconds):
        half = out.shape[0] // 2
        for h in (0, 1):
            nf, ng = rings[h]
            for j in range(1, ng):
                cp, at = second[h]
                cp.wait_recv()
                k = slot(h, 0, (j + 1) % ng)
                add(out, sums, k, h, half, land[at])
                if j < ng - 1:
                    second[h] = (start(sums.at[k, pl.ds(h * half, half)], land.at[used], devs[h][1]), used)
                    used += 1
        yield
    for cp in sends:
        cp.wait_send()
    if g.C == 2:
        for (term, out, (to_sib, sums, land)), base in zip(items, bases):
            for k in range(nb):
                wire.at(base + k, to_sib.at[k], sums.at[k], g.dev(a, b, 1 - c)).wait_send()


def reduce_call(g, pairs, given, cid, name):
    ops, where, items = [], [], []

    def place(x):
        for k, o in enumerate(ops):
            if o is x:
                return k
        ops.append(x)
        return len(ops) - 1

    for l, r in pairs:
        where.append((place(l), place(r)))
        items.append((l.shape[0] // g.N, r.shape[1]))
    for v in given:
        where.append((place(v), None))
        items.append((v.shape[0] // g.N, v.shape[1]))
    n_in, n_out = len(ops), len(items)
    count = n_out * reduce_count(g)

    def kernel(*refs):
        ins, outs = refs[:n_in], refs[n_in : n_in + n_out]
        bufs = refs[n_in + n_out : n_in + 4 * n_out]
        send, recv = refs[n_in + 4 * n_out :]
        greet(plane_peers(g))

        def term_of(where, rows):
            l, r = where

            def term(block, cols):
                at = pl.ds(pl.multiple_of(block * rows, rows), rows)
                if r is None:
                    return ins[l][at, cols]
                return dot(ins[l][at], ins[r][:, cols])

            return term

        work = [
            (term_of(where[k], items[k][0]), outs[k], bufs[3 * k : 3 * k + 3]) for k in range(n_out)
        ]
        for _ in reduce_steps(g, Wire(send, recv), work):
            pass

    scratch = []
    for rows, width in items:
        scratch += reduce_bufs(g, rows, width)
    return pl.pallas_call(
        kernel,
        out_shape=[jax.ShapeDtypeStruct(s, F32) for s in items],
        in_specs=[VM] * n_in,
        out_specs=[VM] * n_out,
        scratch_shapes=scratch
        + [pltpu.SemaphoreType.DMA((count,)), pltpu.SemaphoreType.DMA((count,))],
        compiler_params=pltpu.CompilerParams(
            collective_id=cid, has_side_effects=True, vmem_limit_bytes=VMEM_LIMIT
        ),
        name=name,
    )(*ops)


def up_to(n, k):
    return -(-n // k) * k


def small_pack(parts, rows, width):
    flat = jnp.concatenate([p.reshape(-1) for p in parts])
    return jnp.pad(flat, (0, rows * width - flat.shape[0])).reshape(rows, width)


def block_dense(blocks):
    n, w = blocks.shape[0], blocks.shape[1]
    eye = jnp.eye(n, dtype=blocks.dtype)
    return (blocks[:, :, None, :] * eye[:, None, :, None]).reshape(n * w, n * w)


def local(g, inputs, lengths, cotangent, norm1_gain, branch_weight, rec_in_weight, conv_weight, conv_bias,
          rgate_weight, rgate_bias, igate_weight, igate_bias, decay_param, out_weight, norm2_gain,
          mlp_gate_weight, mlp_up_weight, mlp_down_weight):
    slots, block_len, width = inputs.shape
    L = slots * block_len
    N, T = g.N, g.T
    chunk = L // T
    heads, rb, bw = rgate_weight.shape
    ch = heads * bw
    taps = conv_weight.shape[0]
    small = [rgate_weight, igate_weight, conv_weight, conv_bias, rgate_bias, igate_bias, decay_param, norm1_gain, norm2_gain]
    sizes = [p.size for p in small]
    srows = up_to(-(-sum(sizes) // 256), 32)
    pack = small_pack(small, srows, 256)

    got = gather_call(g, [pack, branch_weight, rec_in_weight, out_weight, mlp_gate_weight, mlp_up_weight, mlp_down_weight], 0)
    packs, w_branch, w_rec, w_out, w_gate, w_up, w_down = got
    packs = packs.reshape(N, -1)
    cut, at = [], 0
    for p, s in zip(small, sizes):
        cut.append(packs[:, at : at + s].reshape((N,) + p.shape))
        at += s
    w_rate = block_dense(cut[0].transpose(1, 0, 2, 3).reshape(heads, bw, bw))
    w_entry = block_dense(cut[1].transpose(1, 0, 2, 3).reshape(heads, bw, bw))
    taps_f = cut[2].transpose(1, 2, 0, 3).reshape(taps, ch).astype(F32)

    def channels(v):
        return v.transpose(1, 0, 2).reshape(1, ch).astype(F32)

    decay_f = channels(cut[6])
    vecs = jnp.concatenate(
        [taps_f, channels(cut[3]), channels(cut[4]), channels(cut[5]), jax.nn.softplus(-decay_f)], axis=0
    )
    gain_one = cut[7].reshape(1, width).astype(F32)
    gain_two = cut[8].reshape(1, width).astype(F32)

    x_low = inputs.reshape(L, width)
    cot = cotangent.reshape(L, width)
    positions = lax.axis_index("ctx") * block_len + jnp.arange(block_len, dtype=jnp.int32)
    live = (positions[None, :] < lengths[:, None]).astype(F32).reshape(L, 1)
    t = lax.axis_index("tp")
    x_f = x_low.astype(F32)
    low_one = (x_f * lax.rsqrt(mean_square(x_f) + EPS) * gain_one).astype(BF16)
    branch_pre = dot(low_one, w_branch)
    rec_pre = dot(low_one, w_rec)
    mixed, conv, rate, entry, state, edge = forward_call(g, rec_pre, branch_pre, w_rate, w_entry, vecs, 1)

    low = jax.ShapeDtypeStruct((L, width), BF16)
    mid = jax.ShapeDtypeStruct((chunk, width), F32)
    vec = jax.ShapeDtypeStruct((1, width), F32)
    low_two, middle = tp_call(g, mix_out_body, (mixed, w_out, x_low, gain_two), [low, mid], chunk, width, 2, "mix_out")
    gate_pre = dot(low_two, w_gate)
    up_pre = dot(low_two, w_up)
    act, slope = gelu_both(gate_pre)
    hidden = (act * up_pre).astype(BF16)
    (output,) = tp_call(g, mlp_out_body, (hidden, w_down, middle, live), [low], chunk, width, 3, "mlp_out")
    grad_low = (cot.astype(F32) * live).astype(BF16)
    grad_hidden = dot(grad_low, w_down)
    gate_low = (grad_hidden * up_pre * slope).astype(BF16)
    up_low = (grad_hidden * act).astype(BF16)
    mid_low, grad_middle, part_two = tp_call(
        g, mlp_back_body, (gate_low, up_low, w_gate, w_up, middle, cot, live, gain_two), [low, mid, vec], chunk, width, 4, "mlp_back"
    )
    g_gate, g_up, g_down = reduce_call(
        g, [(low_two.T, gate_low), (low_two.T, up_low), (grad_low.T, hidden)], [], 5, "reduce_mlp"
    )
    branch_low, rec_low, d_rate, d_entry, d_vecs = backward_call(
        g, mid_low, w_out, branch_pre, rec_pre, conv, rate, entry, state, edge, w_rate, w_entry, vecs, 6
    )
    input_grad, part_one = tp_call(
        g, rec_back_body, (branch_low, rec_low, w_branch, w_rec, x_low, grad_middle, gain_one), [low, vec], chunk, width, 7, "rec_back"
    )

    eye = jnp.eye(heads, dtype=F32)[:, None, :, None]

    def diagonal(d):
        return jnp.sum(d.reshape(heads, bw, heads, bw) * eye, axis=0).reshape(N, rb * ch)

    d_gates = jnp.concatenate([diagonal(d_rate), diagonal(d_entry)], axis=1)
    d_vecs = d_vecs.at[7].multiply(jax.nn.sigmoid(-decay_f[0]))
    d_rows = d_vecs.reshape(8, heads, N, rb).transpose(2, 0, 1, 3).reshape(N, -1)
    gains = lax.psum(jnp.concatenate([part_one, part_two], axis=0), "tp").reshape(2, N, -1).transpose(1, 0, 2).reshape(N, -1)
    flat = jnp.concatenate([d_gates, d_rows, gains], axis=1)
    prows = up_to(-(-flat.shape[1] // 256), 32)
    flat = jnp.pad(flat, ((0, 0), (0, prows * 256 - flat.shape[1]))).reshape(N * prows, 256)
    g_branch, g_rec, g_out, g_small = reduce_call(
        g, [(low_one.T, branch_low), (low_one.T, rec_low), (mid_low.T, mixed)], [flat], 8, "reduce_rec"
    )
    g_small = g_small.reshape(-1)
    n = rb * ch
    g_rate = g_small[:n].reshape(rb, heads, bw).transpose(1, 0, 2)
    g_entry = g_small[n : 2 * n].reshape(rb, heads, bw).transpose(1, 0, 2)
    rest = g_small[2 * n : 2 * n + 8 * heads * rb].reshape(8, heads, rb)
    tail = g_small[2 * n + 8 * heads * rb :]
    m = width // N
    shape = (slots, block_len, width)
    return (
        output.reshape(shape), input_grad.reshape(shape), tail[:m], g_branch, g_rec, rest[:taps], rest[4],
        g_rate, rest[5], g_entry, rest[6], rest[7], g_out, tail[m : 2 * m], g_gate, g_up, g_down,
    )


def solution(mesh):
    plane = ("shard", "ctx")
    rows, cols = P(plane), P(plane, "tp")
    tok, gate, chan = P("shard", "ctx", None), P("tp", plane, None), P("tp", plane)
    taps = P(None, "tp", plane)
    params = (rows, cols, cols, taps, chan, gate, chan, gate, chan, chan, cols, rows, cols, cols, cols)
    return jax.shard_map(
        functools.partial(local, Grid(mesh)),
        mesh=mesh,
        in_specs=(tok, P("shard"), tok) + params,
        out_specs=(tok, tok) + params,
        check_vma=False,
    )
```

```python
import functools

import jax
import jax.numpy as jnp
from jax import lax
from jax.experimental import pallas as pl
from jax.experimental.pallas import tpu as pltpu
from jax.sharding import PartitionSpec as P

EPS = 1e-06
DECAY_SCALE = 8.0
F32 = jnp.float32
BF16 = jnp.bfloat16
MESH = pl.DeviceIdType.MESH
ANY = pl.BlockSpec(memory_space=pl.ANY)
VM = pl.BlockSpec(memory_space=pltpu.VMEM)
VMEM_LIMIT = 63 * 1024 * 1024


def dot(a, b):
    return jnp.dot(a, b, preferred_element_type=F32)


def dot_rows(a, b):
    return lax.dot_general(a, b, (((1,), (1,)), ((), ())), preferred_element_type=F32)


def dot_tokens(a, b):
    return lax.dot_general(a, b, (((0,), (0,)), ((), ())), preferred_element_type=F32)


def halves(v):
    hi = v.astype(BF16)
    return hi, (v - hi.astype(F32)).astype(BF16)


def gelu(v):
    return jax.nn.gelu(v)


def gelu_both(v):
    c = 0.7978845608028654
    th = jnp.tanh(c * (v + 0.044715 * v * v * v))
    half = 0.5 * (1.0 + th)
    return v * half, half + 0.5 * v * (1.0 - th * th) * c * (1.0 + 3 * 0.044715 * v * v)


def sigmoid(v):
    return 1.0 / (1.0 + jnp.exp(-v))


def minus_expm1(v):
    near = -v * (1.0 + v / 2 * (1.0 + v / 3 * (1.0 + v / 4 * (1.0 + v / 5 * (1.0 + v / 6)))))
    return jnp.where(v > -0.25, near, 1.0 - jnp.exp(v))


class Grid:
    def __init__(self, mesh):
        self.S, self.Q, self.T = (mesh.shape[n] for n in ("shard", "ctx", "tp"))
        dev = mesh.devices

        def chip(d):
            return tuple(getattr(d, "coords", None) or ())

        def paired(one, two):
            return bool(chip(one)) and chip(one) == chip(two)

        self.core_in = None
        if self.Q % 2 == 0 and paired(dev[0, 0, 0], dev[0, 1, 0]):
            self.core_in = "ctx"
        elif self.S % 2 == 0 and paired(dev[0, 0, 0], dev[1, 0, 0]):
            self.core_in = "shard"
        self.C = 1 if self.core_in is None else 2
        self.A = self.S // 2 if self.core_in == "shard" else self.S
        self.B = self.Q // 2 if self.core_in == "ctx" else self.Q
        self.N = self.S * self.Q

    def me(self):
        s, q = lax.axis_index("shard"), lax.axis_index("ctx")
        if self.core_in == "ctx":
            return s, q // 2, q % 2
        if self.core_in == "shard":
            return s // 2, q, s % 2
        return s, q, 0

    def shard_ctx(self, a, b, c):
        if self.core_in == "ctx":
            return a, b * 2 + c
        if self.core_in == "shard":
            return a * 2 + c, b
        return a, b

    def block(self, a, b, c):
        s, q = self.shard_ctx(a, b, c)
        return s * self.Q + q

    def dev(self, a, b, c):
        s, q = self.shard_ctx(a, b, c)
        return {"shard": s, "ctx": q}


class Wire:
    def __init__(self, send, recv, base=0):
        self.send, self.recv, self.used = send, recv, base

    def copy(self, src, dst, dev):
        self.used += 1
        return self.at(self.used - 1, src, dst, dev)

    def at(self, k, src, dst, dev):
        return pltpu.make_async_remote_copy(
            src_ref=src,
            dst_ref=dst,
            send_sem=self.send.at[k],
            recv_sem=self.recv.at[k],
            device_id=dev,
            device_id_type=MESH,
        )


def greet(devs):
    bar = pltpu.get_barrier_semaphore()
    for d in devs:
        pl.semaphore_signal(bar, inc=1, device_id=d, device_id_type=MESH)
    pl.semaphore_wait(bar, len(devs))


def ring_peers(size, at, place):
    if size == 1:
        return []
    if size == 2:
        return [place((at + 1) % 2)]
    return [place((at + 1) % size), place((at + size - 1) % size)]


def plane_peers(g):
    a, b, c = g.me()
    out = ring_peers(g.A, a, lambda k: g.dev(k, b, c))
    out += ring_peers(g.B, b, lambda k: g.dev(a, k, c))
    if g.C == 2:
        out.append(g.dev(a, b, 1 - c))
    return out


def braid(main, *sides):
    k = 0
    for _ in main:
        for steps, plan in sides:
            for _ in range(plan[k] if k < len(plan) else 0):
                next(steps, None)
        k += 1
    left = [s[0] for s in sides]
    while left:
        left = [s for s in left if next(s, left) is not left]


def at_steps(*pairs):
    plan = [0] * (1 + max(last for _, last, _ in pairs))
    for first, last, each in pairs:
        for k in range(first, last + 1):
            plan[k] += each
    return tuple(plan)


ALWAYS = (1,) * 64


def run(*steps):
    for s in steps:
        for _ in s:
            pass


class Later:
    def __init__(self, src, dst, sem):
        self.copy, self.dst, self.here = pltpu.make_async_copy(src, dst, sem), dst, False
        self.copy.start()

    def ref(self):
        if not self.here:
            self.copy.wait()
            self.here = True
        return self.dst


def call(kernel, operands, out_shape, scratch, cid, name, in_specs=None, out_specs=None, later=()):
    in_specs = list(in_specs or [VM] * len(operands))
    for k in later:
        in_specs[k] = ANY
    n = len(later)
    n_in = len(operands)

    def body(*refs):
        refs = list(refs)
        if n:
            kept, sem = refs[-n - 1 : -1], refs[-1]
            refs = refs[: -n - 1]
            for j, k in enumerate(later):
                refs[k] = Later(refs[k], kept[j], sem.at[j])
        kernel(*refs)

    extra = [pltpu.VMEM(operands[k].shape, operands[k].dtype) for k in later]
    if n:
        extra.append(pltpu.SemaphoreType.DMA((n,)))
    return pl.pallas_call(
        body,
        out_shape=out_shape,
        in_specs=in_specs,
        out_specs=out_specs or [VM] * len(out_shape),
        scratch_shapes=list(scratch) + extra,
        compiler_params=pltpu.CompilerParams(
            collective_id=cid, has_side_effects=True, vmem_limit_bytes=VMEM_LIMIT
        ),
        name=name,
    )(*operands)


def sems(n):
    return [pltpu.SemaphoreType.DMA((max(1, n),)), pltpu.SemaphoreType.DMA((max(1, n),))]


def gather_count(g):
    ring = 0
    for nf, ng in ((g.A, g.B), (g.B, g.A)):
        ring += (nf - 1) + (ng - 1) * nf
    return ring + (g.C - 1) * (1 + ring)


def gather_steps(g, wire, here, srcs, dsts):
    a, b, c = g.me()
    sib = None if g.C == 1 else g.dev(a, b, 1 - c)
    sends, sib_copies = [], []

    def ring(h):
        if h == 0:
            return g.A, a, (lambda k: g.dev(k, b, c)), g.B, b, (lambda k: g.dev(a, k, c)), (lambda f, s: g.block(f, s, c))
        return g.B, b, (lambda k: g.dev(a, k, c)), g.A, a, (lambda k: g.dev(k, b, c)), (lambda f, s: g.block(s, f, c))

    def start(src, dst, dev):
        cp = wire.copy(src, dst, dev)
        cp.start()
        sends.append(cp)
        return cp

    def rows_of(dst, blk, h, rows):
        half = rows // 2
        return dst.at[pl.ds(pl.multiple_of(blk * rows + h * half, half), half)]

    state = []
    mine = g.block(a, b, c)
    local_copies = []
    for src, dst in zip(srcs, dsts):
        rows = src.shape[0]
        half = rows // 2
        cp = pltpu.make_async_copy(src, dst.at[pl.ds(pl.multiple_of(mine * rows, rows), rows)], here.at[len(local_copies)])
        cp.start()
        local_copies.append(cp)
        per = []
        for h in (0, 1):
            nf, f, fdev, ng, s, sdev, blk = ring(h)
            own = src.at[pl.ds(h * half, half)]
            land = rows_of(dst, mine, h, rows)
            first = start(own, land, fdev((f + 1) % nf)) if nf > 1 else None
            per.append([first, None, own, land])
        for h in (0, 1):
            nf, f, fdev, ng, s, sdev, blk = ring(h)
            _, _, own, land = per[h]
            second = {}
            if ng > 1:
                second[(0, 0)] = start(own, land, sdev((s + 1) % ng))
            per[h][1] = second
        if sib is not None:
            whole = dst.at[pl.ds(pl.multiple_of(mine * rows, rows), rows)]
            sib_copies.append(start(src, whole, sib))
        state.append(per)
        yield
    for (src, dst), per in zip(zip(srcs, dsts), state):
        rows = src.shape[0]
        for h in (0, 1):
            nf, f, fdev, ng, s, sdev, blk = ring(h)
            cp = per[h][0]
            for i in range(1, nf):
                cp.wait_recv()
                at = rows_of(dst, blk((f - i) % nf, s), h, rows)
                if i < nf - 1:
                    cp = start(at, at, fdev((f + 1) % nf))
                if ng > 1:
                    per[h][1][(0, i)] = start(at, at, sdev((s + 1) % ng))
                if sib is not None:
                    sib_copies.append(start(at, at, sib))
        yield
    for (src, dst), per in zip(zip(srcs, dsts), state):
        rows = src.shape[0]
        for h in (0, 1):
            nf, f, fdev, ng, s, sdev, blk = ring(h)
            second = per[h][1]
            for j in range(1, ng):
                for i in range(nf):
                    second[(j - 1, i)].wait_recv()
                    at = rows_of(dst, blk((f - i) % nf, (s - j) % ng), h, rows)
                    if j < ng - 1:
                        second[(j, i)] = start(at, at, sdev((s + 1) % ng))
                    if sib is not None:
                        sib_copies.append(start(at, at, sib))
        yield
    for cp in local_copies:
        cp.wait()
    for cp in sib_copies:
        cp.wait_recv()
    for cp in sends:
        cp.wait_send()


def gather_kernel(g, n, *refs):
    srcs, dsts = refs[:n], refs[n : 2 * n]
    send, recv, here = refs[2 * n :]
    greet(plane_peers(g))
    run(gather_steps(g, Wire(send, recv), here, srcs, dsts))


def gather_call(g, srcs, cid):
    n = len(srcs)
    count = n * gather_count(g)
    return pl.pallas_call(
        functools.partial(gather_kernel, g, n),
        out_shape=[jax.ShapeDtypeStruct((g.N * s.shape[0], s.shape[1]), s.dtype) for s in srcs],
        in_specs=[VM] * n,
        out_specs=[ANY] * n,
        scratch_shapes=[
            pltpu.SemaphoreType.DMA((count,)),
            pltpu.SemaphoreType.DMA((count,)),
            pltpu.SemaphoreType.DMA((n,)),
        ],
        compiler_params=pltpu.CompilerParams(collective_id=cid, has_side_effects=True),
        name="gather",
    )(*srcs)


def tp_peers(g):
    t = lax.axis_index("tp")
    return ring_peers(g.T, t, lambda k: {"tp": k})


MIX_XY = at_steps((6, 6, 1), (12, 12, 1), (16, 16, 1), (19, 19, 1))
BACK_Z = ALWAYS
BACK_DOWN = at_steps((0, 7, 1), (9, 9, 1), (18, 18, 1))
BACK_OUT = at_steps((10, 17, 1), (20, 20, 1))
MLP_GATE = at_steps((0, 3, 2), (8, 8, 1), (14, 14, 1))
MLP_UP = at_steps((4, 7, 2), (14, 14, 1), (21, 21, 1))
REC_BRANCH = at_steps((0, 3, 2), (9, 9, 1), (17, 17, 1))
REC_REC = at_steps((4, 7, 2), (13, 13, 1), (19, 19, 1))
REC_SMALL = at_steps((8, 11, 2), (15, 15, 1), (20, 20, 1))
PIECE = 32
CHUNK = 256


def tp_count(g, rows):
    return 4 * (rows // 2 // PIECE)


def tp_place(g):
    t = lax.axis_index("tp")
    side = jnp.where(t >= (g.T + 1) // 2, 1, 0)
    return side, jnp.where(side == 1, g.T - 1 - t, t)


END = {"send_near": 0, "take_far": 8, "take_near": 14}
INNER = {"send_near": 0, "take_far": 2, "pass_far": 6, "take_near": 8}


def tp_steps(g, wire, rows, out, partial=None, finish=None, bufs=None, gather=True):
    T = g.T
    t = lax.axis_index("tp")
    half = rows // 2
    pieces = half // PIECE
    side, pos = tp_place(g)
    end, inner = pos == 0, pos > 0
    near, far = side, 1 - side
    away = {"tp": jnp.where(side == 1, t - 1, t + 1)}
    home = {"tp": jnp.where(side == 1, (t + 1) % T, (t + T - 1) % T)}
    k_rs = wire.used
    if partial is not None:
        wire.used += 2 * pieces
    k_ag = wire.used
    if gather:
        wire.used += 2 * pieces

    def row(d, p):
        return pl.multiple_of(half * (1 - d) + p * PIECE, PIECE)

    def rs(d, p, dev):
        return wire.at(k_rs + d * pieces + p, bufs[1].at[d, p], bufs[2].at[d, p], dev)

    def ag(d, p, dev):
        at = out.at[pl.ds(row(d, p), PIECE)]
        return wire.at(k_ag + d * pieces + p, at, at, dev)

    step = chunk_rows(g, rows, out.shape[1])
    per = step // PIECE

    def ready(d, p, which):
        term = bufs[0].at[which]
        if p % per == 0:
            partial(pl.multiple_of(half * (1 - d) + p * PIECE, step), step, term)
        return term.at[pl.ds(p % per * PIECE, PIECE)]

    def send_near(p, at_end):
        part = ready(near, p, 0)[...]
        if not at_end:
            rs(near, p, away).wait_recv()
            part = part + bufs[2][near, p].astype(F32)
        bufs[1][near, p] = part.astype(BF16)
        rs(near, p, away).start()

    def take_far(p, at_end):
        part = ready(far, p, 1)
        rs(far, p, home).wait_recv()
        total = part[...] + bufs[2][far, p].astype(F32)
        if not at_end:
            bufs[1][far, p] = total.astype(BF16)
            rs(far, p, home).start()
            return
        done = finish(total, p * PIECE, row(far, p), PIECE)
        if gather:
            out[pl.ds(row(far, p), PIECE)] = done
            ag(far, p, away).start()
        else:
            out[p * PIECE : (p + 1) * PIECE] = done

    def pass_far(p, at_end):
        ag(far, p, away).wait_recv()
        ag(far, p, away).start()

    def take_near(p, at_end):
        ag(near, p, home).wait_recv()
        if not at_end:
            ag(near, p, home).start()

    acts = {"send_near": send_near, "take_far": take_far, "pass_far": pass_far, "take_near": take_near}
    if partial is None:

        @pl.when(end)
        def _():
            for p in range(pieces):
                ag(far, p, away).start()

        acts = {"pass_far": pass_far, "take_near": take_near}
        yield
    elif not gather:
        acts = {"send_near": send_near, "take_far": take_far}

    def schedule(lates):
        lates = {k: v for k, v in lates.items() if k in acts}
        least = min(lates.values())
        return [(acts[k], v - least) for k, v in lates.items()]

    plans = [(end, True, schedule(END)), (inner, False, schedule(INNER))]
    for i in range(pieces + max(late for _, _, plan in plans for _, late in plan)):
        for where, at_end, plan in plans:

            @pl.when(where)
            def _():
                for act, late in plan:
                    if 0 <= i - late < pieces:
                        act(i - late, at_end)

        yield
    if partial is not None:
        for p in range(pieces):
            rs(near, p, away).wait_send()
    if gather:
        for p in range(pieces):
            ag(far, p, away).wait_send()

    @pl.when(inner)
    def _():
        for p in range(pieces):
            if partial is not None:
                rs(far, p, home).wait_send()
            if gather:
                ag(near, p, home).wait_send()


def chunk_rows(g, rows, width):
    return min(CHUNK // 2 if needs_turn(width // g.N) else CHUNK, rows // 2)


def tp_bufs(g, rows, width):
    pieces = rows // 2 // PIECE
    return [
        pltpu.VMEM((2, chunk_rows(g, rows, width), width), F32),
        pltpu.VMEM((2, pieces, PIECE, width), BF16),
        pltpu.VMEM((2, pieces, PIECE, width), BF16),
    ]


def transpose_steps(dst, src, scale=None):
    if isinstance(src, Later):
        src = src.ref()
    width = src.shape[1]
    part = 512
    assert width % part == 0

    for at in range(0, width, part):

        def body(j, _):
            c0 = pl.multiple_of(at + j * 128, 128)
            v = src[:, pl.ds(c0, 128)]
            if scale is not None:
                v = (v.astype(F32) * scale[...]).astype(BF16)
            dst[pl.ds(c0, 128), :] = v.T
            return 0

        lax.fori_loop(0, part // 128, body, 0)
        yield


def chain(*steps):
    for s in steps:
        yield from s


def tile_of(width):
    return 512 if width % 512 == 0 else width


def rows_product(term, at, n, pairs):
    width = term.shape[1]
    tile = tile_of(width)

    def body(j, _):
        c0 = pl.multiple_of(j * tile, tile)
        total = None
        for l, r in pairs:
            p = dot_rows(l[pl.ds(at, n)], r[pl.ds(c0, tile)])
            total = p if total is None else total + p
        term[:, pl.ds(c0, tile)] = total
        return 0

    lax.fori_loop(0, width // tile, body, 0)


def mean_square(v):
    return jnp.mean(v * v, axis=-1, keepdims=True)


def mix_out_body(ins, outs):
    mixed, w_out, x, gain = ins
    _, middle = outs

    def partial(at, n, term):
        rows_product(term, at, n, [(mixed, w_out)])

    def finish(total, near, at, n):
        m = x[pl.ds(at, n)].astype(F32) + total
        middle[near : near + n] = m
        return (m * lax.rsqrt(mean_square(m) + EPS) * gain[...]).astype(BF16)

    return partial, finish


def mlp_out_body(ins, outs):
    hidden, w_down, middle, live = ins

    def partial(at, n, term):
        rows_product(term, at, n, [(hidden, w_down)])

    def finish(total, near, at, n):
        return ((middle[near : near + n] + total) * live[pl.ds(at, n)]).astype(BF16)

    return partial, finish


def norm_back(grad_normed, rows, gain):
    inv = lax.rsqrt(mean_square(rows) + EPS)
    gg = grad_normed * gain
    back = inv * gg - rows * (inv * inv * inv) * jnp.mean(gg * rows, axis=-1, keepdims=True)
    return back, jnp.sum(grad_normed * rows * inv, axis=0, keepdims=True)


def mlp_back_body(ins, outs):
    gate_low, up_low, w_gate, w_up, middle, cot, live, gain = ins
    _, grad_middle, grad_gain = outs
    grad_gain[...] = jnp.zeros_like(grad_gain)

    def partial(at, n, term):
        rows_product(term, at, n, [(gate_low, w_gate), (up_low, w_up)])

    def finish(total, near, at, n):
        back, gain_sum = norm_back(total, middle[near : near + n], gain[...])
        gm = cot[pl.ds(at, n)].astype(F32) * live[pl.ds(at, n)] + back
        grad_middle[near : near + n] = gm
        grad_gain[...] = grad_gain[...] + gain_sum
        return gm.astype(BF16)

    return partial, finish


def rec_back_body(ins, outs):
    branch_low, rec_low, w_branch, w_rec, x, grad_middle, gain = ins
    _, grad_gain = outs
    grad_gain[...] = jnp.zeros_like(grad_gain)

    def partial(at, n, term):
        rows_product(term, at, n, [(branch_low, w_branch), (rec_low, w_rec)])

    def finish(total, near, at, n):
        back, gain_sum = norm_back(total, x[pl.ds(at, n)].astype(F32), gain[...])
        grad_gain[...] = grad_gain[...] + gain_sum
        return (grad_middle[near : near + n] + back).astype(BF16)

    return partial, finish


TAPS, SHIFT, RBIAS, EBIAS, SOFT, SLOPE = 0, 4, 5, 6, 7, 8
ROWS = 64
GROUP = 8


def ctx_peers(g):
    q = lax.axis_index("ctx")
    return [{"ctx": (q + k) % g.Q} for k in range(1, g.Q)]


def swap_edges(g, wire, src, land):
    q = lax.axis_index("ctx")
    cps = []
    for k in range(1, g.Q):
        cp = wire.copy(src, land.at[q], {"ctx": (q + k) % g.Q})
        cp.start()
        cps.append(cp)
    for cp in cps:
        cp.wait_recv()
    for cp in cps:
        cp.wait_send()


def row_shift(v, n):
    return pltpu.roll(v, n % v.shape[0], 0)


def forward_steps(g, wire, rec, branch, w_rate, w_entry, vecs, mixed, conv, rate, entry, state, edge,
                  ext, acum, bcum, tot, halo, gath):
    L, CH = rec.shape
    q = lax.axis_index("ctx")
    ext[8:] = rec[...]
    if g.Q > 1:
        cp = wire.copy(ext.at[pl.ds(L, 8)], halo, {"ctx": (q + 1) % g.Q})
        cp.start()
        yield
        cp.wait()
        ext[0:8] = jnp.where(q > 0, halo[...], 0.0)
    else:
        ext[0:8] = jnp.zeros((8, CH), F32)
    sub = lax.broadcasted_iota(jnp.int32, (GROUP, 1), 0)

    def chunk(i, carry):
        ca, cb = carry
        r0 = i * ROWS
        wide = ext[pl.ds(r0, ROWS + 8)]
        c = vecs[SHIFT : SHIFT + 1] + vecs[TAPS : TAPS + 1] * wide[8:]
        for k in range(1, 4):
            c = c + vecs[TAPS + k : TAPS + k + 1] * row_shift(wide, k)[8:]
        conv[pl.ds(r0, ROWS)] = c
        hi, lo = halves(c)
        gr = sigmoid(dot(hi, w_rate[...]) + dot(lo, w_rate[...]) + vecs[RBIAS : RBIAS + 1])
        ge = sigmoid(dot(hi, w_entry[...]) + dot(lo, w_entry[...]) + vecs[EBIAS : EBIAS + 1])
        rate[pl.ds(r0, ROWS)] = gr
        entry[pl.ds(r0, ROWS)] = ge
        log = -DECAY_SCALE * gr * vecs[SOFT : SOFT + 1]
        dec = jnp.exp(log)
        drive = jnp.sqrt(minus_expm1(2.0 * log)) * ge * c
        for n in range(ROWS // GROUP):
            A = dec[n * GROUP : (n + 1) * GROUP]
            B = drive[n * GROUP : (n + 1) * GROUP]
            for step in (1, 2, 4):
                keep = sub >= step
                As = jnp.where(keep, row_shift(A, step), 1.0)
                Bs = jnp.where(keep, row_shift(B, step), 0.0)
                B = B + A * Bs
                A = A * As
            B = B + A * cb
            A = A * ca
            acum[pl.ds(r0 + n * GROUP, GROUP)] = A
            bcum[pl.ds(r0 + n * GROUP, GROUP)] = B
            ca = A[GROUP - 1 : GROUP]
            cb = B[GROUP - 1 : GROUP]
        return ca, cb

    ca, cb = jnp.ones((1, CH), F32), jnp.zeros((1, CH), F32)
    for i in range(L // ROWS):
        ca, cb = chunk(i, (ca, cb))
        yield
    tot[0:1] = ca
    tot[1:2] = cb
    start = jnp.zeros((1, CH), F32)
    if g.Q > 1:
        swap_edges(g, wire, tot, gath)
        for d in range(g.Q - 1):
            new = gath[d, 0:1] * start + gath[d, 1:2]
            start = jnp.where(d < q, new, start)
    edge[...] = jnp.broadcast_to(start, (8, CH))
    yield

    def fix(i, _):
        r0 = pl.multiple_of(i * ROWS, ROWS)
        s = bcum[pl.ds(r0, ROWS)] + acum[pl.ds(r0, ROWS)] * start
        state[pl.ds(r0, ROWS)] = s
        mixed[pl.ds(r0, ROWS)] = (gelu_both(branch[pl.ds(r0, ROWS)])[0] * s).astype(BF16)
        return 0

    lax.fori_loop(0, L // ROWS, fix, 0)
    yield


def forward_scratch(g, L, CH):
    return [
        pltpu.VMEM((L + 8, CH), F32),
        pltpu.VMEM((L, CH), F32),
        pltpu.VMEM((L, CH), F32),
        pltpu.VMEM((8, CH), F32),
        pltpu.VMEM((8, CH), F32),
        pltpu.VMEM((g.Q, 8, CH), F32),
    ]


def mix_call(g, rec, branch, w_rate, w_entry, vecs, x, gain, out_shard, mlp_shards, cid):
    L, CH = rec.shape
    width = x.shape[1]
    chunk = L // 2
    n = len(mlp_shards)
    wide = jax.ShapeDtypeStruct((L, CH), F32)
    whole = [jax.ShapeDtypeStruct((g.N * s.shape[0], s.shape[1]), s.dtype) for s in [out_shard] + mlp_shards]
    n_fwd = len(forward_scratch(g, L, CH))
    count = 2 * g.Q + tp_count(g, L) + (n + 1) * gather_count(g)

    def kernel(rec, branch, w_rate, w_entry, vecs, x, gain, shard, *refs):
        shards = refs[:n]
        mixed, conv, rate, entry, state, edge, low_two, middle, w_out = refs[n : n + 9]
        full = refs[n + 9 : 2 * n + 9]
        fwd = refs[2 * n + 9 : 2 * n + 9 + n_fwd]
        term, sendbuf, recvbuf, send, recv, here = refs[2 * n + 9 + n_fwd :]
        greet(ctx_peers(g) + plane_peers(g) + tp_peers(g))
        wire = Wire(send, recv)
        fwd_steps = forward_steps(g, wire, rec, branch, w_rate, w_entry, vecs, mixed, conv, rate, entry, state, edge, *fwd)
        first = gather_steps(g, wire, here.at[pl.ds(0, 1)], [shard], [w_out])
        rest = gather_steps(g, wire, here.at[pl.ds(1, n)], shards, full)
        next(fwd_steps)
        next(first)
        for _ in range(L // ROWS + 1):
            next(fwd_steps)
        next(first)
        for _ in range(n):
            next(rest)
        run(fwd_steps)
        run(first)
        partial, finish = mix_out_body((mixed, w_out, x, gain), (low_two, middle))
        braid(
            tp_steps(g, wire, L, low_two, partial, finish, (term, sendbuf, recvbuf)),
            (rest, MIX_XY),
        )

    return call(
        kernel,
        [rec, branch, w_rate, w_entry, vecs, x, gain, out_shard, *mlp_shards],
        [jax.ShapeDtypeStruct((L, CH), BF16), wide, wide, wide, wide, jax.ShapeDtypeStruct((8, CH), F32),
         jax.ShapeDtypeStruct((L, width), BF16), jax.ShapeDtypeStruct((chunk, width), F32), *whole],
        forward_scratch(g, L, CH) + tp_bufs(g, L, width) + sems(count) + [pltpu.SemaphoreType.DMA((n + 1,))],
        cid,
        "mix",
        [VM] * (n + 8),
        [VM] * 9 + [ANY] * n,
    )


def backward_steps(g, wire, mid_low, w_out, branch, rec, conv, rate, entry, state, edge, w_rate, w_entry, vecs,
                    branch_low, rec_low, g_rate, g_entry, g_vecs,
                    sgrad, acum, bcum, conv_h, conv_l, rb_h, rb_l, eb_h, eb_l, tot, gath, halo, prevx):
    L, CH = rec.shape
    gconv = sgrad
    q = lax.axis_index("ctx")
    tail = None
    if g.Q > 1:
        tail = wire.copy(rec.at[pl.ds(L - 8, 8)], prevx, {"ctx": (q + 1) % g.Q})
        tail.start()
    sub = lax.broadcasted_iota(jnp.int32, (GROUP, 1), 0)
    chunks = L // ROWS

    def product_cols(j, _):
        cols = pl.ds(pl.multiple_of(j * 128, 128), 128)
        sgrad[:L, cols] = dot(mid_low[...], w_out[:, cols])
        return 0

    if CH % 128 == 0:
        lax.fori_loop(0, CH // 128, product_cols, 0)
    else:
        sgrad[:L] = dot(mid_low[...], w_out[...])

    def chunk(j, carry):
        ua, ub = carry
        r0 = (chunks - 1 - j) * ROWS
        gm = sgrad[pl.ds(r0, ROWS)]
        act, slope = gelu_both(branch[pl.ds(r0, ROWS)])
        branch_low[pl.ds(r0, ROWS)] = (gm * state[pl.ds(r0, ROWS)] * slope).astype(BF16)
        sg = gm * act
        sgrad[pl.ds(r0, ROWS)] = sg
        dec = jnp.exp(-DECAY_SCALE * rate[pl.ds(r0, ROWS)] * vecs[SOFT : SOFT + 1])
        sg = dec * sg
        for n in reversed(range(ROWS // GROUP)):
            A = dec[n * GROUP : (n + 1) * GROUP]
            B = sg[n * GROUP : (n + 1) * GROUP]
            for step in (1, 2, 4):
                keep = sub < GROUP - step
                As = jnp.where(keep, row_shift(A, -step), 1.0)
                Bs = jnp.where(keep, row_shift(B, -step), 0.0)
                B = B + A * Bs
                A = A * As
            B = B + A * ub
            A = A * ua
            acum[pl.ds(r0 + n * GROUP, GROUP)] = A
            bcum[pl.ds(r0 + n * GROUP, GROUP)] = B
            ua = A[0:1]
            ub = B[0:1]
        return ua, ub

    yield
    ua, ub = jnp.ones((1, CH), F32), jnp.zeros((1, CH), F32)
    for i in range(chunks):
        ua, ub = chunk(i, (ua, ub))
        yield
    tot[0:1] = ua
    tot[1:2] = ub
    arriving = jnp.zeros((1, CH), F32)
    if g.Q > 1:
        swap_edges(g, wire, tot, gath)
        for d in reversed(range(1, g.Q)):
            new = gath[d, 0:1] * arriving + gath[d, 1:2]
            arriving = jnp.where(d > q, new, arriving)
        tail.wait()
    acum[L:] = jnp.ones((8, CH), F32)
    bcum[L:] = jnp.zeros((8, CH), F32)
    zero = jnp.zeros((1, CH), F32)
    if g.Q > 1:
        prev_rows = jnp.where(q > 0, prevx[...], 0.0)
    else:
        prev_rows = jnp.zeros((8, CH), F32)

    def back(i, carry):
        gdec, gbr, gbe, gshift, gt0, gt1, gt2, gt3, last_state, last_rec = carry
        r0 = i * ROWS
        aw = row_shift(acum[pl.ds(r0, ROWS + 8)], -1)[:ROWS]
        bw = row_shift(bcum[pl.ds(r0, ROWS + 8)], -1)[:ROWS]
        car = sgrad[pl.ds(r0, ROWS)] + bw + aw * arriving
        st = state[pl.ds(r0, ROWS)]
        prev = row_shift(jnp.concatenate([last_state, st], axis=0), 1)[8:]
        gr = rate[pl.ds(r0, ROWS)]
        ge = entry[pl.ds(r0, ROWS)]
        c = conv[pl.ds(r0, ROWS)]
        soft = vecs[SOFT : SOFT + 1]
        log = -DECAY_SCALE * gr * soft
        dec = jnp.exp(log)
        scale = jnp.sqrt(minus_expm1(2.0 * log))
        ec = ge * c
        glog = car * prev * dec - car * ec * dec * dec / scale
        glr = 8.0 * glog * gr
        gdec = gdec + jnp.sum(glr, axis=0, keepdims=True)
        rb = -glr * soft * (1.0 - gr)
        cs = car * scale
        eb = cs * ec * (1.0 - ge)
        gbr = gbr + jnp.sum(rb, axis=0, keepdims=True)
        gbe = gbe + jnp.sum(eb, axis=0, keepdims=True)
        rh, rl = halves(rb)
        eh, el = halves(eb)
        ch, cl = halves(c)
        rb_h[pl.ds(r0, ROWS)] = rh
        rb_l[pl.ds(r0, ROWS)] = rl
        eb_h[pl.ds(r0, ROWS)] = eh
        eb_l[pl.ds(r0, ROWS)] = el
        conv_h[pl.ds(r0, ROWS)] = ch
        conv_l[pl.ds(r0, ROWS)] = cl
        wr, we = w_rate[...], w_entry[...]
        gc = cs * ge + dot_rows(rh, wr) + dot_rows(rl, wr) + dot_rows(eh, we) + dot_rows(el, we)
        gconv[pl.ds(r0, ROWS)] = gc
        gshift = gshift + jnp.sum(gc, axis=0, keepdims=True)
        x = rec[pl.ds(r0, ROWS)]
        wide = jnp.concatenate([last_rec, x], axis=0)
        gts = [gt0, gt1, gt2, gt3]
        for k in range(4):
            xk = x if k == 0 else row_shift(wide, k)[8:]
            gts[k] = gts[k] + jnp.sum(gc * xk, axis=0, keepdims=True)
        return (gdec, gbr, gbe, gshift, *gts, st[ROWS - 8 :], x[ROWS - 8 :])

    yield
    carry = (zero,) * 8 + (edge[...], prev_rows)
    for i in range(chunks):
        carry = back(i, carry)
        yield
    gdec, gbr, gbe, gshift, gt0, gt1, gt2, gt3 = carry[:8]
    if g.Q > 1:
        cp = wire.copy(gconv.at[pl.ds(0, 8)], halo, {"ctx": (q + g.Q - 1) % g.Q})
        cp.start()
    gdec = gdec * vecs[SLOPE : SLOPE + 1]
    for k, v in enumerate((gt0, gt1, gt2, gt3, gshift, gbr, gbe, gdec)):
        g_vecs[k : k + 1] = v
    yield

    def product(h, l):
        return dot_tokens(conv_h[...], h[...]) + dot_tokens(conv_l[...], h[...]) + dot_tokens(conv_h[...], l[...])

    bw = g_rate.shape[0]
    head = lax.broadcasted_iota(jnp.int32, (bw, CH), 1) // bw

    def diagonal(dense):
        total = jnp.zeros((bw, CH), F32)
        for h in range(CH // bw):
            total = total + jnp.where(head == h, dense[h * bw : (h + 1) * bw], 0.0)
        return total

    g_rate[...] = diagonal(product(rb_h, rb_l))
    yield
    g_entry[...] = diagonal(product(eb_h, eb_l))
    yield
    if g.Q > 1:
        cp.wait()
        gconv[L:] = jnp.where(q < g.Q - 1, halo[...], 0.0)
    else:
        gconv[L:] = jnp.zeros((8, CH), F32)

    def last(i, _):
        r0 = pl.multiple_of(i * ROWS, ROWS)
        wide = gconv[pl.ds(r0, ROWS + 8)]
        total = vecs[TAPS : TAPS + 1] * wide[:ROWS]
        for k in range(1, 4):
            total = total + vecs[TAPS + k : TAPS + k + 1] * row_shift(wide, -k)[:ROWS]
        rec_low[pl.ds(r0, ROWS)] = total.astype(BF16)
        return 0

    lax.fori_loop(0, chunks, last, 0)
    yield


def back_call(g, mid_low, w_out, branch, rec, conv, rate, entry, state, edge, w_rate, w_entry, vecs, bw, middle,
              cot, live, hidden, w_down, mixed, cid):
    L, CH = rec.shape
    half, width = middle.shape
    low = jax.ShapeDtypeStruct((L, CH), BF16)
    diag = jax.ShapeDtypeStruct((bw, CH), F32)
    F = hidden.shape[1]
    rows = width // g.N
    count = g.Q + 2 + tp_count(g, L) + 2 * reduce_count(g)
    operands = [mid_low, w_out, branch, rec, conv, rate, entry, state, edge, w_rate, w_entry, vecs,
                middle, cot, live, hidden, w_down, mixed]

    def kernel(*refs):
        ins, (middle, cot, live, hidden, w_down, mixed) = refs[:12], refs[12:18]
        outs, (output, g_down, g_out) = refs[18:23], refs[23:26]
        bufs = refs[26:39]
        cot_t, term, sendbuf, recvbuf, *more = refs[39:]
        mid_t = cot_t
        send, recv = more[-2:]
        greet(ctx_peers(g) + tp_peers(g) + plane_peers(g))
        wire = Wire(send, recv)

        def z():
            yield
            body = mlp_out_body((hidden.ref(), w_down.ref(), middle, live), (output,))
            yield from tp_steps(g, wire, L, output, *body, (term, sendbuf, recvbuf))

        def down():
            yield from turn_steps(rows, cot_t, cot, live)
            hidden.ref()
            yield from reduce_steps(g, wire, [(product_term(cot.dst, cot_t, hidden.dst, rows, live), g_down, more[0:3])])

        down_steps = down()
        if needs_turn(rows):
            for _ in range(len(range(0, width, 512)) + g.C * g.A * g.B):
                next(down_steps)

        def out():
            yield from turn_steps(rows, mid_t, ins[0])
            mixed.ref()
            yield from reduce_steps(g, wire, [(product_term(ins[0], mid_t, mixed.dst, rows), g_out, more[3:6])])

        braid(
            chain(backward_steps(g, wire, *ins, *outs, *bufs), iter(range(4))),
            (z(), BACK_Z),
            (down_steps, BACK_DOWN),
            (out(), BACK_OUT),
        )

    return call(
        kernel,
        operands,
        [low, low, diag, diag, jax.ShapeDtypeStruct((8, CH), F32), jax.ShapeDtypeStruct((L, width), BF16),
         jax.ShapeDtypeStruct((rows, F), F32), jax.ShapeDtypeStruct((rows, CH), F32)],
        [
            pltpu.VMEM((L + 8, CH), F32),
            pltpu.VMEM((L + 8, CH), F32),
            pltpu.VMEM((L + 8, CH), F32),
        ]
        + [pltpu.VMEM((L, CH), BF16)] * 6
        + [
            pltpu.VMEM((8, CH), F32),
            pltpu.VMEM((g.Q, 8, CH), F32),
            pltpu.VMEM((8, CH), F32),
            pltpu.VMEM((8, CH), F32),
        ]
        + turn_scratch(rows, width, L)
        + tp_bufs(g, L, width)
        + reduce_bufs(g, rows, F)
        + reduce_bufs(g, rows, CH)
        + sems(count),
        cid,
        "rec_backward",
        later=(15, 16, 13, 17),
    )


def reduce_count(g):
    ring = 0
    for nf, ng in ((g.A, g.B), (g.B, g.A)):
        ring += (nf - 1) * ng + (ng - 1)
    return ring + (g.C - 1) * g.A * g.B


def reduce_bufs(g, rows, width):
    nb = g.A * g.B
    arrivals = reduce_count(g) - (g.C - 1) * nb
    return [
        pltpu.VMEM((nb, rows, width), BF16),
        pltpu.VMEM((nb, rows, width), BF16),
        pltpu.VMEM((max(1, arrivals), rows // 2, width), BF16),
    ]


def reduce_steps(g, wire, items):
    a, b, c = g.me()
    sends = []

    def start(src, dst, dev):
        cp = wire.copy(src, dst, dev)
        cp.start()
        sends.append(cp)
        return cp

    nb = g.A * g.B

    def owner(k, core):
        return g.block((a + g.A - k // g.B) % g.A, (b + g.B - k % g.B) % g.B, core)

    def each_tile(width, fn):
        fn(slice(None))

    rings = [(g.A, g.B), (g.B, g.A)]
    devs = [
        (g.dev((a + 1) % g.A, b, c), g.dev(a, (b + 1) % g.B, c)),
        (g.dev(a, (b + 1) % g.B, c), g.dev((a + 1) % g.A, b, c)),
    ]

    def slot(h, df, dg):
        return df * g.B + dg if h == 0 else dg * g.B + df

    bases = []
    state = []
    for term, out, (to_sib, sums, land) in items:
        half = out.shape[0] // 2
        base = wire.used
        bases.append(base)
        if g.C == 2:
            wire.used += nb
            for k in [(i + 1) % nb for i in range(nb)]:

                def tile(cols):
                    to_sib[k, :, cols] = term(owner(k, 1 - c), cols).astype(BF16)

                each_tile(out.shape[1], tile)
                wire.at(base + k, to_sib.at[k], sums.at[k], g.dev(a, b, 1 - c)).start()
                yield
        used = 0
        first = ({}, {})
        for k in [(i + 1) % nb for i in range(nb)]:
            if g.C == 2:
                wire.at(base + k, to_sib.at[k], sums.at[k], g.dev(a, b, 1 - c)).wait_recv()

            def tile(cols):
                s = term(owner(k, c), cols)
                if g.C == 2:
                    s = s + sums[k, :, cols].astype(F32)
                if k == 0:
                    out[:, cols] = s
                else:
                    sums[k, :, cols] = s.astype(BF16)

            each_tile(out.shape[1], tile)
            for h in (0, 1):
                nf, ng = rings[h]
                df, dg = (k // g.B, k % g.B) if h == 0 else (k % g.B, k // g.B)
                if nf > 1 and df == 1:
                    first[h][dg] = (start(sums.at[k, pl.ds(h * half, half)], land.at[used], devs[h][0]), used)
                    used += 1
            yield
        state.append([first, used])

    def add(out, sums, k, h, half, arrived):
        at = slice(h * half, (h + 1) * half)
        if k == 0:
            out[at] = out[at] + arrived.astype(F32)
        else:
            sums[k, at] = (sums[k, at].astype(F32) + arrived.astype(F32)).astype(BF16)

    seconds = []
    for (term, out, (to_sib, sums, land)), st in zip(items, state):
        half = out.shape[0] // 2
        first, used = st
        second = [None, None]
        for h in (0, 1):
            nf, ng = rings[h]
            for i in range(1, nf):
                df = (i + 1) % nf
                for dg in [d % ng for d in range(1, ng + 1)]:
                    cp, at = first[h][dg]
                    cp.wait_recv()
                    k = slot(h, df, dg)
                    add(out, sums, k, h, half, land[at])
                    if i < nf - 1:
                        first[h][dg] = (start(sums.at[k, pl.ds(h * half, half)], land.at[used], devs[h][0]), used)
                        used += 1
                    elif dg == 1 and ng > 1:
                        second[h] = (start(sums.at[k, pl.ds(h * half, half)], land.at[used], devs[h][1]), used)
                        used += 1
            if nf == 1 and ng > 1:
                k = slot(h, 0, 1)
                second[h] = (start(sums.at[k, pl.ds(h * half, half)], land.at[used], devs[h][1]), used)
                used += 1
        seconds.append([second, used])
        yield
    for (term, out, (to_sib, sums, land)), (second, used) in zip(items, seconds):
        half = out.shape[0] // 2
        for h in (0, 1):
            nf, ng = rings[h]
            for j in range(1, ng):
                cp, at = second[h]
                cp.wait_recv()
                k = slot(h, 0, (j + 1) % ng)
                add(out, sums, k, h, half, land[at])
                if j < ng - 1:
                    second[h] = (start(sums.at[k, pl.ds(h * half, half)], land.at[used], devs[h][1]), used)
                    used += 1
        yield
    for cp in sends:
        cp.wait_send()
    if g.C == 2:
        for (term, out, (to_sib, sums, land)), base in zip(items, bases):
            for k in range(nb):
                wire.at(base + k, to_sib.at[k], sums.at[k], g.dev(a, b, 1 - c)).wait_send()


def needs_turn(rows):
    return rows % 128 != 0


def turn_scratch(rows, width, L):
    return [pltpu.VMEM((width, L) if needs_turn(rows) else (16, 128), BF16)]


def product_term(left, turned, right, rows, mask=None):
    def term(block, cols):
        at = pl.ds(pl.multiple_of(block * rows, rows), rows)
        if needs_turn(rows):
            return dot(turned[at], right[:, cols])
        v = left[:, at]
        if mask is not None:
            v = (v.astype(F32) * mask[...]).astype(BF16)
        return dot_tokens(v, right[:, cols])

    return term


def turn_steps(rows, turned, left, mask=None):
    if isinstance(left, Later):
        left = left.ref()
    if needs_turn(rows):
        yield from transpose_steps(turned, left, mask)


def given_term(part, rows):
    def term(block, cols):
        return part[pl.ds(pl.multiple_of(block * rows, rows), rows), cols]

    return term


def mlp_back_call(g, low_two, gate_low, up_low, w_gate, w_up, middle, cot, live, gain, cid):
    L, width = low_two.shape
    F = gate_low.shape[1]
    half = L // 2
    rows = width // g.N
    count = tp_count(g, L) + 2 * reduce_count(g)
    grad = jax.ShapeDtypeStruct((rows, F), F32)

    def kernel(low_two, gate_low, up_low, w_gate, w_up, middle, cot, live, gain,
               mid_low, grad_middle, grad_gain, g_gate, g_up,
               two_t, term, sendbuf, recvbuf, *refs):
        send, recv = refs[-2:]
        bufs = refs[:-2]
        greet(plane_peers(g) + tp_peers(g))
        wire = Wire(send, recv)
        middle, cot = middle.ref(), cot.ref()
        back = mlp_back_body((gate_low, up_low, w_gate, w_up, middle, cot, live, gain), (mid_low, grad_middle, grad_gain))

        def gate():
            yield from turn_steps(rows, two_t, low_two)
            yield from reduce_steps(g, wire, [(product_term(low_two.dst, two_t, gate_low, rows), g_gate, bufs[0:3])])

        def up():
            yield from reduce_steps(g, wire, [(product_term(low_two.dst, two_t, up_low, rows), g_up, bufs[3:6])])

        braid(
            tp_steps(g, wire, L, mid_low, *back, (term, sendbuf, recvbuf)),
            (gate(), MLP_GATE),
            (up(), MLP_UP),
        )

    scratch = turn_scratch(rows, width, L) + tp_bufs(g, L, width)
    for _ in range(2):
        scratch += reduce_bufs(g, rows, F)
    return call(
        kernel,
        [low_two, gate_low, up_low, w_gate, w_up, middle, cot, live, gain],
        [jax.ShapeDtypeStruct((L, width), BF16), jax.ShapeDtypeStruct((half, width), F32),
         jax.ShapeDtypeStruct((1, width), F32), grad, grad],
        scratch + sems(count),
        cid,
        "mlp_back",
        later=(0, 5, 6),
    )


def plane_others(g):
    s, q = lax.axis_index("shard"), lax.axis_index("ctx")
    me = s * g.Q + q
    out = []
    for k in range(1, g.N):
        d = (me + k) % g.N
        out.append({"shard": d // g.Q, "ctx": d % g.Q})
    return me, out


def total_steps(g, wire, mine, land_t, land_p, out):
    t = lax.axis_index("tp")
    me, others = plane_others(g)
    land_t[t] = mine[...]
    cps = [wire.copy(mine, land_t.at[t], {"tp": (t + k) % g.T}) for k in range(1, g.T)]
    for cp in cps:
        cp.start()
    yield
    for cp in cps:
        cp.wait()
    total = land_t[0]
    for d in range(1, g.T):
        total = total + land_t[d]
    mine[...] = total
    land_p[me] = total
    cps = [wire.copy(mine, land_p.at[me], d) for d in others]
    for cp in cps:
        cp.start()
    yield
    for cp in cps:
        cp.wait()
    total = land_p[0]
    for d in range(1, g.N):
        total = total + land_p[d]
    out[...] = total


def rec_back_call(g, branch_low, rec_low, w_branch, w_rec, x, grad_middle, gain, part_two, low_one, small, cid):
    L, width = x.shape
    CH = branch_low.shape[1]
    rows = width // g.N
    srows = small.shape[0] // g.N
    shapes = [(rows, CH), (rows, CH), (srows, small.shape[1])]
    count = tp_count(g, L) + len(shapes) * reduce_count(g) + g.T + g.N

    def kernel(branch_low, rec_low, w_branch, w_rec, x, grad_middle, gain, part_two, low_one, small,
               input_grad, gains, g_branch, g_rec, g_small,
               part_one, one_t, both, land_t, land_p, term, sendbuf, recvbuf, *refs):
        send, recv = refs[-2:]
        bufs = refs[:-2]
        t = lax.axis_index("tp")
        greet(plane_others(g)[1] + [{"tp": (t + k) % g.T} for k in range(1, g.T)])
        wire = Wire(send, recv)
        x, grad_middle = x.ref(), grad_middle.ref()
        back = rec_back_body((branch_low, rec_low, w_branch, w_rec, x, grad_middle, gain), (input_grad, part_one))

        def one(term, out, bufs):
            yield from reduce_steps(g, wire, [(term, out, bufs)])

        def branch():
            yield from turn_steps(rows, one_t, low_one)
            yield from one(product_term(low_one.dst, one_t, branch_low, rows), g_branch, bufs[0:3])

        def main():
            steps = tp_steps(g, wire, L, input_grad, *back, (term, sendbuf, recvbuf))
            for _ in range(L // 2 // PIECE + END["take_far"]):
                next(steps)
                yield
            both[:, :width] = part_one[...]
            both[:, width:] = part_two[...]
            totals = total_steps(g, wire, both, land_t, land_p, gains)
            next(totals)
            for _ in steps:
                next(totals, None)
                yield
            run(totals)

        braid(
            main(),
            (branch(), REC_BRANCH),
            (one(product_term(low_one.dst, one_t, rec_low, rows), g_rec, bufs[3:6]), REC_REC),
            (one(given_term(small, srows), g_small, bufs[6:9]), REC_SMALL),
        )

    scratch = [pltpu.VMEM((1, width), F32)] + turn_scratch(rows, width, L)
    scratch += [pltpu.VMEM((1, 2 * width), F32), pltpu.VMEM((g.T, 1, 2 * width), F32), pltpu.VMEM((g.N, 1, 2 * width), F32)]
    scratch += tp_bufs(g, L, width)
    for s in shapes:
        scratch += reduce_bufs(g, *s)
    return call(
        kernel,
        [branch_low, rec_low, w_branch, w_rec, x, grad_middle, gain, part_two, low_one, small],
        [jax.ShapeDtypeStruct((L, width), BF16), jax.ShapeDtypeStruct((1, 2 * width), F32)]
        + [jax.ShapeDtypeStruct(s, F32) for s in shapes],
        scratch + sems(count),
        cid,
        "rec_back",
        later=(8, 4, 5),
    )


def settle(arrays):
    n = len(arrays)

    def kernel(*refs):
        ins, outs, kept, sem = refs[:n], refs[n : 2 * n], refs[2 * n : 3 * n], refs[3 * n]
        cps = [pltpu.make_async_copy(ins[k], kept[k], sem.at[k]) for k in range(n)]
        back = [pltpu.make_async_copy(kept[k], outs[k], sem.at[n + k]) for k in range(n)]
        for cp in cps:
            cp.start()
        for k in range(n):
            cps[k].wait()
            back[k].start()
        for cp in back:
            cp.wait()

    return pl.pallas_call(
        kernel,
        out_shape=[jax.ShapeDtypeStruct(v.shape, v.dtype) for v in arrays],
        in_specs=[ANY] * n,
        out_specs=[ANY] * n,
        scratch_shapes=[pltpu.VMEM(v.shape, v.dtype) for v in arrays] + [pltpu.SemaphoreType.DMA((2 * n,))],
        compiler_params=pltpu.CompilerParams(vmem_limit_bytes=VMEM_LIMIT),
        name="settle",
    )(*arrays)


def up_to(n, k):
    return -(-n // k) * k


def small_pack(parts, rows, width):
    flat = jnp.concatenate([p.reshape(-1) for p in parts])
    return jnp.pad(flat, (0, rows * width - flat.shape[0])).reshape(rows, width)


def block_dense(blocks):
    n, w = blocks.shape[0], blocks.shape[1]
    eye = jnp.eye(n, dtype=blocks.dtype)
    return (blocks[:, :, None, :] * eye[:, None, :, None]).reshape(n * w, n * w)


def local(g, inputs, lengths, cotangent, norm1_gain, branch_weight, rec_in_weight, conv_weight, conv_bias,
          rgate_weight, rgate_bias, igate_weight, igate_bias, decay_param, out_weight, norm2_gain,
          mlp_gate_weight, mlp_up_weight, mlp_down_weight):
    slots, block_len, width = inputs.shape
    L = slots * block_len
    N, T = g.N, g.T
    heads, rb, bw = rgate_weight.shape
    ch = heads * bw
    taps = conv_weight.shape[0]
    small = [rgate_weight, igate_weight, conv_weight, conv_bias, rgate_bias, igate_bias, decay_param, norm1_gain, norm2_gain]
    sizes = [p.size for p in small]
    srows = up_to(-(-sum(sizes) // 256), 32)
    pack = small_pack(small, srows, 256)

    packs, w_branch, w_rec = gather_call(g, [pack, branch_weight, rec_in_weight], 0)
    packs = packs.reshape(N, -1)
    cut, at = [], 0
    for p, s in zip(small, sizes):
        cut.append(packs[:, at : at + s].reshape((N,) + p.shape))
        at += s
    w_rate = block_dense(cut[0].transpose(1, 0, 2, 3).reshape(heads, bw, bw))
    w_entry = block_dense(cut[1].transpose(1, 0, 2, 3).reshape(heads, bw, bw))
    taps_f = cut[2].transpose(1, 2, 0, 3).reshape(taps, ch).astype(F32)

    def channels(v):
        return v.transpose(1, 0, 2).reshape(1, ch).astype(F32)

    decay_f = channels(cut[6])
    vecs = jnp.concatenate(
        [taps_f, channels(cut[3]), channels(cut[4]), channels(cut[5]), jax.nn.softplus(-decay_f), jax.nn.sigmoid(-decay_f),
         jnp.zeros((7, ch), F32)], axis=0
    )
    gain_one = cut[7].reshape(1, width).astype(F32)
    gain_two = cut[8].reshape(1, width).astype(F32)

    x_low = inputs.reshape(L, width)
    cot = cotangent.reshape(L, width)
    positions = lax.axis_index("ctx") * block_len + jnp.arange(block_len, dtype=jnp.int32)
    live = (positions[None, :] < lengths[:, None]).astype(F32).reshape(L, 1)
    x_f = x_low.astype(F32)
    low_one = (x_f * lax.rsqrt(mean_square(x_f) + EPS) * gain_one).astype(BF16)
    branch_pre = dot(low_one, w_branch)
    rec_pre = dot(low_one, w_rec)
    mixed, conv, rate, entry, state, edge, low_two, middle, w_out, w_gate, w_up, w_down = mix_call(
        g, rec_pre, branch_pre, w_rate, w_entry, vecs, x_low, gain_two, out_weight,
        [mlp_gate_weight, mlp_up_weight, mlp_down_weight], 1
    )
    gate_pre = dot(low_two, w_gate)
    up_pre = dot(low_two, w_up)
    act, slope = gelu_both(gate_pre)
    hidden = (act * up_pre).astype(BF16)
    grad_low = (cot.astype(F32) * live).astype(BF16)
    grad_hidden = dot(grad_low, w_down)
    gate_low = (grad_hidden * up_pre * slope).astype(BF16)
    up_low = (grad_hidden * act).astype(BF16)
    mid_low, grad_middle, part_two, g_gate, g_up = mlp_back_call(
        g, low_two, gate_low, up_low, w_gate, w_up, middle, cot, live, gain_two, 2
    )
    branch_low, rec_low, d_rate, d_entry, d_vecs, output, g_down, g_out = back_call(
        g, mid_low, w_out, branch_pre, rec_pre, conv, rate, entry, state, edge, w_rate, w_entry, vecs, bw, middle,
        cot, live, hidden, w_down, mixed, 3
    )

    d_vecs = d_vecs.reshape(8, heads, N, rb).transpose(2, 0, 1, 3).reshape(N, -1)
    d_vecs = jnp.pad(d_vecs, ((0, 0), (0, up_to(d_vecs.shape[1], ch) - d_vecs.shape[1]))).reshape(N, -1, ch)
    flat = jnp.concatenate([d_rate.reshape(N, rb, ch), d_entry.reshape(N, rb, ch), d_vecs], axis=1)
    used = flat.shape[1]
    flat = jnp.pad(flat, ((0, 0), (0, up_to(used, 32) - used), (0, 0))).reshape(-1, ch)
    input_grad, gains, g_branch, g_rec, g_small = rec_back_call(
        g, branch_low, rec_low, w_branch, w_rec, x_low, grad_middle, gain_one, part_two, low_one, flat, 4
    )
    gains = lax.dynamic_slice(
        gains.reshape(2, N, -1), (0, lax.axis_index("shard") * g.Q + lax.axis_index("ctx"), 0), (2, 1, width // N)
    )[:, 0]
    g_small = g_small.reshape(-1)
    n = rb * ch
    g_rate = g_small[:n].reshape(rb, heads, bw).transpose(1, 0, 2)
    g_entry = g_small[n : 2 * n].reshape(rb, heads, bw).transpose(1, 0, 2)
    rest = g_small[2 * n : 2 * n + 8 * heads * rb].reshape(8, heads, rb)
    shape = (slots, block_len, width)
    output, input_grad, g_branch, g_rec, g_out, g_gate, g_up, g_down = settle(
        [output, input_grad, g_branch, g_rec, g_out, g_gate, g_up, g_down]
    )
    return (
        output.reshape(shape), input_grad.reshape(shape), gains[0], g_branch, g_rec, rest[:taps], rest[4],
        g_rate, rest[5], g_entry, rest[6], rest[7], g_out, gains[1], g_gate, g_up, g_down,
    )


def solution(mesh):
    plane = ("shard", "ctx")
    rows, cols = P(plane), P(plane, "tp")
    tok, gate, chan = P("shard", "ctx", None), P("tp", plane, None), P("tp", plane)
    taps = P(None, "tp", plane)
    params = (rows, cols, cols, taps, chan, gate, chan, gate, chan, chan, cols, rows, cols, cols, cols)
    return jax.shard_map(
        functools.partial(local, Grid(mesh)),
        mesh=mesh,
        in_specs=(tok, P("shard"), tok) + params,
        out_specs=(tok, tok) + params,
        check_vma=False,
    )
```

```python
import functools

import jax
import jax.numpy as jnp
from jax import lax
from jax.experimental import pallas as pl
from jax.experimental.pallas import tpu as pltpu
from jax.sharding import PartitionSpec as P

EPS = 1e-06
DECAY_SCALE = 8.0
F32 = jnp.float32
BF16 = jnp.bfloat16
MESH = pl.DeviceIdType.MESH
ANY = pl.BlockSpec(memory_space=pl.ANY)
VM = pl.BlockSpec(memory_space=pltpu.VMEM)
VMEM_LIMIT = 63 * 1024 * 1024


def dot(a, b):
    return jnp.dot(a, b, preferred_element_type=F32)


def dot_rows(a, b):
    return lax.dot_general(a, b, (((1,), (1,)), ((), ())), preferred_element_type=F32)


def dot_tokens(a, b):
    return lax.dot_general(a, b, (((0,), (0,)), ((), ())), preferred_element_type=F32)


def halves(v):
    hi = v.astype(BF16)
    return hi, (v - hi.astype(F32)).astype(BF16)


def gelu(v):
    return jax.nn.gelu(v)


def gelu_both(v):
    c = 0.7978845608028654
    th = jnp.tanh(c * (v + 0.044715 * v * v * v))
    half = 0.5 * (1.0 + th)
    return v * half, half + 0.5 * v * (1.0 - th * th) * c * (1.0 + 3 * 0.044715 * v * v)


def sigmoid(v):
    return 1.0 / (1.0 + jnp.exp(-v))


def minus_expm1(v):
    near = -v * (1.0 + v / 2 * (1.0 + v / 3 * (1.0 + v / 4 * (1.0 + v / 5 * (1.0 + v / 6)))))
    return jnp.where(v > -0.25, near, 1.0 - jnp.exp(v))


class Grid:
    def __init__(self, mesh):
        self.S, self.Q, self.T = (mesh.shape[n] for n in ("shard", "ctx", "tp"))
        dev = mesh.devices

        def chip(d):
            return tuple(getattr(d, "coords", None) or ())

        def paired(one, two):
            return bool(chip(one)) and chip(one) == chip(two)

        self.core_in = None
        if self.Q % 2 == 0 and paired(dev[0, 0, 0], dev[0, 1, 0]):
            self.core_in = "ctx"
        elif self.S % 2 == 0 and paired(dev[0, 0, 0], dev[1, 0, 0]):
            self.core_in = "shard"
        self.C = 1 if self.core_in is None else 2
        self.A = self.S // 2 if self.core_in == "shard" else self.S
        self.B = self.Q // 2 if self.core_in == "ctx" else self.Q
        self.N = self.S * self.Q

    def me(self):
        s, q = lax.axis_index("shard"), lax.axis_index("ctx")
        if self.core_in == "ctx":
            return s, q // 2, q % 2
        if self.core_in == "shard":
            return s // 2, q, s % 2
        return s, q, 0

    def shard_ctx(self, a, b, c):
        if self.core_in == "ctx":
            return a, b * 2 + c
        if self.core_in == "shard":
            return a * 2 + c, b
        return a, b

    def block(self, a, b, c):
        s, q = self.shard_ctx(a, b, c)
        return s * self.Q + q

    def dev(self, a, b, c):
        s, q = self.shard_ctx(a, b, c)
        return {"shard": s, "ctx": q}


class Wire:
    def __init__(self, send, recv, base=0):
        self.send, self.recv, self.used = send, recv, base

    def copy(self, src, dst, dev):
        self.used += 1
        return self.at(self.used - 1, src, dst, dev)

    def at(self, k, src, dst, dev):
        return pltpu.make_async_remote_copy(
            src_ref=src,
            dst_ref=dst,
            send_sem=self.send.at[k],
            recv_sem=self.recv.at[k],
            device_id=dev,
            device_id_type=MESH,
        )


def greet(devs):
    bar = pltpu.get_barrier_semaphore()
    for d in devs:
        pl.semaphore_signal(bar, inc=1, device_id=d, device_id_type=MESH)
    pl.semaphore_wait(bar, len(devs))


def ring_peers(size, at, place):
    if size == 1:
        return []
    if size == 2:
        return [place((at + 1) % 2)]
    return [place((at + 1) % size), place((at + size - 1) % size)]


def plane_peers(g):
    a, b, c = g.me()
    out = ring_peers(g.A, a, lambda k: g.dev(k, b, c))
    out += ring_peers(g.B, b, lambda k: g.dev(a, k, c))
    if g.C == 2:
        out.append(g.dev(a, b, 1 - c))
    return out


def braid(main, *sides):
    k = 0
    for _ in main:
        for steps, plan in sides:
            for _ in range(plan[k] if k < len(plan) else 0):
                next(steps, None)
        k += 1
    left = [s[0] for s in sides]
    while left:
        left = [s for s in left if next(s, left) is not left]


def at_steps(*pairs):
    plan = [0] * (1 + max(last for _, last, _ in pairs))
    for first, last, each in pairs:
        for k in range(first, last + 1):
            plan[k] += each
    return tuple(plan)


ALWAYS = (1,) * 64


def run(*steps):
    for s in steps:
        for _ in s:
            pass


class Later:
    def __init__(self, src, dst, sem):
        self.copy, self.dst, self.here = pltpu.make_async_copy(src, dst, sem), dst, False
        self.copy.start()

    def ref(self):
        if not self.here:
            self.copy.wait()
            self.here = True
        return self.dst


def call(kernel, operands, out_shape, scratch, cid, name, in_specs=None, out_specs=None, later=(), early=()):
    in_specs = list(in_specs or [VM] * len(operands))
    out_specs = list(out_specs or [VM] * len(out_shape))
    for k in later:
        in_specs[k] = ANY
    for k in early:
        out_specs[k] = ANY
    n, m = len(later), len(early)
    n_in = len(operands)

    def body(*refs):
        refs = list(refs)
        if m:
            kept, sem = refs[-m - 1 : -1], refs[-1]
            refs = refs[: -m - 1]
            copies = {}
            for j, k in enumerate(early):
                copies[id(kept[j])] = pltpu.make_async_copy(kept[j], refs[n_in + k], sem.at[j])
                refs[n_in + k] = kept[j]
        if n:
            held, sem_in = refs[-n - 1 : -1], refs[-1]
            refs = refs[: -n - 1]
            for j, k in enumerate(later):
                refs[k] = Later(refs[k], held[j], sem_in.at[j])
        if not m:
            kernel(*refs)
            return
        kernel(*refs, send_out=lambda *which: [copies[id(r)].start() for r in which])
        for cp in copies.values():
            cp.wait()

    extra = [pltpu.VMEM(operands[k].shape, operands[k].dtype) for k in later]
    if n:
        extra.append(pltpu.SemaphoreType.DMA((n,)))
    extra += [pltpu.VMEM(out_shape[k].shape, out_shape[k].dtype) for k in early]
    if m:
        extra.append(pltpu.SemaphoreType.DMA((m,)))
    return pl.pallas_call(
        body,
        out_shape=out_shape,
        in_specs=in_specs,
        out_specs=out_specs,
        scratch_shapes=list(scratch) + extra,
        compiler_params=pltpu.CompilerParams(
            collective_id=cid, has_side_effects=True, vmem_limit_bytes=VMEM_LIMIT
        ),
        name=name,
    )(*operands)


def sems(n):
    return [pltpu.SemaphoreType.DMA((max(1, n),)), pltpu.SemaphoreType.DMA((max(1, n),))]


def gather_count(g):
    ring = 0
    for nf, ng in ((g.A, g.B), (g.B, g.A)):
        ring += (nf - 1) + (ng - 1) * nf
    return ring + (g.C - 1) * (1 + ring)


def gather_steps(g, wire, here, srcs, dsts):
    a, b, c = g.me()
    sib = None if g.C == 1 else g.dev(a, b, 1 - c)
    sends, sib_copies = [], []

    def ring(h):
        if h == 0:
            return g.A, a, (lambda k: g.dev(k, b, c)), g.B, b, (lambda k: g.dev(a, k, c)), (lambda f, s: g.block(f, s, c))
        return g.B, b, (lambda k: g.dev(a, k, c)), g.A, a, (lambda k: g.dev(k, b, c)), (lambda f, s: g.block(s, f, c))

    def start(src, dst, dev):
        cp = wire.copy(src, dst, dev)
        cp.start()
        sends.append(cp)
        return cp

    def rows_of(dst, blk, h, rows):
        half = rows // 2
        return dst.at[pl.ds(pl.multiple_of(blk * rows + h * half, half), half)]

    state = []
    mine = g.block(a, b, c)
    local_copies = []
    for src, dst in zip(srcs, dsts):
        rows = src.shape[0]
        half = rows // 2
        cp = pltpu.make_async_copy(src, dst.at[pl.ds(pl.multiple_of(mine * rows, rows), rows)], here.at[len(local_copies)])
        cp.start()
        local_copies.append(cp)
        per = []
        for h in (0, 1):
            nf, f, fdev, ng, s, sdev, blk = ring(h)
            own = src.at[pl.ds(h * half, half)]
            land = rows_of(dst, mine, h, rows)
            first = start(own, land, fdev((f + 1) % nf)) if nf > 1 else None
            per.append([first, None, own, land])
        for h in (0, 1):
            nf, f, fdev, ng, s, sdev, blk = ring(h)
            _, _, own, land = per[h]
            second = {}
            if ng > 1:
                second[(0, 0)] = start(own, land, sdev((s + 1) % ng))
            per[h][1] = second
        if sib is not None:
            whole = dst.at[pl.ds(pl.multiple_of(mine * rows, rows), rows)]
            sib_copies.append(start(src, whole, sib))
        state.append(per)
        yield
    for (src, dst), per in zip(zip(srcs, dsts), state):
        rows = src.shape[0]
        for h in (0, 1):
            nf, f, fdev, ng, s, sdev, blk = ring(h)
            cp = per[h][0]
            for i in range(1, nf):
                cp.wait_recv()
                at = rows_of(dst, blk((f - i) % nf, s), h, rows)
                if i < nf - 1:
                    cp = start(at, at, fdev((f + 1) % nf))
                if ng > 1:
                    per[h][1][(0, i)] = start(at, at, sdev((s + 1) % ng))
                if sib is not None:
                    sib_copies.append(start(at, at, sib))
        yield
    for (src, dst), per in zip(zip(srcs, dsts), state):
        rows = src.shape[0]
        for h in (0, 1):
            nf, f, fdev, ng, s, sdev, blk = ring(h)
            second = per[h][1]
            for j in range(1, ng):
                for i in range(nf):
                    second[(j - 1, i)].wait_recv()
                    at = rows_of(dst, blk((f - i) % nf, (s - j) % ng), h, rows)
                    if j < ng - 1:
                        second[(j, i)] = start(at, at, sdev((s + 1) % ng))
                    if sib is not None:
                        sib_copies.append(start(at, at, sib))
        yield
    for cp in local_copies:
        cp.wait()
    for cp in sib_copies:
        cp.wait_recv()
    for cp in sends:
        cp.wait_send()


def tp_peers(g):
    t = lax.axis_index("tp")
    return ring_peers(g.T, t, lambda k: {"tp": k})


MIX_XY = at_steps((6, 6, 1), (12, 12, 1), (16, 16, 1), (19, 19, 1))
BACK_Z = ALWAYS
BACK_DOWN = at_steps((2, 2, 1), (4, 4, 1), (6, 6, 1), (8, 8, 1), (9, 10, 2), (17, 17, 1))
BACK_OUT = at_steps((11, 12, 2), (13, 16, 1), (21, 21, 1))
MLP_GATE = at_steps((0, 3, 2), (8, 8, 1), (14, 14, 1))
MLP_UP = at_steps((4, 7, 2), (14, 14, 1), (21, 21, 1))
REC_BRANCH = at_steps((0, 3, 2), (9, 9, 1), (17, 17, 1))
REC_REC = at_steps((4, 7, 2), (13, 13, 1), (19, 19, 1))
REC_SMALL = at_steps((8, 11, 2), (15, 15, 1), (20, 20, 1))
PIECE = 32
CHUNK = 256


def tp_count(g, rows):
    return 4 * (rows // 2 // PIECE)


def tp_place(g):
    t = lax.axis_index("tp")
    side = jnp.where(t >= (g.T + 1) // 2, 1, 0)
    return side, jnp.where(side == 1, g.T - 1 - t, t)


END = {"send_near": 0, "take_far": 8, "take_near": 14}
INNER = {"send_near": 0, "take_far": 2, "pass_far": 6, "take_near": 8}


def tp_steps(g, wire, rows, out, partial=None, finish=None, bufs=None, gather=True):
    T = g.T
    t = lax.axis_index("tp")
    half = rows // 2
    pieces = half // PIECE
    side, pos = tp_place(g)
    end, inner = pos == 0, pos > 0
    near, far = side, 1 - side
    away = {"tp": jnp.where(side == 1, t - 1, t + 1)}
    home = {"tp": jnp.where(side == 1, (t + 1) % T, (t + T - 1) % T)}
    k_rs = wire.used
    if partial is not None:
        wire.used += 2 * pieces
    k_ag = wire.used
    if gather:
        wire.used += 2 * pieces

    def row(d, p):
        return pl.multiple_of(half * (1 - d) + p * PIECE, PIECE)

    def rs(d, p, dev):
        return wire.at(k_rs + d * pieces + p, bufs[1].at[d, p], bufs[2].at[d, p], dev)

    def ag(d, p, dev):
        at = out.at[pl.ds(row(d, p), PIECE)]
        return wire.at(k_ag + d * pieces + p, at, at, dev)

    step = chunk_rows(g, rows, out.shape[1])
    per = step // PIECE

    def ready(d, p, which):
        term = bufs[0].at[which]
        if p % per == 0:
            partial(pl.multiple_of(half * (1 - d) + p * PIECE, step), step, term)
        return term.at[pl.ds(p % per * PIECE, PIECE)]

    def send_near(p, at_end):
        part = ready(near, p, 0)[...]
        if not at_end:
            rs(near, p, away).wait_recv()
            part = part + bufs[2][near, p].astype(F32)
        bufs[1][near, p] = part.astype(BF16)
        rs(near, p, away).start()

    def take_far(p, at_end):
        part = ready(far, p, 1)
        rs(far, p, home).wait_recv()
        total = part[...] + bufs[2][far, p].astype(F32)
        if not at_end:
            bufs[1][far, p] = total.astype(BF16)
            rs(far, p, home).start()
            return
        done = finish(total, p * PIECE, row(far, p), PIECE)
        if gather:
            out[pl.ds(row(far, p), PIECE)] = done
            ag(far, p, away).start()
        else:
            out[p * PIECE : (p + 1) * PIECE] = done

    def pass_far(p, at_end):
        ag(far, p, away).wait_recv()
        ag(far, p, away).start()

    def take_near(p, at_end):
        ag(near, p, home).wait_recv()
        if not at_end:
            ag(near, p, home).start()

    acts = {"send_near": send_near, "take_far": take_far, "pass_far": pass_far, "take_near": take_near}
    if partial is None:

        @pl.when(end)
        def _():
            for p in range(pieces):
                ag(far, p, away).start()

        acts = {"pass_far": pass_far, "take_near": take_near}
        yield
    elif not gather:
        acts = {"send_near": send_near, "take_far": take_far}

    def schedule(lates):
        lates = {k: v for k, v in lates.items() if k in acts}
        least = min(lates.values())
        return [(acts[k], v - least) for k, v in lates.items()]

    plans = [(end, True, schedule(END)), (inner, False, schedule(INNER))]
    for i in range(pieces + max(late for _, _, plan in plans for _, late in plan)):
        for where, at_end, plan in plans:

            @pl.when(where)
            def _():
                for act, late in plan:
                    if 0 <= i - late < pieces:
                        act(i - late, at_end)

        yield
    if partial is not None:
        for p in range(pieces):
            rs(near, p, away).wait_send()
    if gather:
        for p in range(pieces):
            ag(far, p, away).wait_send()

    @pl.when(inner)
    def _():
        for p in range(pieces):
            if partial is not None:
                rs(far, p, home).wait_send()
            if gather:
                ag(near, p, home).wait_send()


def chunk_rows(g, rows, width):
    return min(CHUNK // 2 if needs_turn(width // g.N) else CHUNK, rows // 2)


def tp_bufs(g, rows, width):
    pieces = rows // 2 // PIECE
    return [
        pltpu.VMEM((2, chunk_rows(g, rows, width), width), F32),
        pltpu.VMEM((2, pieces, PIECE, width), BF16),
        pltpu.VMEM((2, pieces, PIECE, width), BF16),
    ]


def transpose_steps(dst, src, scale=None):
    if isinstance(src, Later):
        src = src.ref()
    width = src.shape[1]
    part = 512
    assert width % part == 0

    for at in range(0, width, part):

        def body(j, _):
            c0 = pl.multiple_of(at + j * 128, 128)
            v = src[:, pl.ds(c0, 128)]
            if scale is not None:
                v = (v.astype(F32) * scale[...]).astype(BF16)
            dst[pl.ds(c0, 128), :] = v.T
            return 0

        lax.fori_loop(0, part // 128, body, 0)
        yield


def chain(*steps):
    for s in steps:
        yield from s


def tile_of(width):
    return 512 if width % 512 == 0 else width


def rows_product(term, at, n, pairs):
    width = term.shape[1]
    tile = tile_of(width)

    def body(j, _):
        c0 = pl.multiple_of(j * tile, tile)
        total = None
        for l, r in pairs:
            p = dot_rows(l[pl.ds(at, n)], r[pl.ds(c0, tile)])
            total = p if total is None else total + p
        term[:, pl.ds(c0, tile)] = total
        return 0

    lax.fori_loop(0, width // tile, body, 0)


def rows_dot(dst, left, right):
    step = 256 if left.shape[0] % 256 == 0 else left.shape[0]

    def body(i, _):
        r0 = pl.ds(pl.multiple_of(i * step, step), step)
        dst[r0] = dot(left[r0], right[...])
        return 0

    lax.fori_loop(0, left.shape[0] // step, body, 0)


def mean_square(v):
    return jnp.mean(v * v, axis=-1, keepdims=True)


def mix_out_body(ins, outs):
    mixed, w_out, x, gain = ins
    _, middle = outs

    def partial(at, n, term):
        rows_product(term, at, n, [(mixed, w_out)])

    def finish(total, near, at, n):
        m = x[pl.ds(at, n)].astype(F32) + total
        middle[near : near + n] = m
        return (m * lax.rsqrt(mean_square(m) + EPS) * gain[...]).astype(BF16)

    return partial, finish


def mlp_out_body(ins, outs):
    hidden, w_down, middle, live = ins

    def partial(at, n, term):
        rows_product(term, at, n, [(hidden, w_down)])

    def finish(total, near, at, n):
        return ((middle[near : near + n] + total) * live[pl.ds(at, n)]).astype(BF16)

    return partial, finish


def norm_back(grad_normed, rows, gain):
    inv = lax.rsqrt(mean_square(rows) + EPS)
    gg = grad_normed * gain
    back = inv * gg - rows * (inv * inv * inv) * jnp.mean(gg * rows, axis=-1, keepdims=True)
    return back, jnp.sum(grad_normed * rows * inv, axis=0, keepdims=True)


def mlp_back_body(ins, outs):
    gate_low, up_low, w_gate, w_up, middle, cot, live, gain = ins
    _, grad_middle, grad_gain = outs
    grad_gain[...] = jnp.zeros_like(grad_gain)

    def partial(at, n, term):
        rows_product(term, at, n, [(gate_low, w_gate), (up_low, w_up)])

    def finish(total, near, at, n):
        back, gain_sum = norm_back(total, middle[near : near + n], gain[...])
        gm = cot[pl.ds(at, n)].astype(F32) * live[pl.ds(at, n)] + back
        grad_middle[near : near + n] = gm
        grad_gain[...] = grad_gain[...] + gain_sum
        return gm.astype(BF16)

    return partial, finish


def rec_back_body(ins, outs):
    branch_low, rec_low, w_branch, w_rec, x, grad_middle, gain = ins
    _, grad_gain = outs
    grad_gain[...] = jnp.zeros_like(grad_gain)

    def partial(at, n, term):
        rows_product(term, at, n, [(branch_low, w_branch), (rec_low, w_rec)])

    def finish(total, near, at, n):
        back, gain_sum = norm_back(total, x[pl.ds(at, n)].astype(F32), gain[...])
        grad_gain[...] = grad_gain[...] + gain_sum
        return (grad_middle[near : near + n] + back).astype(BF16)

    return partial, finish


TAPS, SHIFT, RBIAS, EBIAS, SOFT, SLOPE = 0, 4, 5, 6, 7, 8
ROWS = 64
GROUP = 8


def ctx_peers(g):
    q = lax.axis_index("ctx")
    return [{"ctx": (q + k) % g.Q} for k in range(1, g.Q)]


def swap_edges(g, wire, src, land):
    q = lax.axis_index("ctx")
    cps = []
    for k in range(1, g.Q):
        cp = wire.copy(src, land.at[q], {"ctx": (q + k) % g.Q})
        cp.start()
        cps.append(cp)
    yield
    for cp in cps:
        cp.wait_recv()
    for cp in cps:
        cp.wait_send()


def row_shift(v, n):
    return pltpu.roll(v, n % v.shape[0], 0)


def forward_steps(g, wire, branch, w_rate, w_entry, vecs, mixed, conv, rate, entry, state, edge,
                  ext, acum, bcum, tot, gath):
    L, CH = branch.shape
    q = lax.axis_index("ctx")
    sub = lax.broadcasted_iota(jnp.int32, (GROUP, 1), 0)

    def chunk(i, carry):
        ca, cb = carry
        r0 = i * ROWS
        wide = ext[pl.ds(r0, ROWS + 8)]
        c = vecs[SHIFT : SHIFT + 1] + vecs[TAPS : TAPS + 1] * wide[8:]
        for k in range(1, 4):
            c = c + vecs[TAPS + k : TAPS + k + 1] * row_shift(wide, k)[8:]
        conv[pl.ds(r0, ROWS)] = c
        hi, lo = halves(c)
        gr = sigmoid(dot(hi, w_rate[...]) + dot(lo, w_rate[...]) + vecs[RBIAS : RBIAS + 1])
        ge = sigmoid(dot(hi, w_entry[...]) + dot(lo, w_entry[...]) + vecs[EBIAS : EBIAS + 1])
        rate[pl.ds(r0, ROWS)] = gr
        entry[pl.ds(r0, ROWS)] = ge
        log = -DECAY_SCALE * gr * vecs[SOFT : SOFT + 1]
        dec = jnp.exp(log)
        drive = jnp.sqrt(minus_expm1(2.0 * log)) * ge * c
        for n in range(ROWS // GROUP):
            A = dec[n * GROUP : (n + 1) * GROUP]
            B = drive[n * GROUP : (n + 1) * GROUP]
            for step in (1, 2, 4):
                keep = sub >= step
                As = jnp.where(keep, row_shift(A, step), 1.0)
                Bs = jnp.where(keep, row_shift(B, step), 0.0)
                B = B + A * Bs
                A = A * As
            B = B + A * cb
            A = A * ca
            acum[pl.ds(r0 + n * GROUP, GROUP)] = A
            bcum[pl.ds(r0 + n * GROUP, GROUP)] = B
            ca = A[GROUP - 1 : GROUP]
            cb = B[GROUP - 1 : GROUP]
        return ca, cb

    ca, cb = jnp.ones((1, CH), F32), jnp.zeros((1, CH), F32)
    for i in range(L // ROWS):
        ca, cb = chunk(i, (ca, cb))
        yield
    tot[0:1] = ca
    tot[1:2] = cb
    start = jnp.zeros((1, CH), F32)
    if g.Q > 1:
        yield from swap_edges(g, wire, tot, gath)
        for d in range(g.Q - 1):
            new = gath[d, 0:1] * start + gath[d, 1:2]
            start = jnp.where(d < q, new, start)
    edge[...] = jnp.broadcast_to(start, (8, CH))
    yield

    def fix(i, _):
        r0 = pl.multiple_of(i * ROWS, ROWS)
        s = bcum[pl.ds(r0, ROWS)] + acum[pl.ds(r0, ROWS)] * start
        state[pl.ds(r0, ROWS)] = s
        mixed[pl.ds(r0, ROWS)] = (gelu_both(branch[pl.ds(r0, ROWS)])[0] * s).astype(BF16)
        return 0

    lax.fori_loop(0, L // ROWS, fix, 0)
    yield


def pack_rows(rb):
    return up_to(2 * rb + 10, 32), 2 * rb, 2 * rb + 8


def iota2(shape):
    return lax.broadcasted_iota(jnp.int32, shape, 0), lax.broadcasted_iota(jnp.int32, shape, 1)


def log1p_small(e):
    return jnp.where(e < 0.02, e * (1.0 - e * (0.5 - e * (1.0 / 3 - e * 0.25))), jnp.log(1.0 + e))


def unpack(packs, bw, rb, rows, w_rate, w_entry, vecs, gains):
    total, CH = packs.shape
    n = bw // rb
    prow, o_vec, o_gain = pack_rows(rb)
    m, l = iota2((bw, total))
    _, lane = iota2((bw, CH))
    for dst, off in ((w_rate, 0), (w_entry, rb)):
        pick = jnp.logical_and(l // prow == m // rb, l % prow == m % rb + off)
        block = dot(jnp.where(pick, 1.0, 0.0).astype(BF16), packs[...])
        for h in range(CH // bw):
            dst[h * bw : (h + 1) * bw] = jnp.where(lane // bw == h, block, 0.0).astype(BF16)

    def rows_at(off):
        m, l = iota2((n * 8, total))
        pick = l == (m // 8) * prow + off + m % 8
        return dot(jnp.where(pick, 1.0, 0.0).astype(BF16), packs[...])

    short = rows_at(o_vec)[:, :128].astype(BF16)
    l, m = iota2((128, CH))
    spread = jnp.logical_and(l // rb == m // bw, l % rb == m % rb)
    wide = dot(short, jnp.where(spread, 1.0, 0.0).astype(BF16))
    _, lane = iota2((8, CH))
    vec = jnp.zeros((8, CH), F32)
    for j in range(n):
        vec = vec + jnp.where(lane % bw // rb == j, wide[j * 8 : (j + 1) * 8], 0.0)
    decay = vec[7:8]
    e = jnp.exp(-jnp.abs(decay))
    vecs[0:7] = vec[0:7]
    vecs[SOFT : SOFT + 1] = jnp.maximum(-decay, 0.0) + log1p_small(e)
    vecs[SLOPE : SLOPE + 1] = sigmoid(-decay)
    vecs[SLOPE + 1 :] = jnp.zeros((16 - SLOPE - 1, CH), F32)
    both = rows_at(o_gain)
    if rows % 128 == 0:
        for j in range(n):
            for u in range(2):
                gains[u : u + 1, j * rows : (j + 1) * rows] = both[j * 8 + u : j * 8 + u + 1, :rows]
    else:
        l, m = iota2((128, gains.shape[1]))
        row = jnp.zeros((8, gains.shape[1]), F32)
        for j in range(n):
            place = jnp.logical_and(l < rows, m == l + j * rows)
            row = row + dot(both[j * 8 : (j + 1) * 8, :128].astype(BF16), jnp.where(place, 1.0, 0.0).astype(BF16))
        gains[...] = row[:2]


def front_call(g, pack, rec_shard, branch_shard, out_shard, mlp_shards, x, bw, rb, cid):
    L, width = x.shape
    CH = pack.shape[1]
    half = L // 2
    n = len(mlp_shards)
    rows = out_shard.shape[0]
    wide = jax.ShapeDtypeStruct((L, CH), F32)
    dense = jax.ShapeDtypeStruct((CH, CH), BF16)

    def whole(s):
        return jax.ShapeDtypeStruct((g.N * s.shape[0], s.shape[1]), s.dtype)

    low = jax.ShapeDtypeStruct((L, width), BF16)
    outs = [low, wide, wide, jax.ShapeDtypeStruct((L, CH), BF16), wide, wide, wide, wide, jax.ShapeDtypeStruct((8, CH), F32),
            low, jax.ShapeDtypeStruct((half, width), F32), dense, dense, jax.ShapeDtypeStruct((16, CH), F32),
            jax.ShapeDtypeStruct((2, width), F32), whole(rec_shard), whole(branch_shard), whole(out_shard)]
    outs += [whole(s) for s in mlp_shards]
    count = 2 * g.Q + tp_count(g, L) + (n + 4) * gather_count(g)

    def kernel(pack, rec_shard, branch_shard, out_shard, *refs, send_out):
        shards, x = refs[:n], refs[n]
        (low_one, branch, rec, mixed, conv, rate, entry, state, edge, low_two, middle, w_rate, w_entry, vecs, gains,
         w_rec, w_branch, w_out) = refs[n + 1 : n + 19]
        full = refs[n + 19 : 2 * n + 19]
        (packs, x_edge, a_edge, ext, acum, bcum, tot, gath, term, sendbuf, recvbuf, send, recv, here) = refs[2 * n + 19 :]
        q = lax.axis_index("ctx")
        greet(ctx_peers(g) + plane_peers(g) + tp_peers(g))
        wire = Wire(send, recv)
        slots = iter(range(n + 4))

        def gather(srcs, dsts):
            at = [next(slots) for _ in srcs]
            return gather_steps(g, wire, here.at[pl.ds(at[0], len(at))], srcs, dsts)

        small = gather([pack], [packs])
        next(small)
        edge_copy = None
        if g.Q > 1:
            edge_copy = wire.copy(x.at[pl.ds(L - 16, 16)], x_edge, {"ctx": (q + 1) % g.Q})
            edge_copy.start()
        of_rec = gather([rec_shard], [w_rec])
        of_branch = gather([branch_shard], [w_branch])
        of_out = gather([out_shard], [w_out])
        rest = gather(shards, full)
        next(of_rec)
        next(of_branch)
        run(small)
        unpack(packs, bw, rb, rows, w_rate, w_entry, vecs, gains)

        def norm_rows(i, _):
            r0 = pl.ds(pl.multiple_of(i * ROWS, ROWS), ROWS)
            v = x[r0].astype(F32)
            low_one[r0] = (v * lax.rsqrt(mean_square(v) + EPS) * gains[0:1]).astype(BF16)
            return 0

        lax.fori_loop(0, L // ROWS, norm_rows, 0)
        next(of_rec)
        next(of_branch)
        next(of_out)
        next(of_rec)
        next(of_branch)
        if g.Q > 1:
            edge_copy.wait()
            v = x_edge[...].astype(F32)
            a_edge[...] = (v * lax.rsqrt(mean_square(v) + EPS) * gains[0:1]).astype(BF16)
        run(of_rec)
        rows_dot(rec, low_one, w_rec)
        ext[8:] = rec[...]
        if g.Q > 1:
            ext[0:8] = jnp.where(q > 0, dot(a_edge[...], w_rec[...])[8:], 0.0)
        else:
            ext[0:8] = jnp.zeros((8, CH), F32)
        fwd = forward_steps(g, wire, branch, w_rate, w_entry, vecs, mixed, conv, rate, entry, state, edge,
                            ext, acum, bcum, tot, gath)
        for k in range(L // ROWS):
            next(fwd)
            if k == 2:
                next(of_out)
            if k == 6:
                next(of_out)
        if g.Q > 1:
            next(fwd)
        for _ in range(n):
            next(rest)
        run(of_branch)
        rows_dot(branch, low_one, w_branch)
        send_out(low_one, rec, conv, rate, entry, w_rate, w_entry, w_rec, w_branch, branch)
        run(fwd, of_out)
        send_out(mixed, state, w_out)
        partial, finish = mix_out_body((mixed, w_out, x, gains.at[pl.ds(1, 1)]), (low_two, middle))
        braid(
            tp_steps(g, wire, L, low_two, partial, finish, (term, sendbuf, recvbuf)),
            (rest, MIX_XY),
        )

    return call(
        kernel,
        [pack, rec_shard, branch_shard, out_shard, *mlp_shards, x],
        outs,
        [
            pltpu.VMEM((g.N * pack.shape[0], CH), BF16),
            pltpu.VMEM((16, width), BF16),
            pltpu.VMEM((16, width), BF16),
            pltpu.VMEM((L + 8, CH), F32),
            pltpu.VMEM((L, CH), F32),
            pltpu.VMEM((L, CH), F32),
            pltpu.VMEM((8, CH), F32),
            pltpu.VMEM((g.Q, 8, CH), F32),
        ]
        + tp_bufs(g, L, width)
        + sems(count)
        + [pltpu.SemaphoreType.DMA((n + 4,))],
        cid,
        "front",
        [VM] * (n + 5),
        [VM] * 18 + [ANY] * n,
        early=(0, 1, 2, 3, 4, 5, 6, 7, 11, 12, 15, 16, 17),
    )


def backward_steps(g, wire, mid_low, w_out, branch, rec, conv, rate, entry, state, edge, w_rate, w_entry, vecs,
                    branch_low, rec_low, g_rate, g_entry, g_vecs,
                    sgrad, acum, bcum, conv_h, conv_l, rb_h, rb_l, eb_h, eb_l, tot, gath, halo, prevx, slow=()):
    L, CH = rec.shape
    gconv = sgrad
    q = lax.axis_index("ctx")
    tail = None
    rows_dot(sgrad.at[pl.ds(0, L)], mid_low, w_out)
    for v in slow:
        v.ref()
    if g.Q > 1:
        tail = wire.copy(rec.at[pl.ds(L - 8, 8)], prevx, {"ctx": (q + 1) % g.Q})
        tail.start()
    sub = lax.broadcasted_iota(jnp.int32, (GROUP, 1), 0)
    chunks = L // ROWS

    def chunk(j, carry):
        ua, ub = carry
        r0 = (chunks - 1 - j) * ROWS
        gm = sgrad[pl.ds(r0, ROWS)]
        act, slope = gelu_both(branch[pl.ds(r0, ROWS)])
        branch_low[pl.ds(r0, ROWS)] = (gm * state[pl.ds(r0, ROWS)] * slope).astype(BF16)
        sg = gm * act
        sgrad[pl.ds(r0, ROWS)] = sg
        dec = jnp.exp(-DECAY_SCALE * rate[pl.ds(r0, ROWS)] * vecs[SOFT : SOFT + 1])
        sg = dec * sg
        for n in reversed(range(ROWS // GROUP)):
            A = dec[n * GROUP : (n + 1) * GROUP]
            B = sg[n * GROUP : (n + 1) * GROUP]
            for step in (1, 2, 4):
                keep = sub < GROUP - step
                As = jnp.where(keep, row_shift(A, -step), 1.0)
                Bs = jnp.where(keep, row_shift(B, -step), 0.0)
                B = B + A * Bs
                A = A * As
            B = B + A * ub
            A = A * ua
            acum[pl.ds(r0 + n * GROUP, GROUP)] = A
            bcum[pl.ds(r0 + n * GROUP, GROUP)] = B
            ua = A[0:1]
            ub = B[0:1]
        return ua, ub

    yield
    ua, ub = jnp.ones((1, CH), F32), jnp.zeros((1, CH), F32)
    for i in range(chunks):
        ua, ub = chunk(i, (ua, ub))
        yield
    tot[0:1] = ua
    tot[1:2] = ub
    arriving = jnp.zeros((1, CH), F32)
    if g.Q > 1:
        swap = swap_edges(g, wire, tot, gath)
        next(swap)
        for _ in range(3):
            yield
        run(swap)
        for d in reversed(range(1, g.Q)):
            new = gath[d, 0:1] * arriving + gath[d, 1:2]
            arriving = jnp.where(d > q, new, arriving)
        tail.wait()
    acum[L:] = jnp.ones((8, CH), F32)
    bcum[L:] = jnp.zeros((8, CH), F32)
    zero = jnp.zeros((1, CH), F32)
    if g.Q > 1:
        prev_rows = jnp.where(q > 0, prevx[...], 0.0)
    else:
        prev_rows = jnp.zeros((8, CH), F32)

    def back(i, carry):
        gdec, gbr, gbe, gshift, gt0, gt1, gt2, gt3, last_state, last_rec = carry
        r0 = i * ROWS
        aw = row_shift(acum[pl.ds(r0, ROWS + 8)], -1)[:ROWS]
        bw = row_shift(bcum[pl.ds(r0, ROWS + 8)], -1)[:ROWS]
        car = sgrad[pl.ds(r0, ROWS)] + bw + aw * arriving
        st = state[pl.ds(r0, ROWS)]
        prev = row_shift(jnp.concatenate([last_state, st], axis=0), 1)[8:]
        gr = rate[pl.ds(r0, ROWS)]
        ge = entry[pl.ds(r0, ROWS)]
        c = conv[pl.ds(r0, ROWS)]
        soft = vecs[SOFT : SOFT + 1]
        log = -DECAY_SCALE * gr * soft
        dec = jnp.exp(log)
        scale = jnp.sqrt(minus_expm1(2.0 * log))
        ec = ge * c
        glog = car * prev * dec - car * ec * dec * dec / scale
        glr = 8.0 * glog * gr
        gdec = gdec + jnp.sum(glr, axis=0, keepdims=True)
        rb = -glr * soft * (1.0 - gr)
        cs = car * scale
        eb = cs * ec * (1.0 - ge)
        gbr = gbr + jnp.sum(rb, axis=0, keepdims=True)
        gbe = gbe + jnp.sum(eb, axis=0, keepdims=True)
        rh, rl = halves(rb)
        eh, el = halves(eb)
        ch, cl = halves(c)
        rb_h[pl.ds(r0, ROWS)] = rh
        rb_l[pl.ds(r0, ROWS)] = rl
        eb_h[pl.ds(r0, ROWS)] = eh
        eb_l[pl.ds(r0, ROWS)] = el
        conv_h[pl.ds(r0, ROWS)] = ch
        conv_l[pl.ds(r0, ROWS)] = cl
        wr, we = w_rate[...], w_entry[...]
        gc = cs * ge + dot_rows(rh, wr) + dot_rows(rl, wr) + dot_rows(eh, we) + dot_rows(el, we)
        gconv[pl.ds(r0, ROWS)] = gc
        gshift = gshift + jnp.sum(gc, axis=0, keepdims=True)
        x = rec[pl.ds(r0, ROWS)]
        wide = jnp.concatenate([last_rec, x], axis=0)
        gts = [gt0, gt1, gt2, gt3]
        for k in range(4):
            xk = x if k == 0 else row_shift(wide, k)[8:]
            gts[k] = gts[k] + jnp.sum(gc * xk, axis=0, keepdims=True)
        return (gdec, gbr, gbe, gshift, *gts, st[ROWS - 8 :], x[ROWS - 8 :])

    yield
    carry = (zero,) * 8 + (edge[...], prev_rows)
    for i in range(chunks):
        carry = back(i, carry)
        yield
    gdec, gbr, gbe, gshift, gt0, gt1, gt2, gt3 = carry[:8]
    if g.Q > 1:
        cp = wire.copy(gconv.at[pl.ds(0, 8)], halo, {"ctx": (q + g.Q - 1) % g.Q})
        cp.start()
    gdec = gdec * vecs[SLOPE : SLOPE + 1]
    for k, v in enumerate((gt0, gt1, gt2, gt3, gshift, gbr, gbe, gdec)):
        g_vecs[k : k + 1] = v
    yield

    def product(h, l):
        return dot_tokens(conv_h[...], h[...]) + dot_tokens(conv_l[...], h[...]) + dot_tokens(conv_h[...], l[...])

    bw = g_rate.shape[0]
    head = lax.broadcasted_iota(jnp.int32, (bw, CH), 1) // bw

    def diagonal(dense):
        total = jnp.zeros((bw, CH), F32)
        for h in range(CH // bw):
            total = total + jnp.where(head == h, dense[h * bw : (h + 1) * bw], 0.0)
        return total

    g_rate[...] = diagonal(product(rb_h, rb_l))
    yield
    g_entry[...] = diagonal(product(eb_h, eb_l))
    yield
    if g.Q > 1:
        cp.wait()
        gconv[L:] = jnp.where(q < g.Q - 1, halo[...], 0.0)
    else:
        gconv[L:] = jnp.zeros((8, CH), F32)

    def last(i, _):
        r0 = pl.multiple_of(i * ROWS, ROWS)
        wide = gconv[pl.ds(r0, ROWS + 8)]
        total = vecs[TAPS : TAPS + 1] * wide[:ROWS]
        for k in range(1, 4):
            total = total + vecs[TAPS + k : TAPS + k + 1] * row_shift(wide, -k)[:ROWS]
        rec_low[pl.ds(r0, ROWS)] = total.astype(BF16)
        return 0

    lax.fori_loop(0, chunks, last, 0)
    yield


def back_call(g, mid_low, w_out, branch, rec, conv, rate, entry, state, edge, w_rate, w_entry, vecs, bw, middle,
              cot, live, hidden, w_down, mixed, cid):
    L, CH = rec.shape
    half, width = middle.shape
    low = jax.ShapeDtypeStruct((L, CH), BF16)
    diag = jax.ShapeDtypeStruct((bw, CH), F32)
    F = hidden.shape[1]
    rows = width // g.N
    count = g.Q + 2 + tp_count(g, L) + 2 * reduce_count(g)
    operands = [mid_low, w_out, branch, rec, conv, rate, entry, state, edge, w_rate, w_entry, vecs,
                middle, cot, live, hidden, w_down, mixed]

    def kernel(*refs):
        ins, (middle, cot, live, hidden, w_down, mixed) = refs[:12], refs[12:18]
        slow = [v for v in ins if isinstance(v, Later)]
        outs, (output, g_down, g_out) = refs[18:23], refs[23:26]
        bufs = refs[26:39]
        cot_t, term, sendbuf, recvbuf, *more = refs[39:]
        mid_t = cot_t
        send, recv = more[-2:]
        greet(ctx_peers(g) + tp_peers(g) + plane_peers(g))
        wire = Wire(send, recv)
        ins = [v.dst if isinstance(v, Later) else v for v in ins]

        def z():
            yield
            body = mlp_out_body((hidden.ref(), w_down.ref(), middle, live), (output,))
            yield from tp_steps(g, wire, L, output, *body, (term, sendbuf, recvbuf))

        def down():
            yield from turn_steps(rows, cot_t, cot, live)
            hidden.ref()
            yield from reduce_steps(g, wire, [(product_term(cot.dst, cot_t, hidden.dst, rows, live), g_down, more[0:3])])

        down_steps = down()
        if needs_turn(rows):
            for _ in range(len(range(0, width, 512)) + g.C * g.A * g.B):
                next(down_steps)

        def out():
            yield from turn_steps(rows, mid_t, ins[0])
            mixed.ref()
            yield from reduce_steps(g, wire, [(product_term(ins[0], mid_t, mixed.dst, rows), g_out, more[3:6])])

        braid(
            chain(backward_steps(g, wire, *ins, *outs, *bufs, slow), iter(range(4))),
            (z(), BACK_Z),
            (down_steps, BACK_DOWN),
            (out(), BACK_OUT),
        )

    return call(
        kernel,
        operands,
        [low, low, diag, diag, jax.ShapeDtypeStruct((8, CH), F32), jax.ShapeDtypeStruct((L, width), BF16),
         jax.ShapeDtypeStruct((rows, F), F32), jax.ShapeDtypeStruct((rows, CH), F32)],
        [
            pltpu.VMEM((L + 8, CH), F32),
            pltpu.VMEM((L + 8, CH), F32),
            pltpu.VMEM((L + 8, CH), F32),
        ]
        + [pltpu.VMEM((L, CH), BF16)] * 6
        + [
            pltpu.VMEM((8, CH), F32),
            pltpu.VMEM((g.Q, 8, CH), F32),
            pltpu.VMEM((8, CH), F32),
            pltpu.VMEM((8, CH), F32),
        ]
        + turn_scratch(rows, width, L)
        + tp_bufs(g, L, width)
        + reduce_bufs(g, rows, F)
        + reduce_bufs(g, rows, CH)
        + sems(count),
        cid,
        "rec_backward",
        later=(15, 16, 13, 17, 3, 4, 6),
    )


def reduce_count(g):
    ring = 0
    for nf, ng in ((g.A, g.B), (g.B, g.A)):
        ring += (nf - 1) * ng + (ng - 1)
    return ring + (g.C - 1) * g.A * g.B


def reduce_bufs(g, rows, width):
    nb = g.A * g.B
    arrivals = reduce_count(g) - (g.C - 1) * nb
    return [
        pltpu.VMEM((nb, rows, width), BF16),
        pltpu.VMEM((nb, rows, width), BF16),
        pltpu.VMEM((max(1, arrivals), rows // 2, width), BF16),
    ]


def reduce_steps(g, wire, items):
    a, b, c = g.me()
    sends = []

    def start(src, dst, dev):
        cp = wire.copy(src, dst, dev)
        cp.start()
        sends.append(cp)
        return cp

    nb = g.A * g.B

    def owner(k, core):
        return g.block((a + g.A - k // g.B) % g.A, (b + g.B - k % g.B) % g.B, core)

    def each_tile(width, fn):
        fn(slice(None))

    rings = [(g.A, g.B), (g.B, g.A)]
    devs = [
        (g.dev((a + 1) % g.A, b, c), g.dev(a, (b + 1) % g.B, c)),
        (g.dev(a, (b + 1) % g.B, c), g.dev((a + 1) % g.A, b, c)),
    ]

    def slot(h, df, dg):
        return df * g.B + dg if h == 0 else dg * g.B + df

    bases = []
    state = []
    for term, out, (to_sib, sums, land) in items:
        half = out.shape[0] // 2
        base = wire.used
        bases.append(base)
        if g.C == 2:
            wire.used += nb
            for k in [(i + 1) % nb for i in range(nb)]:

                def tile(cols):
                    to_sib[k, :, cols] = term(owner(k, 1 - c), cols).astype(BF16)

                each_tile(out.shape[1], tile)
                wire.at(base + k, to_sib.at[k], sums.at[k], g.dev(a, b, 1 - c)).start()
                yield
        used = 0
        first = ({}, {})
        for k in [(i + 1) % nb for i in range(nb)]:
            if g.C == 2:
                wire.at(base + k, to_sib.at[k], sums.at[k], g.dev(a, b, 1 - c)).wait_recv()

            def tile(cols):
                s = term(owner(k, c), cols)
                if g.C == 2:
                    s = s + sums[k, :, cols].astype(F32)
                if k == 0:
                    out[:, cols] = s
                else:
                    sums[k, :, cols] = s.astype(BF16)

            each_tile(out.shape[1], tile)
            for h in (0, 1):
                nf, ng = rings[h]
                df, dg = (k // g.B, k % g.B) if h == 0 else (k % g.B, k // g.B)
                if nf > 1 and df == 1:
                    first[h][dg] = (start(sums.at[k, pl.ds(h * half, half)], land.at[used], devs[h][0]), used)
                    used += 1
            yield
        state.append([first, used])

    def add(out, sums, k, h, half, arrived):
        at = slice(h * half, (h + 1) * half)
        if k == 0:
            out[at] = out[at] + arrived.astype(F32)
        else:
            sums[k, at] = (sums[k, at].astype(F32) + arrived.astype(F32)).astype(BF16)

    seconds = []
    for (term, out, (to_sib, sums, land)), st in zip(items, state):
        half = out.shape[0] // 2
        first, used = st
        second = [None, None]
        for h in (0, 1):
            nf, ng = rings[h]
            for i in range(1, nf):
                df = (i + 1) % nf
                for dg in [d % ng for d in range(1, ng + 1)]:
                    cp, at = first[h][dg]
                    cp.wait_recv()
                    k = slot(h, df, dg)
                    add(out, sums, k, h, half, land[at])
                    if i < nf - 1:
                        first[h][dg] = (start(sums.at[k, pl.ds(h * half, half)], land.at[used], devs[h][0]), used)
                        used += 1
                    elif dg == 1 and ng > 1:
                        second[h] = (start(sums.at[k, pl.ds(h * half, half)], land.at[used], devs[h][1]), used)
                        used += 1
            if nf == 1 and ng > 1:
                k = slot(h, 0, 1)
                second[h] = (start(sums.at[k, pl.ds(h * half, half)], land.at[used], devs[h][1]), used)
                used += 1
        seconds.append([second, used])
        yield
    for (term, out, (to_sib, sums, land)), (second, used) in zip(items, seconds):
        half = out.shape[0] // 2
        for h in (0, 1):
            nf, ng = rings[h]
            for j in range(1, ng):
                cp, at = second[h]
                cp.wait_recv()
                k = slot(h, 0, (j + 1) % ng)
                add(out, sums, k, h, half, land[at])
                if j < ng - 1:
                    second[h] = (start(sums.at[k, pl.ds(h * half, half)], land.at[used], devs[h][1]), used)
                    used += 1
        yield
    for cp in sends:
        cp.wait_send()
    if g.C == 2:
        for (term, out, (to_sib, sums, land)), base in zip(items, bases):
            for k in range(nb):
                wire.at(base + k, to_sib.at[k], sums.at[k], g.dev(a, b, 1 - c)).wait_send()


def needs_turn(rows):
    return rows % 128 != 0


def turn_scratch(rows, width, L):
    return [pltpu.VMEM((width, L) if needs_turn(rows) else (16, 128), BF16)]


def product_term(left, turned, right, rows, mask=None):
    def term(block, cols):
        at = pl.ds(pl.multiple_of(block * rows, rows), rows)
        if needs_turn(rows):
            return dot(turned[at], right[:, cols])
        v = left[:, at]
        if mask is not None:
            v = (v.astype(F32) * mask[...]).astype(BF16)
        return dot_tokens(v, right[:, cols])

    return term


def turn_steps(rows, turned, left, mask=None):
    if isinstance(left, Later):
        left = left.ref()
    if needs_turn(rows):
        yield from transpose_steps(turned, left, mask)


def given_term(part, rows):
    def term(block, cols):
        return part[pl.ds(pl.multiple_of(block * rows, rows), rows), cols]

    return term


def mlp_back_call(g, low_two, gate_low, up_low, w_gate, w_up, middle, cot, live, gain, cid):
    L, width = low_two.shape
    F = gate_low.shape[1]
    half = L // 2
    rows = width // g.N
    count = tp_count(g, L) + 2 * reduce_count(g)
    grad = jax.ShapeDtypeStruct((rows, F), F32)

    def kernel(low_two, gate_low, up_low, w_gate, w_up, middle, cot, live, gain,
               mid_low, grad_middle, grad_gain, g_gate, g_up,
               two_t, term, sendbuf, recvbuf, *refs):
        send, recv = refs[-2:]
        bufs = refs[:-2]
        greet(plane_peers(g) + tp_peers(g))
        wire = Wire(send, recv)
        gate_low, up_low, w_gate, w_up, middle, cot = (v.ref() for v in (gate_low, up_low, w_gate, w_up, middle, cot))
        back = mlp_back_body((gate_low, up_low, w_gate, w_up, middle, cot, live, gain), (mid_low, grad_middle, grad_gain))

        def gate():
            yield from turn_steps(rows, two_t, low_two)
            yield from reduce_steps(g, wire, [(product_term(low_two.dst, two_t, gate_low, rows), g_gate, bufs[0:3])])

        def up():
            yield from reduce_steps(g, wire, [(product_term(low_two.dst, two_t, up_low, rows), g_up, bufs[3:6])])

        braid(
            tp_steps(g, wire, L, mid_low, *back, (term, sendbuf, recvbuf)),
            (gate(), MLP_GATE),
            (up(), MLP_UP),
        )

    scratch = turn_scratch(rows, width, L) + tp_bufs(g, L, width)
    for _ in range(2):
        scratch += reduce_bufs(g, rows, F)
    return call(
        kernel,
        [low_two, gate_low, up_low, w_gate, w_up, middle, cot, live, gain],
        [jax.ShapeDtypeStruct((L, width), BF16), jax.ShapeDtypeStruct((half, width), F32),
         jax.ShapeDtypeStruct((1, width), F32), grad, grad],
        scratch + sems(count),
        cid,
        "mlp_back",
        later=(1, 3, 2, 4, 0, 5, 6),
    )


def plane_others(g):
    s, q = lax.axis_index("shard"), lax.axis_index("ctx")
    me = s * g.Q + q
    out = []
    for k in range(1, g.N):
        d = (me + k) % g.N
        out.append({"shard": d // g.Q, "ctx": d % g.Q})
    return me, out


def total_steps(g, wire, mine, land_t, land_p, out):
    t = lax.axis_index("tp")
    me, others = plane_others(g)
    land_t[t] = mine[...]
    cps = [wire.copy(mine, land_t.at[t], {"tp": (t + k) % g.T}) for k in range(1, g.T)]
    for cp in cps:
        cp.start()
    yield
    for cp in cps:
        cp.wait()
    total = land_t[0]
    for d in range(1, g.T):
        total = total + land_t[d]
    mine[...] = total
    land_p[me] = total
    cps = [wire.copy(mine, land_p.at[me], d) for d in others]
    for cp in cps:
        cp.start()
    yield
    for cp in cps:
        cp.wait()
    total = land_p[0]
    for d in range(1, g.N):
        total = total + land_p[d]
    out[...] = total


def rec_back_call(g, branch_low, rec_low, w_branch, w_rec, x, grad_middle, gain, part_two, low_one, small, cid):
    L, width = x.shape
    CH = branch_low.shape[1]
    rows = width // g.N
    srows = small.shape[0] // g.N
    shapes = [(rows, CH), (rows, CH), (srows, small.shape[1])]
    count = tp_count(g, L) + len(shapes) * reduce_count(g) + g.T + g.N

    def kernel(branch_low, rec_low, w_branch, w_rec, x, grad_middle, gain, part_two, low_one, small,
               input_grad, gains, g_branch, g_rec, g_small,
               part_one, one_t, both, land_t, land_p, term, sendbuf, recvbuf, *refs):
        send, recv = refs[-2:]
        bufs = refs[:-2]
        t = lax.axis_index("tp")
        greet(plane_others(g)[1] + [{"tp": (t + k) % g.T} for k in range(1, g.T)])
        wire = Wire(send, recv)
        branch_low, rec_low, w_branch, w_rec, x, grad_middle = (
            v.ref() for v in (branch_low, rec_low, w_branch, w_rec, x, grad_middle)
        )
        back = rec_back_body((branch_low, rec_low, w_branch, w_rec, x, grad_middle, gain), (input_grad, part_one))

        def one(term, out, bufs):
            yield from reduce_steps(g, wire, [(term, out, bufs)])

        def branch():
            yield from turn_steps(rows, one_t, low_one)
            yield from one(product_term(low_one.dst, one_t, branch_low, rows), g_branch, bufs[0:3])

        def main():
            steps = tp_steps(g, wire, L, input_grad, *back, (term, sendbuf, recvbuf))
            for _ in range(L // 2 // PIECE + END["take_far"]):
                next(steps)
                yield
            both[:, :width] = part_one[...]
            both[:, width:] = part_two[...]
            totals = total_steps(g, wire, both, land_t, land_p, gains)
            next(totals)
            for _ in steps:
                next(totals, None)
                yield
            run(totals)

        braid(
            main(),
            (branch(), REC_BRANCH),
            (one(product_term(low_one.dst, one_t, rec_low, rows), g_rec, bufs[3:6]), REC_REC),
            (one(given_term(small, srows), g_small, bufs[6:9]), REC_SMALL),
        )

    scratch = [pltpu.VMEM((1, width), F32)] + turn_scratch(rows, width, L)
    scratch += [pltpu.VMEM((1, 2 * width), F32), pltpu.VMEM((g.T, 1, 2 * width), F32), pltpu.VMEM((g.N, 1, 2 * width), F32)]
    scratch += tp_bufs(g, L, width)
    for s in shapes:
        scratch += reduce_bufs(g, *s)
    return call(
        kernel,
        [branch_low, rec_low, w_branch, w_rec, x, grad_middle, gain, part_two, low_one, small],
        [jax.ShapeDtypeStruct((L, width), BF16), jax.ShapeDtypeStruct((1, 2 * width), F32)]
        + [jax.ShapeDtypeStruct(s, F32) for s in shapes],
        scratch + sems(count),
        cid,
        "rec_back",
        later=(0, 2, 1, 3, 8, 4, 5),
    )


def settle(arrays):
    n = len(arrays)

    def kernel(*refs):
        ins, outs, kept, sem = refs[:n], refs[n : 2 * n], refs[2 * n : 3 * n], refs[3 * n]
        cps = [pltpu.make_async_copy(ins[k], kept[k], sem.at[k]) for k in range(n)]
        back = [pltpu.make_async_copy(kept[k], outs[k], sem.at[n + k]) for k in range(n)]
        for cp in cps:
            cp.start()
        for k in range(n):
            cps[k].wait()
            back[k].start()
        for cp in back:
            cp.wait()

    return pl.pallas_call(
        kernel,
        out_shape=[jax.ShapeDtypeStruct(v.shape, v.dtype) for v in arrays],
        in_specs=[ANY] * n,
        out_specs=[ANY] * n,
        scratch_shapes=[pltpu.VMEM(v.shape, v.dtype) for v in arrays] + [pltpu.SemaphoreType.DMA((2 * n,))],
        compiler_params=pltpu.CompilerParams(vmem_limit_bytes=VMEM_LIMIT),
        name="settle",
    )(*arrays)


def up_to(n, k):
    return -(-n // k) * k


def local(g, inputs, lengths, cotangent, norm1_gain, branch_weight, rec_in_weight, conv_weight, conv_bias,
          rgate_weight, rgate_bias, igate_weight, igate_bias, decay_param, out_weight, norm2_gain,
          mlp_gate_weight, mlp_up_weight, mlp_down_weight):
    slots, block_len, width = inputs.shape
    L = slots * block_len
    N = g.N
    heads, rb, bw = rgate_weight.shape
    ch = heads * bw
    taps = conv_weight.shape[0]
    prow = pack_rows(rb)[0]

    def across(v):
        return jnp.pad(v, ((0, 0), (0, ch - v.shape[1])))

    vectors = jnp.concatenate([conv_weight.reshape(taps, -1)] + [p.reshape(1, -1) for p in (conv_bias, rgate_bias, igate_bias, decay_param)], axis=0)
    gains = jnp.stack([norm1_gain, norm2_gain])
    pack = jnp.concatenate(
        [rgate_weight.transpose(1, 0, 2).reshape(rb, ch), igate_weight.transpose(1, 0, 2).reshape(rb, ch), across(vectors), across(gains)],
        axis=0,
    )
    pack = jnp.pad(pack, ((0, prow - pack.shape[0]), (0, 0)))
    x_low = inputs.reshape(L, width)
    cot = cotangent.reshape(L, width)
    positions = lax.axis_index("ctx") * block_len + jnp.arange(block_len, dtype=jnp.int32)
    live = (positions[None, :] < lengths[:, None]).astype(F32).reshape(L, 1)
    (low_one, branch_pre, rec_pre, mixed, conv, rate, entry, state, edge, low_two, middle, w_rate, w_entry, vecs, gains,
     w_rec, w_branch, w_out, w_gate, w_up, w_down) = front_call(
        g, pack, rec_in_weight, branch_weight, out_weight, [mlp_gate_weight, mlp_up_weight, mlp_down_weight], x_low, bw, rb, 0
    )
    gain_one, gain_two = gains[0:1], gains[1:2]
    gate_pre = dot(low_two, w_gate)
    up_pre = dot(low_two, w_up)
    act, slope = gelu_both(gate_pre)
    hidden = (act * up_pre).astype(BF16)
    grad_low = (cot.astype(F32) * live).astype(BF16)
    grad_hidden = dot(grad_low, w_down)
    gate_low = (grad_hidden * up_pre * slope).astype(BF16)
    up_low = (grad_hidden * act).astype(BF16)
    mid_low, grad_middle, part_two, g_gate, g_up = mlp_back_call(
        g, low_two, gate_low, up_low, w_gate, w_up, middle, cot, live, gain_two, 2
    )
    branch_low, rec_low, d_rate, d_entry, d_vecs, output, g_down, g_out = back_call(
        g, mid_low, w_out, branch_pre, rec_pre, conv, rate, entry, state, edge, w_rate, w_entry, vecs, bw, middle,
        cot, live, hidden, w_down, mixed, 3
    )

    d_vecs = d_vecs.reshape(8, heads, N, rb).transpose(2, 0, 1, 3).reshape(N, -1)
    d_vecs = jnp.pad(d_vecs, ((0, 0), (0, up_to(d_vecs.shape[1], ch) - d_vecs.shape[1]))).reshape(N, -1, ch)
    flat = jnp.concatenate([d_rate.reshape(N, rb, ch), d_entry.reshape(N, rb, ch), d_vecs], axis=1)
    used = flat.shape[1]
    flat = jnp.pad(flat, ((0, 0), (0, up_to(used, 32) - used), (0, 0))).reshape(-1, ch)
    input_grad, gains, g_branch, g_rec, g_small = rec_back_call(
        g, branch_low, rec_low, w_branch, w_rec, x_low, grad_middle, gain_one, part_two, low_one, flat, 4
    )
    gains = lax.dynamic_slice(
        gains.reshape(2, N, -1), (0, lax.axis_index("shard") * g.Q + lax.axis_index("ctx"), 0), (2, 1, width // N)
    )[:, 0]
    g_small = g_small.reshape(-1)
    n = rb * ch
    g_rate = g_small[:n].reshape(rb, heads, bw).transpose(1, 0, 2)
    g_entry = g_small[n : 2 * n].reshape(rb, heads, bw).transpose(1, 0, 2)
    rest = g_small[2 * n : 2 * n + 8 * heads * rb].reshape(8, heads, rb)
    shape = (slots, block_len, width)
    output, input_grad, g_branch, g_rec, g_out, g_gate, g_up, g_down = settle(
        [output, input_grad, g_branch, g_rec, g_out, g_gate, g_up, g_down]
    )
    return (
        output.reshape(shape), input_grad.reshape(shape), gains[0], g_branch, g_rec, rest[:taps], rest[4],
        g_rate, rest[5], g_entry, rest[6], rest[7], g_out, gains[1], g_gate, g_up, g_down,
    )


def solution(mesh):
    plane = ("shard", "ctx")
    rows, cols = P(plane), P(plane, "tp")
    tok, gate, chan = P("shard", "ctx", None), P("tp", plane, None), P("tp", plane)
    taps = P(None, "tp", plane)
    params = (rows, cols, cols, taps, chan, gate, chan, gate, chan, chan, cols, rows, cols, cols, cols)
    return jax.shard_map(
        functools.partial(local, Grid(mesh)),
        mesh=mesh,
        in_specs=(tok, P("shard"), tok) + params,
        out_specs=(tok, tok) + params,
        check_vma=False,
    )
```

```python
import functools

import jax
import jax.numpy as jnp
from jax import lax
from jax.experimental import pallas as pl
from jax.experimental.pallas import tpu as pltpu
from jax.sharding import PartitionSpec as P

EPS = 1e-06
DECAY_SCALE = 8.0
F32 = jnp.float32
BF16 = jnp.bfloat16
MESH = pl.DeviceIdType.MESH
ANY = pl.BlockSpec(memory_space=pl.ANY)
VM = pl.BlockSpec(memory_space=pltpu.VMEM)
VMEM_LIMIT = 63 * 1024 * 1024


def dot(a, b):
    return jnp.dot(a, b, preferred_element_type=F32)


def dot_rows(a, b):
    return lax.dot_general(a, b, (((1,), (1,)), ((), ())), preferred_element_type=F32)


def dot_tokens(a, b):
    return lax.dot_general(a, b, (((0,), (0,)), ((), ())), preferred_element_type=F32)


def halves(v):
    hi = v.astype(BF16)
    return hi, (v - hi.astype(F32)).astype(BF16)


def gelu(v):
    return jax.nn.gelu(v)


def gelu_both(v):
    c = 0.7978845608028654
    th = jnp.tanh(c * (v + 0.044715 * v * v * v))
    half = 0.5 * (1.0 + th)
    return v * half, half + 0.5 * v * (1.0 - th * th) * c * (1.0 + 3 * 0.044715 * v * v)


def sigmoid(v):
    return 1.0 / (1.0 + jnp.exp(-v))


def minus_expm1(v):
    near = -v * (1.0 + v / 2 * (1.0 + v / 3 * (1.0 + v / 4 * (1.0 + v / 5 * (1.0 + v / 6)))))
    return jnp.where(v > -0.25, near, 1.0 - jnp.exp(v))


class Grid:
    def __init__(self, mesh):
        self.S, self.Q, self.T = (mesh.shape[n] for n in ("shard", "ctx", "tp"))
        dev = mesh.devices

        def chip(d):
            return tuple(getattr(d, "coords", None) or ())

        def paired(one, two):
            return bool(chip(one)) and chip(one) == chip(two)

        self.core_in = None
        if self.Q % 2 == 0 and paired(dev[0, 0, 0], dev[0, 1, 0]):
            self.core_in = "ctx"
        elif self.S % 2 == 0 and paired(dev[0, 0, 0], dev[1, 0, 0]):
            self.core_in = "shard"
        self.C = 1 if self.core_in is None else 2
        self.A = self.S // 2 if self.core_in == "shard" else self.S
        self.B = self.Q // 2 if self.core_in == "ctx" else self.Q
        self.N = self.S * self.Q

    def me(self):
        s, q = lax.axis_index("shard"), lax.axis_index("ctx")
        if self.core_in == "ctx":
            return s, q // 2, q % 2
        if self.core_in == "shard":
            return s // 2, q, s % 2
        return s, q, 0

    def shard_ctx(self, a, b, c):
        if self.core_in == "ctx":
            return a, b * 2 + c
        if self.core_in == "shard":
            return a * 2 + c, b
        return a, b

    def block(self, a, b, c):
        s, q = self.shard_ctx(a, b, c)
        return s * self.Q + q

    def dev(self, a, b, c):
        s, q = self.shard_ctx(a, b, c)
        return {"shard": s, "ctx": q}


class Wire:
    def __init__(self, send, recv, base=0):
        self.send, self.recv, self.used = send, recv, base

    def copy(self, src, dst, dev):
        self.used += 1
        return self.at(self.used - 1, src, dst, dev)

    def at(self, k, src, dst, dev):
        return pltpu.make_async_remote_copy(
            src_ref=src,
            dst_ref=dst,
            send_sem=self.send.at[k],
            recv_sem=self.recv.at[k],
            device_id=dev,
            device_id_type=MESH,
        )


def greet(devs):
    bar = pltpu.get_barrier_semaphore()
    for d in devs:
        pl.semaphore_signal(bar, inc=1, device_id=d, device_id_type=MESH)
    pl.semaphore_wait(bar, len(devs))


def ring_peers(size, at, place):
    if size == 1:
        return []
    if size == 2:
        return [place((at + 1) % 2)]
    return [place((at + 1) % size), place((at + size - 1) % size)]


def plane_peers(g):
    a, b, c = g.me()
    out = ring_peers(g.A, a, lambda k: g.dev(k, b, c))
    out += ring_peers(g.B, b, lambda k: g.dev(a, k, c))
    if g.C == 2:
        out.append(g.dev(a, b, 1 - c))
    return out


def braid(main, *sides):
    k = 0
    for _ in main:
        for steps, plan in sides:
            for _ in range(plan[k] if k < len(plan) else 0):
                next(steps, None)
        k += 1
    left = [s[0] for s in sides]
    while left:
        left = [s for s in left if next(s, left) is not left]


def only(steps, n):
    for _ in range(n):
        next(steps)
        yield


def at_steps(*pairs):
    plan = [0] * (1 + max(last for _, last, _ in pairs))
    for first, last, each in pairs:
        for k in range(first, last + 1):
            plan[k] += each
    return tuple(plan)


ALWAYS = (1,) * 64


def run(*steps):
    for s in steps:
        for _ in s:
            pass


class Later:
    def __init__(self, src, dst, sem):
        self.copy, self.dst, self.here = pltpu.make_async_copy(src, dst, sem), dst, False
        self.copy.start()

    def ref(self):
        if not self.here:
            self.copy.wait()
            self.here = True
        return self.dst


def call(kernel, operands, out_shape, scratch, cid, name, in_specs=None, out_specs=None, later=(), early=()):
    in_specs = list(in_specs or [VM] * len(operands))
    out_specs = list(out_specs or [VM] * len(out_shape))
    for k in later:
        in_specs[k] = ANY
    for k in early:
        out_specs[k] = ANY
    n, m = len(later), len(early)
    n_in = len(operands)

    def body(*refs):
        refs = list(refs)
        if m:
            kept, sem = refs[-m - 1 : -1], refs[-1]
            refs = refs[: -m - 1]
            copies = {}
            for j, k in enumerate(early):
                copies[id(kept[j])] = pltpu.make_async_copy(kept[j], refs[n_in + k], sem.at[j])
                refs[n_in + k] = kept[j]
        if n:
            held, sem_in = refs[-n - 1 : -1], refs[-1]
            refs = refs[: -n - 1]
            for j, k in enumerate(later):
                refs[k] = Later(refs[k], held[j], sem_in.at[j])
        if not m:
            kernel(*refs)
            return
        kernel(*refs, send_out=lambda *which: [copies[id(r)].start() for r in which])
        for cp in copies.values():
            cp.wait()

    extra = [pltpu.VMEM(operands[k].shape, operands[k].dtype) for k in later]
    if n:
        extra.append(pltpu.SemaphoreType.DMA((n,)))
    extra += [pltpu.VMEM(out_shape[k].shape, out_shape[k].dtype) for k in early]
    if m:
        extra.append(pltpu.SemaphoreType.DMA((m,)))
    return pl.pallas_call(
        body,
        out_shape=out_shape,
        in_specs=in_specs,
        out_specs=out_specs,
        scratch_shapes=list(scratch) + extra,
        compiler_params=pltpu.CompilerParams(
            collective_id=cid, has_side_effects=True, vmem_limit_bytes=VMEM_LIMIT
        ),
        name=name,
    )(*operands)


def sems(n):
    return [pltpu.SemaphoreType.DMA((max(1, n),)), pltpu.SemaphoreType.DMA((max(1, n),))]


def gather_count(g):
    ring = 0
    for nf, ng in ((g.A, g.B), (g.B, g.A)):
        ring += (nf - 1) + (ng - 1) * nf
    return ring + (g.C - 1) * (1 + ring)


def gather_steps(g, wire, here, srcs, dsts):
    a, b, c = g.me()
    sib = None if g.C == 1 else g.dev(a, b, 1 - c)
    sends, sib_copies = [], []

    def ring(h):
        if h == 0:
            return g.A, a, (lambda k: g.dev(k, b, c)), g.B, b, (lambda k: g.dev(a, k, c)), (lambda f, s: g.block(f, s, c))
        return g.B, b, (lambda k: g.dev(a, k, c)), g.A, a, (lambda k: g.dev(k, b, c)), (lambda f, s: g.block(s, f, c))

    def start(src, dst, dev):
        cp = wire.copy(src, dst, dev)
        cp.start()
        sends.append(cp)
        return cp

    def rows_of(dst, blk, h, rows):
        half = rows // 2
        return dst.at[pl.ds(pl.multiple_of(blk * rows + h * half, half), half)]

    state = []
    mine = g.block(a, b, c)
    local_copies = []
    for src, dst in zip(srcs, dsts):
        rows = src.shape[0]
        half = rows // 2
        cp = pltpu.make_async_copy(src, dst.at[pl.ds(pl.multiple_of(mine * rows, rows), rows)], here.at[len(local_copies)])
        cp.start()
        local_copies.append(cp)
        per = []
        for h in (0, 1):
            nf, f, fdev, ng, s, sdev, blk = ring(h)
            own = src.at[pl.ds(h * half, half)]
            land = rows_of(dst, mine, h, rows)
            first = start(own, land, fdev((f + 1) % nf)) if nf > 1 else None
            per.append([first, None, own, land])
        for h in (0, 1):
            nf, f, fdev, ng, s, sdev, blk = ring(h)
            _, _, own, land = per[h]
            second = {}
            if ng > 1:
                second[(0, 0)] = start(own, land, sdev((s + 1) % ng))
            per[h][1] = second
        if sib is not None:
            whole = dst.at[pl.ds(pl.multiple_of(mine * rows, rows), rows)]
            sib_copies.append(start(src, whole, sib))
        state.append(per)
        yield
    for (src, dst), per in zip(zip(srcs, dsts), state):
        rows = src.shape[0]
        for h in (0, 1):
            nf, f, fdev, ng, s, sdev, blk = ring(h)
            cp = per[h][0]
            for i in range(1, nf):
                cp.wait_recv()
                at = rows_of(dst, blk((f - i) % nf, s), h, rows)
                if i < nf - 1:
                    cp = start(at, at, fdev((f + 1) % nf))
                if ng > 1:
                    per[h][1][(0, i)] = start(at, at, sdev((s + 1) % ng))
                if sib is not None:
                    sib_copies.append(start(at, at, sib))
        yield
    for (src, dst), per in zip(zip(srcs, dsts), state):
        rows = src.shape[0]
        for h in (0, 1):
            nf, f, fdev, ng, s, sdev, blk = ring(h)
            second = per[h][1]
            for j in range(1, ng):
                for i in range(nf):
                    second[(j - 1, i)].wait_recv()
                    at = rows_of(dst, blk((f - i) % nf, (s - j) % ng), h, rows)
                    if j < ng - 1:
                        second[(j, i)] = start(at, at, sdev((s + 1) % ng))
                    if sib is not None:
                        sib_copies.append(start(at, at, sib))
        yield
    for cp in local_copies:
        cp.wait()
    for cp in sib_copies:
        cp.wait_recv()
    for cp in sends:
        cp.wait_send()


def tp_peers(g):
    t = lax.axis_index("tp")
    return ring_peers(g.T, t, lambda k: {"tp": k})


MIX_GATE = at_steps((6, 6, 1), (15, 15, 1))
MIX_UP = at_steps((11, 11, 1), (19, 19, 1))
MIX_DOWN = at_steps((11, 11, 1))
BACK_Z = ALWAYS
BACK_DOWN = at_steps((2, 2, 1), (4, 4, 1), (6, 6, 1), (8, 8, 1), (9, 10, 2), (17, 17, 1))
BACK_OUT = at_steps((11, 12, 2), (13, 16, 1), (21, 21, 1))
MLP_GATE = at_steps((0, 3, 2), (8, 8, 1), (14, 14, 1))
MLP_UP = at_steps((4, 7, 2), (14, 14, 1), (21, 21, 1))
REC_BRANCH = at_steps((0, 3, 2), (9, 9, 1), (17, 17, 1))
REC_REC = at_steps((4, 7, 2), (13, 13, 1), (19, 19, 1))
REC_SMALL = at_steps((8, 11, 2), (15, 15, 1), (20, 20, 1))
PIECE = 32
CHUNK = 256


def tp_count(g, rows):
    return 4 * (rows // 2 // PIECE)


def tp_place(g):
    t = lax.axis_index("tp")
    side = jnp.where(t >= (g.T + 1) // 2, 1, 0)
    return side, jnp.where(side == 1, g.T - 1 - t, t)


END = {"send_near": 0, "take_far": 8, "take_near": 14}
INNER = {"send_near": 0, "take_far": 2, "pass_far": 6, "take_near": 8}


def tp_steps(g, wire, rows, out, partial=None, finish=None, bufs=None, gather=True):
    T = g.T
    t = lax.axis_index("tp")
    half = rows // 2
    pieces = half // PIECE
    side, pos = tp_place(g)
    end, inner = pos == 0, pos > 0
    near, far = side, 1 - side
    away = {"tp": jnp.where(side == 1, t - 1, t + 1)}
    home = {"tp": jnp.where(side == 1, (t + 1) % T, (t + T - 1) % T)}
    k_rs = wire.used
    if partial is not None:
        wire.used += 2 * pieces
    k_ag = wire.used
    if gather:
        wire.used += 2 * pieces

    def row(d, p):
        return pl.multiple_of(half * (1 - d) + p * PIECE, PIECE)

    def rs(d, p, dev):
        return wire.at(k_rs + d * pieces + p, bufs[1].at[d, p], bufs[2].at[d, p], dev)

    def ag(d, p, dev):
        at = out.at[pl.ds(row(d, p), PIECE)]
        return wire.at(k_ag + d * pieces + p, at, at, dev)

    step = chunk_rows(g, rows, out.shape[1])
    per = step // PIECE

    def ready(d, p, which):
        term = bufs[0].at[which]
        if p % per == 0:
            partial(pl.multiple_of(half * (1 - d) + p * PIECE, step), step, term)
        return term.at[pl.ds(p % per * PIECE, PIECE)]

    def send_near(p, at_end):
        part = ready(near, p, 0)[...]
        if not at_end:
            rs(near, p, away).wait_recv()
            part = part + bufs[2][near, p].astype(F32)
        bufs[1][near, p] = part.astype(BF16)
        rs(near, p, away).start()

    def take_far(p, at_end):
        part = ready(far, p, 1)
        rs(far, p, home).wait_recv()
        total = part[...] + bufs[2][far, p].astype(F32)
        if not at_end:
            bufs[1][far, p] = total.astype(BF16)
            rs(far, p, home).start()
            return
        done = finish(total, p * PIECE, row(far, p), PIECE)
        if gather:
            out[pl.ds(row(far, p), PIECE)] = done
            ag(far, p, away).start()
        else:
            out[p * PIECE : (p + 1) * PIECE] = done

    def pass_far(p, at_end):
        ag(far, p, away).wait_recv()
        ag(far, p, away).start()

    def take_near(p, at_end):
        ag(near, p, home).wait_recv()
        if not at_end:
            ag(near, p, home).start()

    acts = {"send_near": send_near, "take_far": take_far, "pass_far": pass_far, "take_near": take_near}
    if partial is None:

        @pl.when(end)
        def _():
            for p in range(pieces):
                ag(far, p, away).start()

        acts = {"pass_far": pass_far, "take_near": take_near}
        yield
    elif not gather:
        acts = {"send_near": send_near, "take_far": take_far}

    def schedule(lates):
        lates = {k: v for k, v in lates.items() if k in acts}
        least = min(lates.values())
        return [(acts[k], v - least) for k, v in lates.items()]

    plans = [(end, True, schedule(END)), (inner, False, schedule(INNER))]
    for i in range(pieces + max(late for _, _, plan in plans for _, late in plan)):
        for where, at_end, plan in plans:

            @pl.when(where)
            def _():
                for act, late in plan:
                    if 0 <= i - late < pieces:
                        act(i - late, at_end)

        yield
    if partial is not None:
        for p in range(pieces):
            rs(near, p, away).wait_send()
    if gather:
        for p in range(pieces):
            ag(far, p, away).wait_send()

    @pl.when(inner)
    def _():
        for p in range(pieces):
            if partial is not None:
                rs(far, p, home).wait_send()
            if gather:
                ag(near, p, home).wait_send()


def chunk_rows(g, rows, width):
    return min(CHUNK // 4 if needs_turn(width // g.N) else CHUNK, rows // 2)


def tp_bufs(g, rows, width):
    pieces = rows // 2 // PIECE
    return [
        pltpu.VMEM((2, chunk_rows(g, rows, width), width), F32),
        pltpu.VMEM((2, pieces, PIECE, width), BF16),
        pltpu.VMEM((2, pieces, PIECE, width), BF16),
    ]


def transpose_steps(dst, src, scale=None):
    if isinstance(src, Later):
        src = src.ref()
    width = src.shape[1]
    part = 512
    assert width % part == 0

    for at in range(0, width, part):

        def body(j, _):
            c0 = pl.multiple_of(at + j * 128, 128)
            v = src[:, pl.ds(c0, 128)]
            if scale is not None:
                v = (v.astype(F32) * scale[...]).astype(BF16)
            dst[pl.ds(c0, 128), :] = v.T
            return 0

        lax.fori_loop(0, part // 128, body, 0)
        yield


def chain(*steps):
    for s in steps:
        yield from s


def tile_of(width):
    return 512 if width % 512 == 0 else width


def rows_product(term, at, n, pairs):
    width = term.shape[1]
    tile = tile_of(width)

    def body(j, _):
        c0 = pl.multiple_of(j * tile, tile)
        total = None
        for l, r in pairs:
            p = dot_rows(l[pl.ds(at, n)], r[pl.ds(c0, tile)])
            total = p if total is None else total + p
        term[:, pl.ds(c0, tile)] = total
        return 0

    lax.fori_loop(0, width // tile, body, 0)


def rows_dot(dst, left, right):
    step = 256 if left.shape[0] % 256 == 0 else left.shape[0]

    def body(i, _):
        r0 = pl.ds(pl.multiple_of(i * step, step), step)
        dst[r0] = dot(left[r0], right[...])
        return 0

    lax.fori_loop(0, left.shape[0] // step, body, 0)


def mean_square(v):
    return jnp.mean(v * v, axis=-1, keepdims=True)


def mix_out_body(ins, outs):
    mixed, w_out, x, gain = ins
    _, middle = outs

    def partial(at, n, term):
        rows_product(term, at, n, [(mixed, w_out)])

    def finish(total, near, at, n):
        m = x[pl.ds(at, n)].astype(F32) + total
        middle[near : near + n] = m
        return (m * lax.rsqrt(mean_square(m) + EPS) * gain[...]).astype(BF16)

    return partial, finish


def mlp_out_body(ins, outs):
    hidden, w_down, middle, live = ins

    def partial(at, n, term):
        rows_product(term, at, n, [(hidden, w_down)])

    def finish(total, near, at, n):
        return ((middle[near : near + n] + total) * live[pl.ds(at, n)]).astype(BF16)

    return partial, finish


def norm_back(grad_normed, rows, gain):
    inv = lax.rsqrt(mean_square(rows) + EPS)
    gg = grad_normed * gain
    back = inv * gg - rows * (inv * inv * inv) * jnp.mean(gg * rows, axis=-1, keepdims=True)
    return back, jnp.sum(grad_normed * rows * inv, axis=0, keepdims=True)


def mlp_back_body(ins, outs):
    gate_low, up_low, w_gate, w_up, middle, cot, live, gain = ins
    _, grad_middle, grad_gain = outs
    grad_gain[...] = jnp.zeros_like(grad_gain)

    def partial(at, n, term):
        rows_product(term, at, n, [(gate_low, w_gate), (up_low, w_up)])

    def finish(total, near, at, n):
        back, gain_sum = norm_back(total, middle[near : near + n], gain[...])
        gm = cot[pl.ds(at, n)].astype(F32) * live[pl.ds(at, n)] + back
        grad_middle[near : near + n] = gm
        grad_gain[...] = grad_gain[...] + gain_sum
        return gm.astype(BF16)

    return partial, finish


def rec_back_body(ins, outs):
    branch_low, rec_low, w_branch, w_rec, x, grad_middle, gain = ins
    _, grad_gain = outs
    grad_gain[...] = jnp.zeros_like(grad_gain)

    def partial(at, n, term):
        rows_product(term, at, n, [(branch_low, w_branch), (rec_low, w_rec)])

    def finish(total, near, at, n):
        back, gain_sum = norm_back(total, x[pl.ds(at, n)].astype(F32), gain[...])
        grad_gain[...] = grad_gain[...] + gain_sum
        return (grad_middle[near : near + n] + back).astype(BF16)

    return partial, finish


TAPS, SHIFT, RBIAS, EBIAS, SOFT, SLOPE = 0, 4, 5, 6, 7, 8
ROWS = 64
GROUP = 8


def ctx_peers(g):
    q = lax.axis_index("ctx")
    return [{"ctx": (q + k) % g.Q} for k in range(1, g.Q)]


def swap_edges(g, wire, src, land):
    q = lax.axis_index("ctx")
    cps = []
    for k in range(1, g.Q):
        cp = wire.copy(src, land.at[q], {"ctx": (q + k) % g.Q})
        cp.start()
        cps.append(cp)
    yield
    for cp in cps:
        cp.wait_recv()
    for cp in cps:
        cp.wait_send()


def row_shift(v, n):
    return pltpu.roll(v, n % v.shape[0], 0)


def forward_steps(g, wire, branch, w_rate, w_entry, vecs, mixed, conv, rate, entry, state, edge,
                  ext, acum, bcum, tot, gath):
    L, CH = branch.shape
    q = lax.axis_index("ctx")
    sub = lax.broadcasted_iota(jnp.int32, (GROUP, 1), 0)

    def chunk(i, carry):
        ca, cb = carry
        r0 = i * ROWS
        wide = ext[pl.ds(r0, ROWS + 8)]
        c = vecs[SHIFT : SHIFT + 1] + vecs[TAPS : TAPS + 1] * wide[8:]
        for k in range(1, 4):
            c = c + vecs[TAPS + k : TAPS + k + 1] * row_shift(wide, k)[8:]
        conv[pl.ds(r0, ROWS)] = c
        hi, lo = halves(c)
        gr = sigmoid(dot(hi, w_rate[...]) + dot(lo, w_rate[...]) + vecs[RBIAS : RBIAS + 1])
        ge = sigmoid(dot(hi, w_entry[...]) + dot(lo, w_entry[...]) + vecs[EBIAS : EBIAS + 1])
        rate[pl.ds(r0, ROWS)] = gr
        entry[pl.ds(r0, ROWS)] = ge
        log = -DECAY_SCALE * gr * vecs[SOFT : SOFT + 1]
        dec = jnp.exp(log)
        drive = jnp.sqrt(minus_expm1(2.0 * log)) * ge * c
        for n in range(ROWS // GROUP):
            A = dec[n * GROUP : (n + 1) * GROUP]
            B = drive[n * GROUP : (n + 1) * GROUP]
            for step in (1, 2, 4):
                keep = sub >= step
                As = jnp.where(keep, row_shift(A, step), 1.0)
                Bs = jnp.where(keep, row_shift(B, step), 0.0)
                B = B + A * Bs
                A = A * As
            B = B + A * cb
            A = A * ca
            acum[pl.ds(r0 + n * GROUP, GROUP)] = A
            bcum[pl.ds(r0 + n * GROUP, GROUP)] = B
            ca = A[GROUP - 1 : GROUP]
            cb = B[GROUP - 1 : GROUP]
        return ca, cb

    ca, cb = jnp.ones((1, CH), F32), jnp.zeros((1, CH), F32)
    for i in range(L // ROWS):
        ca, cb = chunk(i, (ca, cb))
        yield
    tot[0:1] = ca
    tot[1:2] = cb
    start = jnp.zeros((1, CH), F32)
    if g.Q > 1:
        yield from swap_edges(g, wire, tot, gath)
        for d in range(g.Q - 1):
            new = gath[d, 0:1] * start + gath[d, 1:2]
            start = jnp.where(d < q, new, start)
    edge[...] = jnp.broadcast_to(start, (8, CH))
    yield

    def fix(i, _):
        r0 = pl.multiple_of(i * ROWS, ROWS)
        s = bcum[pl.ds(r0, ROWS)] + acum[pl.ds(r0, ROWS)] * start
        state[pl.ds(r0, ROWS)] = s
        mixed[pl.ds(r0, ROWS)] = (gelu_both(branch[pl.ds(r0, ROWS)])[0] * s).astype(BF16)
        return 0

    lax.fori_loop(0, L // ROWS, fix, 0)
    yield


def small_rows(rb):
    return up_to(2 * rb + 8, 32)


def pack_rows(rb):
    return up_to(2 * rb + 10, 32), 2 * rb, 2 * rb + 8


def iota2(shape):
    return lax.broadcasted_iota(jnp.int32, shape, 0), lax.broadcasted_iota(jnp.int32, shape, 1)


def log1p_small(e):
    return jnp.where(e < 0.02, e * (1.0 - e * (0.5 - e * (1.0 / 3 - e * 0.25))), jnp.log(1.0 + e))


def unpack(packs, bw, rb, rows, w_rate, w_entry, vecs, gains):
    total, CH = packs.shape
    n = bw // rb
    prow, o_vec, o_gain = pack_rows(rb)
    m, l = iota2((bw, total))
    _, lane = iota2((bw, CH))
    for dst, off in ((w_rate, 0), (w_entry, rb)):
        pick = jnp.logical_and(l // prow == m // rb, l % prow == m % rb + off)
        block = dot(jnp.where(pick, 1.0, 0.0).astype(BF16), packs[...])
        for h in range(CH // bw):
            dst[h * bw : (h + 1) * bw] = jnp.where(lane // bw == h, block, 0.0).astype(BF16)

    def rows_at(off):
        m, l = iota2((n * 8, total))
        pick = l == (m // 8) * prow + off + m % 8
        return dot(jnp.where(pick, 1.0, 0.0).astype(BF16), packs[...])

    short = rows_at(o_vec)[:, :128].astype(BF16)
    l, m = iota2((128, CH))
    spread = jnp.logical_and(l // rb == m // bw, l % rb == m % rb)
    wide = dot(short, jnp.where(spread, 1.0, 0.0).astype(BF16))
    _, lane = iota2((8, CH))
    vec = jnp.zeros((8, CH), F32)
    for j in range(n):
        vec = vec + jnp.where(lane % bw // rb == j, wide[j * 8 : (j + 1) * 8], 0.0)
    decay = vec[7:8]
    e = jnp.exp(-jnp.abs(decay))
    vecs[0:7] = vec[0:7]
    vecs[SOFT : SOFT + 1] = jnp.maximum(-decay, 0.0) + log1p_small(e)
    vecs[SLOPE : SLOPE + 1] = sigmoid(-decay)
    vecs[SLOPE + 1 :] = jnp.zeros((16 - SLOPE - 1, CH), F32)
    both = rows_at(o_gain)
    if rows % 128 == 0:
        for j in range(n):
            for u in range(2):
                gains[u : u + 1, j * rows : (j + 1) * rows] = both[j * 8 + u : j * 8 + u + 1, :rows]
    else:
        l, m = iota2((128, gains.shape[1]))
        row = jnp.zeros((8, gains.shape[1]), F32)
        for j in range(n):
            place = jnp.logical_and(l < rows, m == l + j * rows)
            row = row + dot(both[j * 8 : (j + 1) * 8, :128].astype(BF16), jnp.where(place, 1.0, 0.0).astype(BF16))
        gains[...] = row[:2]


def mlp_forward_steps(w_gate, w_up, low_two, gate_pre, up_pre, hidden, wg, wu, og, ou, oh, sem_in, sem_out):
    L, tile = og.shape[1], og.shape[2]
    nt = w_gate.shape[1] // tile

    def loads(j):
        cols = pl.ds(j * tile, tile)
        return [pltpu.make_async_copy(w.at[:, cols], b.at[j % 2], sem_in.at[j % 2, i]) for i, (w, b) in enumerate(((w_gate, wg), (w_up, wu)))]

    def stores(j):
        cols = pl.ds(j * tile, tile)
        return [pltpu.make_async_copy(b.at[j % 2], o.at[:, cols], sem_out.at[j % 2, i]) for i, (b, o) in enumerate(((og, gate_pre), (ou, up_pre), (oh, hidden)))]

    for cp in loads(0):
        cp.start()
    for j in range(nt):
        if j + 1 < nt:
            for cp in loads(j + 1):
                cp.start()
        for cp in loads(j):
            cp.wait()
        if j >= 2:
            for cp in stores(j - 2):
                cp.wait()
        gate, up, out = og.at[j % 2], ou.at[j % 2], oh.at[j % 2]
        rows_dot(gate, low_two, wg.at[j % 2])
        rows_dot(up, low_two, wu.at[j % 2])

        def act(i, _):
            r0 = pl.ds(pl.multiple_of(i * 32, 32), 32)
            out[r0] = (gelu_both(gate[r0])[0] * up[r0]).astype(BF16)
            return 0

        lax.fori_loop(0, L // 32, act, 0)
        for cp in stores(j):
            cp.start()
        yield
    for j in range(max(0, nt - 2), nt):
        for cp in stores(j):
            cp.wait()


def front_call(g, pack, rec_shard, branch_shard, out_shard, mlp_shards, x, bw, rb, cid):
    L, width = x.shape
    CH = pack.shape[1]
    half = L // 2
    n = len(mlp_shards)
    rows = out_shard.shape[0]
    wide = jax.ShapeDtypeStruct((L, CH), F32)
    dense = jax.ShapeDtypeStruct((CH, CH), BF16)

    def whole(s):
        return jax.ShapeDtypeStruct((g.N * s.shape[0], s.shape[1]), s.dtype)

    low = jax.ShapeDtypeStruct((L, width), BF16)
    outs = [low, wide, wide, jax.ShapeDtypeStruct((L, CH), BF16), wide, wide, wide, wide, jax.ShapeDtypeStruct((8, CH), F32),
            low, jax.ShapeDtypeStruct((half, width), F32), dense, dense, jax.ShapeDtypeStruct((16, CH), F32),
            jax.ShapeDtypeStruct((2, width), F32), whole(rec_shard), whole(branch_shard), whole(out_shard)]
    outs += [whole(s) for s in mlp_shards]
    F = mlp_shards[0].shape[1]
    tile = tile_of(F)
    outs += [jax.ShapeDtypeStruct((L, F), F32), jax.ShapeDtypeStruct((L, F), F32), jax.ShapeDtypeStruct((L, F), BF16)]
    count = 2 * g.Q + tp_count(g, L) + (n + 4) * gather_count(g)

    def kernel(pack, rec_shard, branch_shard, out_shard, *refs, send_out):
        shards, x = refs[:n], refs[n]
        (low_one, branch, rec, mixed, conv, rate, entry, state, edge, low_two, middle, w_rate, w_entry, vecs, gains,
         w_rec, w_branch, w_out) = refs[n + 1 : n + 19]
        full = refs[n + 19 : 2 * n + 19]
        made = refs[2 * n + 19 : 2 * n + 22]
        (packs, x_edge, a_edge, ext, acum, bcum, tot, gath, term, sendbuf, recvbuf, send, recv, here, *tiles) = refs[2 * n + 22 :]
        q = lax.axis_index("ctx")
        greet(ctx_peers(g) + plane_peers(g) + tp_peers(g))
        wire = Wire(send, recv)
        slots = iter(range(n + 4))

        def gather(srcs, dsts):
            at = [next(slots) for _ in srcs]
            return gather_steps(g, wire, here.at[pl.ds(at[0], len(at))], srcs, dsts)

        small = gather([pack], [packs])
        next(small)
        edge_copy = None
        if g.Q > 1:
            edge_copy = wire.copy(x.at[pl.ds(L - 16, 16)], x_edge, {"ctx": (q + 1) % g.Q})
            edge_copy.start()
        of_rec = gather([rec_shard], [w_rec])
        of_branch = gather([branch_shard], [w_branch])
        of_out = gather([out_shard], [w_out])
        of_gate, of_up, of_down = (gather([s], [d]) for s, d in zip(shards, full))
        next(of_rec)
        next(of_branch)
        run(small)
        unpack(packs, bw, rb, rows, w_rate, w_entry, vecs, gains)

        def norm_rows(i, _):
            r0 = pl.ds(pl.multiple_of(i * ROWS, ROWS), ROWS)
            v = x[r0].astype(F32)
            low_one[r0] = (v * lax.rsqrt(mean_square(v) + EPS) * gains[0:1]).astype(BF16)
            return 0

        lax.fori_loop(0, L // ROWS, norm_rows, 0)
        next(of_rec)
        next(of_branch)
        next(of_out)
        next(of_rec)
        next(of_branch)
        if g.Q > 1:
            edge_copy.wait()
            v = x_edge[...].astype(F32)
            a_edge[...] = (v * lax.rsqrt(mean_square(v) + EPS) * gains[0:1]).astype(BF16)
        run(of_rec)
        rows_dot(rec, low_one, w_rec)
        ext[8:] = rec[...]
        if g.Q > 1:
            ext[0:8] = jnp.where(q > 0, dot(a_edge[...], w_rec[...])[8:], 0.0)
        else:
            ext[0:8] = jnp.zeros((8, CH), F32)
        fwd = forward_steps(g, wire, branch, w_rate, w_entry, vecs, mixed, conv, rate, entry, state, edge,
                            ext, acum, bcum, tot, gath)
        for k in range(L // ROWS):
            next(fwd)
            if k == 2:
                next(of_out)
            if k == 6:
                next(of_out)
        if g.Q > 1:
            next(fwd)
        next(of_gate)
        next(of_up)
        run(of_branch)
        rows_dot(branch, low_one, w_branch)
        send_out(low_one, rec, conv, rate, entry, w_rate, w_entry, w_rec, w_branch, branch)
        run(fwd, of_out)
        send_out(mixed, state, w_out)
        partial, finish = mix_out_body((mixed, w_out, x, gains.at[pl.ds(1, 1)]), (low_two, middle))
        braid(
            tp_steps(g, wire, L, low_two, partial, finish, (term, sendbuf, recvbuf)),
            (of_gate, MIX_GATE),
            (of_up, MIX_UP),
            (only(of_down, 1), MIX_DOWN),
        )
        for _ in mlp_forward_steps(full[0], full[1], low_two, *made, *tiles):
            next(of_down, None)
        run(of_down)

    return call(
        kernel,
        [pack, rec_shard, branch_shard, out_shard, *mlp_shards, x],
        outs,
        [
            pltpu.VMEM((g.N * pack.shape[0], CH), BF16),
            pltpu.VMEM((16, width), BF16),
            pltpu.VMEM((16, width), BF16),
            pltpu.VMEM((L + 8, CH), F32),
            pltpu.VMEM((L, CH), F32),
            pltpu.VMEM((L, CH), F32),
            pltpu.VMEM((8, CH), F32),
            pltpu.VMEM((g.Q, 8, CH), F32),
        ]
        + tp_bufs(g, L, width)
        + sems(count)
        + [pltpu.SemaphoreType.DMA((n + 4,))]
        + [pltpu.VMEM((2, width, tile), BF16)] * 2
        + [pltpu.VMEM((2, L, tile), F32)] * 2
        + [pltpu.VMEM((2, L, tile), BF16), pltpu.SemaphoreType.DMA((2, 2)), pltpu.SemaphoreType.DMA((2, 3))],
        cid,
        "front",
        [VM] * (n + 5),
        [VM] * 18 + [ANY] * (n + 3),
        early=(0, 1, 2, 3, 4, 5, 6, 7, 11, 12, 15, 16, 17),
    )


def backward_steps(g, wire, mid_low, w_out, branch, rec, conv, rate, entry, state, edge, w_rate, w_entry, vecs,
                    branch_low, rec_low, g_small,
                    sgrad, acum, bcum, conv_h, conv_l, rb_h, rb_l, eb_h, eb_l, tot, gath, halo, prevx, slow, bw, rb):
    L, CH = rec.shape
    gconv = sgrad
    q = lax.axis_index("ctx")
    tail = None
    rows_dot(sgrad.at[pl.ds(0, L)], mid_low, w_out)
    for v in slow:
        v.ref()
    if g.Q > 1:
        tail = wire.copy(rec.at[pl.ds(L - 8, 8)], prevx, {"ctx": (q + 1) % g.Q})
        tail.start()
    sub = lax.broadcasted_iota(jnp.int32, (GROUP, 1), 0)
    chunks = L // ROWS

    def chunk(j, carry):
        ua, ub = carry
        r0 = (chunks - 1 - j) * ROWS
        gm = sgrad[pl.ds(r0, ROWS)]
        act, slope = gelu_both(branch[pl.ds(r0, ROWS)])
        branch_low[pl.ds(r0, ROWS)] = (gm * state[pl.ds(r0, ROWS)] * slope).astype(BF16)
        sg = gm * act
        sgrad[pl.ds(r0, ROWS)] = sg
        dec = jnp.exp(-DECAY_SCALE * rate[pl.ds(r0, ROWS)] * vecs[SOFT : SOFT + 1])
        sg = dec * sg
        for n in reversed(range(ROWS // GROUP)):
            A = dec[n * GROUP : (n + 1) * GROUP]
            B = sg[n * GROUP : (n + 1) * GROUP]
            for step in (1, 2, 4):
                keep = sub < GROUP - step
                As = jnp.where(keep, row_shift(A, -step), 1.0)
                Bs = jnp.where(keep, row_shift(B, -step), 0.0)
                B = B + A * Bs
                A = A * As
            B = B + A * ub
            A = A * ua
            acum[pl.ds(r0 + n * GROUP, GROUP)] = A
            bcum[pl.ds(r0 + n * GROUP, GROUP)] = B
            ua = A[0:1]
            ub = B[0:1]
        return ua, ub

    yield
    ua, ub = jnp.ones((1, CH), F32), jnp.zeros((1, CH), F32)
    for i in range(chunks):
        ua, ub = chunk(i, (ua, ub))
        yield
    tot[0:1] = ua
    tot[1:2] = ub
    arriving = jnp.zeros((1, CH), F32)
    if g.Q > 1:
        swap = swap_edges(g, wire, tot, gath)
        next(swap)
        for _ in range(3):
            yield
        run(swap)
        for d in reversed(range(1, g.Q)):
            new = gath[d, 0:1] * arriving + gath[d, 1:2]
            arriving = jnp.where(d > q, new, arriving)
        tail.wait()
    acum[L:] = jnp.ones((8, CH), F32)
    bcum[L:] = jnp.zeros((8, CH), F32)
    zero = jnp.zeros((1, CH), F32)
    if g.Q > 1:
        prev_rows = jnp.where(q > 0, prevx[...], 0.0)
    else:
        prev_rows = jnp.zeros((8, CH), F32)

    def back(i, carry):
        gdec, gbr, gbe, gshift, gt0, gt1, gt2, gt3, last_state, last_rec = carry
        r0 = i * ROWS
        aw = row_shift(acum[pl.ds(r0, ROWS + 8)], -1)[:ROWS]
        bw = row_shift(bcum[pl.ds(r0, ROWS + 8)], -1)[:ROWS]
        car = sgrad[pl.ds(r0, ROWS)] + bw + aw * arriving
        st = state[pl.ds(r0, ROWS)]
        prev = row_shift(jnp.concatenate([last_state, st], axis=0), 1)[8:]
        gr = rate[pl.ds(r0, ROWS)]
        ge = entry[pl.ds(r0, ROWS)]
        c = conv[pl.ds(r0, ROWS)]
        soft = vecs[SOFT : SOFT + 1]
        log = -DECAY_SCALE * gr * soft
        dec = jnp.exp(log)
        scale = jnp.sqrt(minus_expm1(2.0 * log))
        ec = ge * c
        glog = car * prev * dec - car * ec * dec * dec / scale
        glr = 8.0 * glog * gr
        gdec = gdec + jnp.sum(glr, axis=0, keepdims=True)
        rb = -glr * soft * (1.0 - gr)
        cs = car * scale
        eb = cs * ec * (1.0 - ge)
        gbr = gbr + jnp.sum(rb, axis=0, keepdims=True)
        gbe = gbe + jnp.sum(eb, axis=0, keepdims=True)
        rh, rl = halves(rb)
        eh, el = halves(eb)
        ch, cl = halves(c)
        rb_h[pl.ds(r0, ROWS)] = rh
        rb_l[pl.ds(r0, ROWS)] = rl
        eb_h[pl.ds(r0, ROWS)] = eh
        eb_l[pl.ds(r0, ROWS)] = el
        conv_h[pl.ds(r0, ROWS)] = ch
        conv_l[pl.ds(r0, ROWS)] = cl
        wr, we = w_rate[...], w_entry[...]
        gc = cs * ge + dot_rows(rh, wr) + dot_rows(rl, wr) + dot_rows(eh, we) + dot_rows(el, we)
        gconv[pl.ds(r0, ROWS)] = gc
        gshift = gshift + jnp.sum(gc, axis=0, keepdims=True)
        x = rec[pl.ds(r0, ROWS)]
        wide = jnp.concatenate([last_rec, x], axis=0)
        gts = [gt0, gt1, gt2, gt3]
        for k in range(4):
            xk = x if k == 0 else row_shift(wide, k)[8:]
            gts[k] = gts[k] + jnp.sum(gc * xk, axis=0, keepdims=True)
        return (gdec, gbr, gbe, gshift, *gts, st[ROWS - 8 :], x[ROWS - 8 :])

    yield
    carry = (zero,) * 8 + (edge[...], prev_rows)
    for i in range(chunks):
        carry = back(i, carry)
        yield
    gdec, gbr, gbe, gshift, gt0, gt1, gt2, gt3 = carry[:8]
    if g.Q > 1:
        cp = wire.copy(gconv.at[pl.ds(0, 8)], halo, {"ctx": (q + g.Q - 1) % g.Q})
        cp.start()
    gdec = gdec * vecs[SLOPE : SLOPE + 1]
    srows = small_rows(rb)
    for k, v in enumerate((gt0, gt1, gt2, gt3, gshift, gbr, gbe, gdec)):
        tot[k : k + 1] = v
    for j in range(bw // rb):
        g_small[j * srows + 2 * rb : j * srows + 2 * rb + 8] = tot[...]
        g_small[j * srows + 2 * rb + 8 : (j + 1) * srows] = jnp.zeros((srows - 2 * rb - 8, CH), F32)
    yield

    def product(h, l):
        return dot_tokens(conv_h[...], h[...]) + dot_tokens(conv_l[...], h[...]) + dot_tokens(conv_h[...], l[...])

    head = lax.broadcasted_iota(jnp.int32, (bw, CH), 1) // bw

    def diagonal(dense):
        total = jnp.zeros((bw, CH), F32)
        for h in range(CH // bw):
            total = total + jnp.where(head == h, dense[h * bw : (h + 1) * bw], 0.0)
        return total

    for off, (h, l) in ((0, (rb_h, rb_l)), (rb, (eb_h, eb_l))):
        block = diagonal(product(h, l))
        for j in range(bw // rb):
            g_small[j * srows + off : j * srows + off + rb] = block[j * rb : (j + 1) * rb]
        yield
    if g.Q > 1:
        cp.wait()
        gconv[L:] = jnp.where(q < g.Q - 1, halo[...], 0.0)
    else:
        gconv[L:] = jnp.zeros((8, CH), F32)

    def last(i, _):
        r0 = pl.multiple_of(i * ROWS, ROWS)
        wide = gconv[pl.ds(r0, ROWS + 8)]
        total = vecs[TAPS : TAPS + 1] * wide[:ROWS]
        for k in range(1, 4):
            total = total + vecs[TAPS + k : TAPS + k + 1] * row_shift(wide, -k)[:ROWS]
        rec_low[pl.ds(r0, ROWS)] = total.astype(BF16)
        return 0

    lax.fori_loop(0, chunks, last, 0)
    yield


def back_call(g, mid_low, w_out, branch, rec, conv, rate, entry, state, edge, w_rate, w_entry, vecs, bw, rb, middle,
              cot, live, hidden, w_down, mixed, cid):
    L, CH = rec.shape
    half, width = middle.shape
    low = jax.ShapeDtypeStruct((L, CH), BF16)
    F = hidden.shape[1]
    rows = width // g.N
    count = g.Q + 2 + tp_count(g, L) + 2 * reduce_count(g)
    operands = [mid_low, w_out, branch, rec, conv, rate, entry, state, edge, w_rate, w_entry, vecs,
                middle, cot, live, hidden, w_down, mixed]

    def kernel(*refs):
        ins, (middle, cot, live, hidden, w_down, mixed) = refs[:12], refs[12:18]
        slow = [v for v in ins if isinstance(v, Later)]
        outs, (output, g_down, g_out) = refs[18:21], refs[21:24]
        bufs = refs[24:37]
        cot_t, term, sendbuf, recvbuf, *more = refs[37:]
        mid_t = cot_t
        send, recv = more[-2:]
        greet(ctx_peers(g) + tp_peers(g) + plane_peers(g))
        wire = Wire(send, recv)
        ins = [v.dst if isinstance(v, Later) else v for v in ins]

        def z():
            yield
            body = mlp_out_body((hidden.ref(), w_down.ref(), middle, live), (output,))
            yield from tp_steps(g, wire, L, output, *body, (term, sendbuf, recvbuf))

        def down():
            yield from turn_steps(rows, cot_t, cot, live)
            hidden.ref()
            yield from reduce_steps(g, wire, [(product_term(cot.dst, cot_t, hidden.dst, rows, live), g_down, more[0:3])])

        down_steps = down()
        if needs_turn(rows):
            for _ in range(len(range(0, width, 512)) + g.C * g.A * g.B):
                next(down_steps)

        def out():
            yield from turn_steps(rows, mid_t, ins[0])
            mixed.ref()
            yield from reduce_steps(g, wire, [(product_term(ins[0], mid_t, mixed.dst, rows), g_out, more[3:6])])

        braid(
            chain(backward_steps(g, wire, *ins, *outs, *bufs, slow, bw, rb), iter(range(4))),
            (z(), BACK_Z),
            (down_steps, BACK_DOWN),
            (out(), BACK_OUT),
        )

    return call(
        kernel,
        operands,
        [low, low, jax.ShapeDtypeStruct((bw // rb * small_rows(rb), CH), F32), jax.ShapeDtypeStruct((L, width), BF16),
         jax.ShapeDtypeStruct((rows, F), F32), jax.ShapeDtypeStruct((rows, CH), F32)],
        [
            pltpu.VMEM((L + 8, CH), F32),
            pltpu.VMEM((L + 8, CH), F32),
            pltpu.VMEM((L + 8, CH), F32),
        ]
        + [pltpu.VMEM((L, CH), BF16)] * 6
        + [
            pltpu.VMEM((8, CH), F32),
            pltpu.VMEM((g.Q, 8, CH), F32),
            pltpu.VMEM((8, CH), F32),
            pltpu.VMEM((8, CH), F32),
        ]
        + turn_scratch(rows, width, L)
        + tp_bufs(g, L, width)
        + reduce_bufs(g, rows, F)
        + reduce_bufs(g, rows, CH)
        + sems(count),
        cid,
        "rec_backward",
        later=(15, 16, 13, 17, 3, 4, 6),
    )


def reduce_count(g):
    ring = 0
    for nf, ng in ((g.A, g.B), (g.B, g.A)):
        ring += (nf - 1) * ng + (ng - 1)
    return ring + (g.C - 1) * g.A * g.B


def reduce_bufs(g, rows, width):
    nb = g.A * g.B
    arrivals = reduce_count(g) - (g.C - 1) * nb
    return [
        pltpu.VMEM((nb, rows, width), BF16),
        pltpu.VMEM((nb, rows, width), BF16),
        pltpu.VMEM((max(1, arrivals), rows // 2, width), BF16),
    ]


def reduce_steps(g, wire, items):
    a, b, c = g.me()
    sends = []

    def start(src, dst, dev):
        cp = wire.copy(src, dst, dev)
        cp.start()
        sends.append(cp)
        return cp

    nb = g.A * g.B

    def owner(k, core):
        return g.block((a + g.A - k // g.B) % g.A, (b + g.B - k % g.B) % g.B, core)

    def each_tile(width, fn):
        fn(slice(None))

    rings = [(g.A, g.B), (g.B, g.A)]
    devs = [
        (g.dev((a + 1) % g.A, b, c), g.dev(a, (b + 1) % g.B, c)),
        (g.dev(a, (b + 1) % g.B, c), g.dev((a + 1) % g.A, b, c)),
    ]

    def slot(h, df, dg):
        return df * g.B + dg if h == 0 else dg * g.B + df

    bases = []
    state = []
    for term, out, (to_sib, sums, land) in items:
        half = out.shape[0] // 2
        base = wire.used
        bases.append(base)
        if g.C == 2:
            wire.used += nb
            for k in [(i + 1) % nb for i in range(nb)]:

                def tile(cols):
                    to_sib[k, :, cols] = term(owner(k, 1 - c), cols).astype(BF16)

                each_tile(out.shape[1], tile)
                wire.at(base + k, to_sib.at[k], sums.at[k], g.dev(a, b, 1 - c)).start()
                yield
        used = 0
        first = ({}, {})
        for k in [(i + 1) % nb for i in range(nb)]:
            if g.C == 2:
                wire.at(base + k, to_sib.at[k], sums.at[k], g.dev(a, b, 1 - c)).wait_recv()

            def tile(cols):
                s = term(owner(k, c), cols)
                if g.C == 2:
                    s = s + sums[k, :, cols].astype(F32)
                if k == 0:
                    out[:, cols] = s
                else:
                    sums[k, :, cols] = s.astype(BF16)

            each_tile(out.shape[1], tile)
            for h in (0, 1):
                nf, ng = rings[h]
                df, dg = (k // g.B, k % g.B) if h == 0 else (k % g.B, k // g.B)
                if nf > 1 and df == 1:
                    first[h][dg] = (start(sums.at[k, pl.ds(h * half, half)], land.at[used], devs[h][0]), used)
                    used += 1
            yield
        state.append([first, used])

    def add(out, sums, k, h, half, arrived):
        at = slice(h * half, (h + 1) * half)
        if k == 0:
            out[at] = out[at] + arrived.astype(F32)
        else:
            sums[k, at] = (sums[k, at].astype(F32) + arrived.astype(F32)).astype(BF16)

    seconds = []
    for (term, out, (to_sib, sums, land)), st in zip(items, state):
        half = out.shape[0] // 2
        first, used = st
        second = [None, None]
        for h in (0, 1):
            nf, ng = rings[h]
            for i in range(1, nf):
                df = (i + 1) % nf
                for dg in [d % ng for d in range(1, ng + 1)]:
                    cp, at = first[h][dg]
                    cp.wait_recv()
                    k = slot(h, df, dg)
                    add(out, sums, k, h, half, land[at])
                    if i < nf - 1:
                        first[h][dg] = (start(sums.at[k, pl.ds(h * half, half)], land.at[used], devs[h][0]), used)
                        used += 1
                    elif dg == 1 and ng > 1:
                        second[h] = (start(sums.at[k, pl.ds(h * half, half)], land.at[used], devs[h][1]), used)
                        used += 1
            if nf == 1 and ng > 1:
                k = slot(h, 0, 1)
                second[h] = (start(sums.at[k, pl.ds(h * half, half)], land.at[used], devs[h][1]), used)
                used += 1
        seconds.append([second, used])
        yield
    for (term, out, (to_sib, sums, land)), (second, used) in zip(items, seconds):
        half = out.shape[0] // 2
        for h in (0, 1):
            nf, ng = rings[h]
            for j in range(1, ng):
                cp, at = second[h]
                cp.wait_recv()
                k = slot(h, 0, (j + 1) % ng)
                add(out, sums, k, h, half, land[at])
                if j < ng - 1:
                    second[h] = (start(sums.at[k, pl.ds(h * half, half)], land.at[used], devs[h][1]), used)
                    used += 1
        yield
    for cp in sends:
        cp.wait_send()
    if g.C == 2:
        for (term, out, (to_sib, sums, land)), base in zip(items, bases):
            for k in range(nb):
                wire.at(base + k, to_sib.at[k], sums.at[k], g.dev(a, b, 1 - c)).wait_send()


def needs_turn(rows):
    return rows % 128 != 0


def turn_scratch(rows, width, L):
    return [pltpu.VMEM((width, L) if needs_turn(rows) else (16, 128), BF16)]


def product_term(left, turned, right, rows, mask=None):
    def term(block, cols):
        at = pl.ds(pl.multiple_of(block * rows, rows), rows)
        if needs_turn(rows):
            return dot(turned[at], right[:, cols])
        v = left[:, at]
        if mask is not None:
            v = (v.astype(F32) * mask[...]).astype(BF16)
        return dot_tokens(v, right[:, cols])

    return term


def turn_steps(rows, turned, left, mask=None):
    if isinstance(left, Later):
        left = left.ref()
    if needs_turn(rows):
        yield from transpose_steps(turned, left, mask)


def given_term(part, rows):
    def term(block, cols):
        return part[pl.ds(pl.multiple_of(block * rows, rows), rows), cols]

    return term


def mlp_back_call(g, low_two, gate_low, up_low, w_gate, w_up, middle, cot, live, gain, cid):
    L, width = low_two.shape
    F = gate_low.shape[1]
    half = L // 2
    rows = width // g.N
    count = tp_count(g, L) + 2 * reduce_count(g)
    grad = jax.ShapeDtypeStruct((rows, F), F32)

    def kernel(low_two, gate_low, up_low, w_gate, w_up, middle, cot, live, gain,
               mid_low, grad_middle, grad_gain, g_gate, g_up,
               two_t, term, sendbuf, recvbuf, *refs):
        send, recv = refs[-2:]
        bufs = refs[:-2]
        greet(plane_peers(g) + tp_peers(g))
        wire = Wire(send, recv)
        gate_low, up_low, w_gate, w_up, middle, cot = (v.ref() for v in (gate_low, up_low, w_gate, w_up, middle, cot))
        back = mlp_back_body((gate_low, up_low, w_gate, w_up, middle, cot, live, gain), (mid_low, grad_middle, grad_gain))

        def gate():
            yield from turn_steps(rows, two_t, low_two)
            yield from reduce_steps(g, wire, [(product_term(low_two.dst, two_t, gate_low, rows), g_gate, bufs[0:3])])

        def up():
            yield from reduce_steps(g, wire, [(product_term(low_two.dst, two_t, up_low, rows), g_up, bufs[3:6])])

        braid(
            tp_steps(g, wire, L, mid_low, *back, (term, sendbuf, recvbuf)),
            (gate(), MLP_GATE),
            (up(), MLP_UP),
        )

    scratch = turn_scratch(rows, width, L) + tp_bufs(g, L, width)
    for _ in range(2):
        scratch += reduce_bufs(g, rows, F)
    return call(
        kernel,
        [low_two, gate_low, up_low, w_gate, w_up, middle, cot, live, gain],
        [jax.ShapeDtypeStruct((L, width), BF16), jax.ShapeDtypeStruct((half, width), F32),
         jax.ShapeDtypeStruct((1, width), F32), grad, grad],
        scratch + sems(count),
        cid,
        "mlp_back",
        later=(1, 3, 2, 4, 0, 5, 6),
    )


def plane_others(g):
    s, q = lax.axis_index("shard"), lax.axis_index("ctx")
    me = s * g.Q + q
    out = []
    for k in range(1, g.N):
        d = (me + k) % g.N
        out.append({"shard": d // g.Q, "ctx": d % g.Q})
    return me, out


def total_steps(g, wire, mine, land_t, land_p, out):
    t = lax.axis_index("tp")
    me, others = plane_others(g)
    land_t[t] = mine[...]
    cps = [wire.copy(mine, land_t.at[t], {"tp": (t + k) % g.T}) for k in range(1, g.T)]
    for cp in cps:
        cp.start()
    yield
    for cp in cps:
        cp.wait()
    total = land_t[0]
    for d in range(1, g.T):
        total = total + land_t[d]
    mine[...] = total
    land_p[me] = total
    cps = [wire.copy(mine, land_p.at[me], d) for d in others]
    for cp in cps:
        cp.start()
    yield
    for cp in cps:
        cp.wait()
    total = land_p[0]
    for d in range(1, g.N):
        total = total + land_p[d]
    out[...] = total


def rec_back_call(g, branch_low, rec_low, w_branch, w_rec, x, grad_middle, gain, part_two, low_one, small, cid):
    L, width = x.shape
    CH = branch_low.shape[1]
    rows = width // g.N
    srows = small.shape[0] // g.N
    shapes = [(rows, CH), (rows, CH), (srows, small.shape[1])]
    count = tp_count(g, L) + len(shapes) * reduce_count(g) + g.T + g.N

    def kernel(branch_low, rec_low, w_branch, w_rec, x, grad_middle, gain, part_two, low_one, small,
               input_grad, gains, g_branch, g_rec, g_small,
               part_one, one_t, both, land_t, land_p, term, sendbuf, recvbuf, *refs):
        send, recv = refs[-2:]
        bufs = refs[:-2]
        t = lax.axis_index("tp")
        greet(plane_others(g)[1] + [{"tp": (t + k) % g.T} for k in range(1, g.T)])
        wire = Wire(send, recv)
        branch_low, rec_low, w_branch, w_rec, x, grad_middle = (
            v.ref() for v in (branch_low, rec_low, w_branch, w_rec, x, grad_middle)
        )
        back = rec_back_body((branch_low, rec_low, w_branch, w_rec, x, grad_middle, gain), (input_grad, part_one))

        def one(term, out, bufs):
            yield from reduce_steps(g, wire, [(term, out, bufs)])

        def branch():
            yield from turn_steps(rows, one_t, low_one)
            yield from one(product_term(low_one.dst, one_t, branch_low, rows), g_branch, bufs[0:3])

        def main():
            steps = tp_steps(g, wire, L, input_grad, *back, (term, sendbuf, recvbuf))
            for _ in range(L // 2 // PIECE + END["take_far"]):
                next(steps)
                yield
            both[:, :width] = part_one[...]
            both[:, width:] = part_two[...]
            totals = total_steps(g, wire, both, land_t, land_p, gains)
            next(totals)
            for _ in steps:
                next(totals, None)
                yield
            run(totals)

        braid(
            main(),
            (branch(), REC_BRANCH),
            (one(product_term(low_one.dst, one_t, rec_low, rows), g_rec, bufs[3:6]), REC_REC),
            (one(given_term(small, srows), g_small, bufs[6:9]), REC_SMALL),
        )

    scratch = [pltpu.VMEM((1, width), F32)] + turn_scratch(rows, width, L)
    scratch += [pltpu.VMEM((1, 2 * width), F32), pltpu.VMEM((g.T, 1, 2 * width), F32), pltpu.VMEM((g.N, 1, 2 * width), F32)]
    scratch += tp_bufs(g, L, width)
    for s in shapes:
        scratch += reduce_bufs(g, *s)
    return call(
        kernel,
        [branch_low, rec_low, w_branch, w_rec, x, grad_middle, gain, part_two, low_one, small],
        [jax.ShapeDtypeStruct((L, width), BF16), jax.ShapeDtypeStruct((1, 2 * width), F32)]
        + [jax.ShapeDtypeStruct(s, F32) for s in shapes],
        scratch + sems(count),
        cid,
        "rec_back",
        later=(0, 2, 1, 3, 8, 4, 5),
    )


def settle(arrays):
    n = len(arrays)

    def kernel(*refs):
        ins, outs, kept, sem = refs[:n], refs[n : 2 * n], refs[2 * n : 3 * n], refs[3 * n]
        cps = [pltpu.make_async_copy(ins[k], kept[k], sem.at[k]) for k in range(n)]
        back = [pltpu.make_async_copy(kept[k], outs[k], sem.at[n + k]) for k in range(n)]
        for cp in cps:
            cp.start()
        for k in range(n):
            cps[k].wait()
            back[k].start()
        for cp in back:
            cp.wait()

    return pl.pallas_call(
        kernel,
        out_shape=[jax.ShapeDtypeStruct(v.shape, v.dtype) for v in arrays],
        in_specs=[ANY] * n,
        out_specs=[ANY] * n,
        scratch_shapes=[pltpu.VMEM(v.shape, v.dtype) for v in arrays] + [pltpu.SemaphoreType.DMA((2 * n,))],
        compiler_params=pltpu.CompilerParams(vmem_limit_bytes=VMEM_LIMIT),
        name="settle",
    )(*arrays)


def up_to(n, k):
    return -(-n // k) * k


def local(g, inputs, lengths, cotangent, norm1_gain, branch_weight, rec_in_weight, conv_weight, conv_bias,
          rgate_weight, rgate_bias, igate_weight, igate_bias, decay_param, out_weight, norm2_gain,
          mlp_gate_weight, mlp_up_weight, mlp_down_weight):
    slots, block_len, width = inputs.shape
    L = slots * block_len
    N = g.N
    heads, rb, bw = rgate_weight.shape
    ch = heads * bw
    taps = conv_weight.shape[0]
    prow = pack_rows(rb)[0]

    def across(v):
        return jnp.pad(v, ((0, 0), (0, ch - v.shape[1])))

    vectors = jnp.concatenate([conv_weight] + [p[None] for p in (conv_bias, rgate_bias, igate_bias, decay_param)], axis=0)
    gates, vectors, gains = lax.optimization_barrier(
        (jnp.stack([rgate_weight, igate_weight]), vectors, jnp.concatenate([norm1_gain, norm2_gain]))
    )
    pack = jnp.concatenate(
        [gates.transpose(0, 2, 1, 3).reshape(2 * rb, ch), across(vectors.reshape(2 * taps, -1)), across(gains.reshape(2, -1))],
        axis=0,
    )
    pack = jnp.pad(pack, ((0, prow - pack.shape[0]), (0, 0)))
    x_low = inputs.reshape(L, width)
    cot = cotangent.reshape(L, width)
    positions = lax.axis_index("ctx") * block_len + jnp.arange(block_len, dtype=jnp.int32)
    live = (positions[None, :] < lengths[:, None]).astype(F32).reshape(L, 1)
    (low_one, branch_pre, rec_pre, mixed, conv, rate, entry, state, edge, low_two, middle, w_rate, w_entry, vecs, gains,
     w_rec, w_branch, w_out, w_gate, w_up, w_down, gate_pre, up_pre, hidden) = front_call(
        g, pack, rec_in_weight, branch_weight, out_weight, [mlp_gate_weight, mlp_up_weight, mlp_down_weight], x_low, bw, rb, 0
    )
    gain_one, gain_two = gains[0:1], gains[1:2]
    act, slope = gelu_both(gate_pre)
    grad_low = (cot.astype(F32) * live).astype(BF16)
    grad_hidden = dot(grad_low, w_down)
    gate_low = (grad_hidden * up_pre * slope).astype(BF16)
    up_low = (grad_hidden * act).astype(BF16)
    mid_low, grad_middle, part_two, g_gate, g_up = mlp_back_call(
        g, low_two, gate_low, up_low, w_gate, w_up, middle, cot, live, gain_two, 2
    )
    branch_low, rec_low, flat, output, g_down, g_out = back_call(
        g, mid_low, w_out, branch_pre, rec_pre, conv, rate, entry, state, edge, w_rate, w_entry, vecs, bw, rb, middle,
        cot, live, hidden, w_down, mixed, 3
    )
    input_grad, gains, g_branch, g_rec, g_small = rec_back_call(
        g, branch_low, rec_low, w_branch, w_rec, x_low, grad_middle, gain_one, part_two, low_one, flat, 4
    )
    gains = lax.dynamic_slice(
        gains.reshape(2, N, -1), (0, lax.axis_index("shard") * g.Q + lax.axis_index("ctx"), 0), (2, 1, width // N)
    )[:, 0]
    me = lax.axis_index("shard") * g.Q + lax.axis_index("ctx")
    g_rate = g_small[:rb].reshape(rb, heads, bw).transpose(1, 0, 2)
    g_entry = g_small[rb : 2 * rb].reshape(rb, heads, bw).transpose(1, 0, 2)
    rest = lax.dynamic_slice(g_small[2 * rb : 2 * rb + 8].reshape(8, heads, bw), (0, 0, me * rb), (8, heads, rb))
    shape = (slots, block_len, width)
    output, input_grad, g_branch, g_rec, g_out, g_gate, g_up, g_down = settle(
        [output, input_grad, g_branch, g_rec, g_out, g_gate, g_up, g_down]
    )
    return (
        output.reshape(shape), input_grad.reshape(shape), gains[0], g_branch, g_rec, rest[:taps], rest[4],
        g_rate, rest[5], g_entry, rest[6], rest[7], g_out, gains[1], g_gate, g_up, g_down,
    )


def solution(mesh):
    plane = ("shard", "ctx")
    rows, cols = P(plane), P(plane, "tp")
    tok, gate, chan = P("shard", "ctx", None), P("tp", plane, None), P("tp", plane)
    taps = P(None, "tp", plane)
    params = (rows, cols, cols, taps, chan, gate, chan, gate, chan, chan, cols, rows, cols, cols, cols)
    return jax.shard_map(
        functools.partial(local, Grid(mesh)),
        mesh=mesh,
        in_specs=(tok, P("shard"), tok) + params,
        out_specs=(tok, tok) + params,
        check_vma=False,
    )
```

```python
import functools

import jax
import jax.numpy as jnp
from jax import lax
from jax.experimental import pallas as pl
from jax.experimental.pallas import tpu as pltpu
from jax.sharding import PartitionSpec as P

EPS = 1e-06
DECAY_SCALE = 8.0
F32 = jnp.float32
BF16 = jnp.bfloat16
MESH = pl.DeviceIdType.MESH
ANY = pl.BlockSpec(memory_space=pl.ANY)
VM = pl.BlockSpec(memory_space=pltpu.VMEM)
VMEM_LIMIT = 63 * 1024 * 1024


def dot(a, b):
    return jnp.dot(a, b, preferred_element_type=F32)


def dot_rows(a, b):
    return lax.dot_general(a, b, (((1,), (1,)), ((), ())), preferred_element_type=F32)


def dot_tokens(a, b):
    return lax.dot_general(a, b, (((0,), (0,)), ((), ())), preferred_element_type=F32)


def halves(v):
    hi = v.astype(BF16)
    return hi, (v - hi.astype(F32)).astype(BF16)


def gelu(v):
    return jax.nn.gelu(v)


def gelu_both(v):
    c = 0.7978845608028654
    th = jnp.tanh(c * (v + 0.044715 * v * v * v))
    half = 0.5 * (1.0 + th)
    return v * half, half + 0.5 * v * (1.0 - th * th) * c * (1.0 + 3 * 0.044715 * v * v)


def sigmoid(v):
    return 1.0 / (1.0 + jnp.exp(-v))


def minus_expm1(v):
    near = -v * (1.0 + v / 2 * (1.0 + v / 3 * (1.0 + v / 4 * (1.0 + v / 5 * (1.0 + v / 6)))))
    return jnp.where(v > -0.25, near, 1.0 - jnp.exp(v))


class Grid:
    def __init__(self, mesh):
        self.S, self.Q, self.T = (mesh.shape[n] for n in ("shard", "ctx", "tp"))
        dev = mesh.devices

        def chip(d):
            return tuple(getattr(d, "coords", None) or ())

        def paired(one, two):
            return bool(chip(one)) and chip(one) == chip(two)

        self.core_in = None
        if self.Q % 2 == 0 and paired(dev[0, 0, 0], dev[0, 1, 0]):
            self.core_in = "ctx"
        elif self.S % 2 == 0 and paired(dev[0, 0, 0], dev[1, 0, 0]):
            self.core_in = "shard"
        self.C = 1 if self.core_in is None else 2
        self.A = self.S // 2 if self.core_in == "shard" else self.S
        self.B = self.Q // 2 if self.core_in == "ctx" else self.Q
        self.N = self.S * self.Q

    def me(self):
        s, q = lax.axis_index("shard"), lax.axis_index("ctx")
        if self.core_in == "ctx":
            return s, q // 2, q % 2
        if self.core_in == "shard":
            return s // 2, q, s % 2
        return s, q, 0

    def shard_ctx(self, a, b, c):
        if self.core_in == "ctx":
            return a, b * 2 + c
        if self.core_in == "shard":
            return a * 2 + c, b
        return a, b

    def block(self, a, b, c):
        s, q = self.shard_ctx(a, b, c)
        return s * self.Q + q

    def dev(self, a, b, c):
        s, q = self.shard_ctx(a, b, c)
        return {"shard": s, "ctx": q}


class Wire:
    def __init__(self, send, recv, base=0):
        self.send, self.recv, self.used = send, recv, base

    def copy(self, src, dst, dev):
        self.used += 1
        return self.at(self.used - 1, src, dst, dev)

    def at(self, k, src, dst, dev):
        return pltpu.make_async_remote_copy(
            src_ref=src,
            dst_ref=dst,
            send_sem=self.send.at[k],
            recv_sem=self.recv.at[k],
            device_id=dev,
            device_id_type=MESH,
        )


def greet(devs):
    bar = pltpu.get_barrier_semaphore()
    for d in devs:
        pl.semaphore_signal(bar, inc=1, device_id=d, device_id_type=MESH)
    pl.semaphore_wait(bar, len(devs))


def ring_peers(size, at, place):
    if size == 1:
        return []
    if size == 2:
        return [place((at + 1) % 2)]
    return [place((at + 1) % size), place((at + size - 1) % size)]


def plane_peers(g):
    a, b, c = g.me()
    out = ring_peers(g.A, a, lambda k: g.dev(k, b, c))
    out += ring_peers(g.B, b, lambda k: g.dev(a, k, c))
    if g.C == 2:
        out.append(g.dev(a, b, 1 - c))
    return out


def braid(main, *sides):
    k = 0
    for _ in main:
        for steps, plan in sides:
            for _ in range(plan[k] if k < len(plan) else 0):
                next(steps, None)
        k += 1
    left = [s[0] for s in sides]
    while left:
        left = [s for s in left if next(s, left) is not left]


def only(steps, n):
    for _ in range(n):
        next(steps)
        yield


def at_steps(*pairs):
    plan = [0] * (1 + max(last for _, last, _ in pairs))
    for first, last, each in pairs:
        for k in range(first, last + 1):
            plan[k] += each
    return tuple(plan)


ALWAYS = (1,) * 64


def run(*steps):
    for s in steps:
        for _ in s:
            pass


class Later:
    def __init__(self, src, dst, sem):
        self.copy, self.dst, self.here = pltpu.make_async_copy(src, dst, sem), dst, False
        self.copy.start()

    def ref(self):
        if not self.here:
            self.copy.wait()
            self.here = True
        return self.dst


def call(kernel, operands, out_shape, scratch, cid, name, in_specs=None, out_specs=None, later=(), early=()):
    in_specs = list(in_specs or [VM] * len(operands))
    out_specs = list(out_specs or [VM] * len(out_shape))
    for k in later:
        in_specs[k] = ANY
    for k in early:
        out_specs[k] = ANY
    n, m = len(later), len(early)
    n_in = len(operands)

    def body(*refs):
        refs = list(refs)
        if m:
            kept, sem = refs[-m - 1 : -1], refs[-1]
            refs = refs[: -m - 1]
            copies = {}
            for j, k in enumerate(early):
                copies[id(kept[j])] = pltpu.make_async_copy(kept[j], refs[n_in + k], sem.at[j])
                refs[n_in + k] = kept[j]
        if n:
            held, sem_in = refs[-n - 1 : -1], refs[-1]
            refs = refs[: -n - 1]
            for j, k in enumerate(later):
                refs[k] = Later(refs[k], held[j], sem_in.at[j])
        if not m:
            kernel(*refs)
            return
        kernel(*refs, send_out=lambda *which: [copies[id(r)].start() for r in which])
        for cp in copies.values():
            cp.wait()

    extra = [pltpu.VMEM(operands[k].shape, operands[k].dtype) for k in later]
    if n:
        extra.append(pltpu.SemaphoreType.DMA((n,)))
    extra += [pltpu.VMEM(out_shape[k].shape, out_shape[k].dtype) for k in early]
    if m:
        extra.append(pltpu.SemaphoreType.DMA((m,)))
    return pl.pallas_call(
        body,
        out_shape=out_shape,
        in_specs=in_specs,
        out_specs=out_specs,
        scratch_shapes=list(scratch) + extra,
        compiler_params=pltpu.CompilerParams(
            collective_id=cid, has_side_effects=True, vmem_limit_bytes=VMEM_LIMIT
        ),
        name=name,
    )(*operands)


def sems(n):
    return [pltpu.SemaphoreType.DMA((max(1, n),)), pltpu.SemaphoreType.DMA((max(1, n),))]


def gather_count(g):
    ring = 0
    for nf, ng in ((g.A, g.B), (g.B, g.A)):
        ring += (nf - 1) + (ng - 1) * nf
    return ring + (g.C - 1) * (1 + ring)


def gather_steps(g, wire, here, srcs, dsts):
    a, b, c = g.me()
    sib = None if g.C == 1 else g.dev(a, b, 1 - c)
    sends, sib_copies = [], []

    def ring(h):
        if h == 0:
            return g.A, a, (lambda k: g.dev(k, b, c)), g.B, b, (lambda k: g.dev(a, k, c)), (lambda f, s: g.block(f, s, c))
        return g.B, b, (lambda k: g.dev(a, k, c)), g.A, a, (lambda k: g.dev(k, b, c)), (lambda f, s: g.block(s, f, c))

    def start(src, dst, dev):
        cp = wire.copy(src, dst, dev)
        cp.start()
        sends.append(cp)
        return cp

    def rows_of(dst, blk, h, rows):
        half = rows // 2
        return dst.at[pl.ds(pl.multiple_of(blk * rows + h * half, half), half)]

    state = []
    mine = g.block(a, b, c)
    local_copies = []
    for src, dst in zip(srcs, dsts):
        rows = src.shape[0]
        half = rows // 2
        cp = pltpu.make_async_copy(src, dst.at[pl.ds(pl.multiple_of(mine * rows, rows), rows)], here.at[len(local_copies)])
        cp.start()
        local_copies.append(cp)
        per = []
        for h in (0, 1):
            nf, f, fdev, ng, s, sdev, blk = ring(h)
            own = src.at[pl.ds(h * half, half)]
            land = rows_of(dst, mine, h, rows)
            first = start(own, land, fdev((f + 1) % nf)) if nf > 1 else None
            per.append([first, None, own, land])
        for h in (0, 1):
            nf, f, fdev, ng, s, sdev, blk = ring(h)
            _, _, own, land = per[h]
            second = {}
            if ng > 1:
                second[(0, 0)] = start(own, land, sdev((s + 1) % ng))
            per[h][1] = second
        if sib is not None:
            whole = dst.at[pl.ds(pl.multiple_of(mine * rows, rows), rows)]
            sib_copies.append(start(src, whole, sib))
        state.append(per)
        yield
    for (src, dst), per in zip(zip(srcs, dsts), state):
        rows = src.shape[0]
        for h in (0, 1):
            nf, f, fdev, ng, s, sdev, blk = ring(h)
            cp = per[h][0]
            for i in range(1, nf):
                cp.wait_recv()
                at = rows_of(dst, blk((f - i) % nf, s), h, rows)
                if i < nf - 1:
                    cp = start(at, at, fdev((f + 1) % nf))
                if ng > 1:
                    per[h][1][(0, i)] = start(at, at, sdev((s + 1) % ng))
                if sib is not None:
                    sib_copies.append(start(at, at, sib))
        yield
    for (src, dst), per in zip(zip(srcs, dsts), state):
        rows = src.shape[0]
        for h in (0, 1):
            nf, f, fdev, ng, s, sdev, blk = ring(h)
            second = per[h][1]
            for j in range(1, ng):
                for i in range(nf):
                    second[(j - 1, i)].wait_recv()
                    at = rows_of(dst, blk((f - i) % nf, (s - j) % ng), h, rows)
                    if j < ng - 1:
                        second[(j, i)] = start(at, at, sdev((s + 1) % ng))
                    if sib is not None:
                        sib_copies.append(start(at, at, sib))
        yield
    for cp in local_copies:
        cp.wait()
    for cp in sib_copies:
        cp.wait_recv()
    for cp in sends:
        cp.wait_send()


def tp_peers(g):
    t = lax.axis_index("tp")
    return ring_peers(g.T, t, lambda k: {"tp": k})


MIX_GATE = at_steps((6, 6, 1), (15, 15, 1))
MIX_UP = at_steps((11, 11, 1), (19, 19, 1))
MIX_DOWN = at_steps((11, 11, 1))
BACK_Z = ALWAYS
BACK_DOWN = at_steps((2, 2, 1), (4, 4, 1), (6, 6, 1), (8, 8, 1), (9, 10, 2), (17, 17, 1))
BACK_OUT = at_steps((11, 12, 2), (13, 16, 1), (21, 21, 1))
MLP_GATE = at_steps((0, 3, 2), (8, 8, 1), (14, 14, 1))
MLP_UP = at_steps((4, 7, 2), (14, 14, 1), (21, 21, 1))
REC_BRANCH = at_steps((0, 3, 2), (9, 9, 1), (17, 17, 1))
REC_REC = at_steps((4, 7, 2), (13, 13, 1), (19, 19, 1))
REC_SMALL = at_steps((8, 11, 2), (15, 15, 1), (20, 20, 1))
PIECE = 32
CHUNK = 256


def tp_count(g, rows):
    return 4 * (rows // 2 // PIECE)


def tp_place(g):
    t = lax.axis_index("tp")
    side = jnp.where(t >= (g.T + 1) // 2, 1, 0)
    return side, jnp.where(side == 1, g.T - 1 - t, t)


END = {"send_near": 0, "take_far": 8, "take_near": 14}
INNER = {"send_near": 0, "take_far": 3, "pass_far": 8, "take_near": 10}


def tp_steps(g, wire, rows, out, partial=None, finish=None, bufs=None, gather=True):
    T = g.T
    t = lax.axis_index("tp")
    half = rows // 2
    pieces = half // PIECE
    side, pos = tp_place(g)
    end, inner = pos == 0, pos > 0
    near, far = side, 1 - side
    away = {"tp": jnp.where(side == 1, t - 1, t + 1)}
    home = {"tp": jnp.where(side == 1, (t + 1) % T, (t + T - 1) % T)}
    k_rs = wire.used
    if partial is not None:
        wire.used += 2 * pieces
    k_ag = wire.used
    if gather:
        wire.used += 2 * pieces

    def row(d, p):
        return pl.multiple_of(half * (1 - d) + p * PIECE, PIECE)

    def rs(d, p, dev):
        return wire.at(k_rs + d * pieces + p, bufs[1].at[d, p], bufs[2].at[d, p], dev)

    def ag(d, p, dev):
        at = out.at[pl.ds(row(d, p), PIECE)]
        return wire.at(k_ag + d * pieces + p, at, at, dev)

    step = chunk_rows(g, rows, out.shape[1])
    per = step // PIECE

    def ready(d, p, which):
        term = bufs[0].at[which]
        if p % per == 0:
            partial(pl.multiple_of(half * (1 - d) + p * PIECE, step), step, term)
        return term.at[pl.ds(p % per * PIECE, PIECE)]

    def send_near(p, at_end):
        part = ready(near, p, 0)[...]
        if not at_end:
            rs(near, p, away).wait_recv()
            part = part + bufs[2][near, p].astype(F32)
        bufs[1][near, p] = part.astype(BF16)
        rs(near, p, away).start()

    def take_far(p, at_end):
        part = ready(far, p, 1)
        rs(far, p, home).wait_recv()
        total = part[...] + bufs[2][far, p].astype(F32)
        if not at_end:
            bufs[1][far, p] = total.astype(BF16)
            rs(far, p, home).start()
            return
        done = finish(total, p * PIECE, row(far, p), PIECE)
        if gather:
            out[pl.ds(row(far, p), PIECE)] = done
            ag(far, p, away).start()
        else:
            out[p * PIECE : (p + 1) * PIECE] = done

    def pass_far(p, at_end):
        ag(far, p, away).wait_recv()
        ag(far, p, away).start()

    def take_near(p, at_end):
        ag(near, p, home).wait_recv()
        if not at_end:
            ag(near, p, home).start()

    acts = {"send_near": send_near, "take_far": take_far, "pass_far": pass_far, "take_near": take_near}
    if partial is None:

        @pl.when(end)
        def _():
            for p in range(pieces):
                ag(far, p, away).start()

        acts = {"pass_far": pass_far, "take_near": take_near}
        yield
    elif not gather:
        acts = {"send_near": send_near, "take_far": take_far}

    def schedule(lates):
        lates = {k: v for k, v in lates.items() if k in acts}
        least = min(lates.values())
        return [(acts[k], v - least) for k, v in lates.items()]

    plans = [(end, True, schedule(END)), (inner, False, schedule(INNER))]
    for i in range(pieces + max(late for _, _, plan in plans for _, late in plan)):
        for where, at_end, plan in plans:

            @pl.when(where)
            def _():
                for act, late in plan:
                    if 0 <= i - late < pieces:
                        act(i - late, at_end)

        yield
    if partial is not None:
        for p in range(pieces):
            rs(near, p, away).wait_send()
    if gather:
        for p in range(pieces):
            ag(far, p, away).wait_send()

    @pl.when(inner)
    def _():
        for p in range(pieces):
            if partial is not None:
                rs(far, p, home).wait_send()
            if gather:
                ag(near, p, home).wait_send()


def chunk_rows(g, rows, width):
    return min(CHUNK // 4 if needs_turn(width // g.N) else CHUNK, rows // 2)


def tp_bufs(g, rows, width):
    pieces = rows // 2 // PIECE
    return [
        pltpu.VMEM((2, chunk_rows(g, rows, width), width), F32),
        pltpu.VMEM((2, pieces, PIECE, width), BF16),
        pltpu.VMEM((2, pieces, PIECE, width), BF16),
    ]


def transpose_steps(dst, src, scale=None):
    if isinstance(src, Later):
        src = src.ref()
    width = src.shape[1]
    part = 512
    assert width % part == 0

    for at in range(0, width, part):

        def body(j, _):
            c0 = pl.multiple_of(at + j * 128, 128)
            v = src[:, pl.ds(c0, 128)]
            if scale is not None:
                v = (v.astype(F32) * scale[...]).astype(BF16)
            dst[pl.ds(c0, 128), :] = v.T
            return 0

        lax.fori_loop(0, part // 128, body, 0)
        yield


def chain(*steps):
    for s in steps:
        yield from s


def tile_of(width):
    return 512 if width % 512 == 0 else width


def rows_product(term, at, n, pairs):
    width = term.shape[1]
    tile = tile_of(width)

    def body(j, _):
        c0 = pl.multiple_of(j * tile, tile)
        total = None
        for l, r in pairs:
            p = dot_rows(l[pl.ds(at, n)], r[pl.ds(c0, tile)])
            total = p if total is None else total + p
        term[:, pl.ds(c0, tile)] = total
        return 0

    lax.fori_loop(0, width // tile, body, 0)


def rows_dot(dst, left, right):
    step = 256 if left.shape[0] % 256 == 0 else left.shape[0]

    def body(i, _):
        r0 = pl.ds(pl.multiple_of(i * step, step), step)
        dst[r0] = dot(left[r0], right[...])
        return 0

    lax.fori_loop(0, left.shape[0] // step, body, 0)


def mean_square(v):
    return jnp.mean(v * v, axis=-1, keepdims=True)


def mix_out_body(ins, outs):
    mixed, w_out, x, gain = ins
    _, middle = outs

    def partial(at, n, term):
        rows_product(term, at, n, [(mixed, w_out)])

    def finish(total, near, at, n):
        m = x[pl.ds(at, n)].astype(F32) + total
        middle[near : near + n] = m
        return (m * lax.rsqrt(mean_square(m) + EPS) * gain[...]).astype(BF16)

    return partial, finish


def mlp_out_body(ins, outs):
    hidden, w_down, middle, live = ins

    def partial(at, n, term):
        rows_product(term, at, n, [(hidden, w_down)])

    def finish(total, near, at, n):
        return ((middle[near : near + n] + total) * live[pl.ds(at, n)]).astype(BF16)

    return partial, finish


def norm_back(grad_normed, rows, gain):
    inv = lax.rsqrt(mean_square(rows) + EPS)
    gg = grad_normed * gain
    back = inv * gg - rows * (inv * inv * inv) * jnp.mean(gg * rows, axis=-1, keepdims=True)
    return back, jnp.sum(grad_normed * rows * inv, axis=0, keepdims=True)


def mlp_back_body(ins, outs):
    gate_low, up_low, w_gate, w_up, middle, cot, live, gain = ins
    _, grad_middle, grad_gain = outs
    grad_gain[...] = jnp.zeros_like(grad_gain)

    def partial(at, n, term):
        rows_product(term, at, n, [(gate_low, w_gate), (up_low, w_up)])

    def finish(total, near, at, n):
        back, gain_sum = norm_back(total, middle[near : near + n], gain[...])
        gm = cot[pl.ds(at, n)].astype(F32) * live[pl.ds(at, n)] + back
        grad_middle[near : near + n] = gm
        grad_gain[...] = grad_gain[...] + gain_sum
        return gm.astype(BF16)

    return partial, finish


def rec_back_body(ins, outs):
    branch_low, rec_low, w_branch, w_rec, x, grad_middle, gain = ins
    _, grad_gain = outs
    grad_gain[...] = jnp.zeros_like(grad_gain)

    def partial(at, n, term):
        rows_product(term, at, n, [(branch_low, w_branch), (rec_low, w_rec)])

    def finish(total, near, at, n):
        back, gain_sum = norm_back(total, x[pl.ds(at, n)].astype(F32), gain[...])
        grad_gain[...] = grad_gain[...] + gain_sum
        return (grad_middle[near : near + n] + back).astype(BF16)

    return partial, finish


TAPS, SHIFT, RBIAS, EBIAS, SOFT, SLOPE = 0, 4, 5, 6, 7, 8
ROWS = 64
GROUP = 8


def ctx_peers(g):
    q = lax.axis_index("ctx")
    return [{"ctx": (q + k) % g.Q} for k in range(1, g.Q)]


def swap_edges(g, wire, src, land):
    q = lax.axis_index("ctx")
    cps = []
    for k in range(1, g.Q):
        cp = wire.copy(src, land.at[q], {"ctx": (q + k) % g.Q})
        cp.start()
        cps.append(cp)
    yield
    for cp in cps:
        cp.wait_recv()
    for cp in cps:
        cp.wait_send()


def row_shift(v, n):
    return pltpu.roll(v, n % v.shape[0], 0)


def forward_steps(g, wire, branch, w_rate, w_entry, vecs, mixed, conv, rate, entry, state, edge,
                  ext, acum, bcum, tot, gath):
    L, CH = branch.shape
    q = lax.axis_index("ctx")
    sub = lax.broadcasted_iota(jnp.int32, (GROUP, 1), 0)

    def chunk(i, carry):
        ca, cb = carry
        r0 = i * ROWS
        wide = ext[pl.ds(r0, ROWS + 8)]
        c = vecs[SHIFT : SHIFT + 1] + vecs[TAPS : TAPS + 1] * wide[8:]
        for k in range(1, 4):
            c = c + vecs[TAPS + k : TAPS + k + 1] * row_shift(wide, k)[8:]
        conv[pl.ds(r0, ROWS)] = c
        hi, lo = halves(c)
        gr = sigmoid(dot(hi, w_rate[...]) + dot(lo, w_rate[...]) + vecs[RBIAS : RBIAS + 1])
        ge = sigmoid(dot(hi, w_entry[...]) + dot(lo, w_entry[...]) + vecs[EBIAS : EBIAS + 1])
        rate[pl.ds(r0, ROWS)] = gr
        entry[pl.ds(r0, ROWS)] = ge
        log = -DECAY_SCALE * gr * vecs[SOFT : SOFT + 1]
        dec = jnp.exp(log)
        drive = jnp.sqrt(minus_expm1(2.0 * log)) * ge * c
        for n in range(ROWS // GROUP):
            A = dec[n * GROUP : (n + 1) * GROUP]
            B = drive[n * GROUP : (n + 1) * GROUP]
            for step in (1, 2, 4):
                keep = sub >= step
                As = jnp.where(keep, row_shift(A, step), 1.0)
                Bs = jnp.where(keep, row_shift(B, step), 0.0)
                B = B + A * Bs
                A = A * As
            B = B + A * cb
            A = A * ca
            acum[pl.ds(r0 + n * GROUP, GROUP)] = A
            bcum[pl.ds(r0 + n * GROUP, GROUP)] = B
            ca = A[GROUP - 1 : GROUP]
            cb = B[GROUP - 1 : GROUP]
        return ca, cb

    ca, cb = jnp.ones((1, CH), F32), jnp.zeros((1, CH), F32)
    for i in range(L // ROWS):
        ca, cb = chunk(i, (ca, cb))
        yield
    tot[0:1] = ca
    tot[1:2] = cb
    start = jnp.zeros((1, CH), F32)
    if g.Q > 1:
        yield from swap_edges(g, wire, tot, gath)
        for d in range(g.Q - 1):
            new = gath[d, 0:1] * start + gath[d, 1:2]
            start = jnp.where(d < q, new, start)
    edge[...] = jnp.broadcast_to(start, (8, CH))
    yield

    def fix(i, _):
        r0 = pl.multiple_of(i * ROWS, ROWS)
        s = bcum[pl.ds(r0, ROWS)] + acum[pl.ds(r0, ROWS)] * start
        state[pl.ds(r0, ROWS)] = s
        mixed[pl.ds(r0, ROWS)] = (gelu_both(branch[pl.ds(r0, ROWS)])[0] * s).astype(BF16)
        return 0

    lax.fori_loop(0, L // ROWS, fix, 0)
    yield


def small_rows(rb):
    return up_to(2 * rb + 8, 32)


def pack_rows(rb):
    return up_to(2 * rb + 10, 32), 2 * rb, 2 * rb + 8


def iota2(shape):
    return lax.broadcasted_iota(jnp.int32, shape, 0), lax.broadcasted_iota(jnp.int32, shape, 1)


def log1p_small(e):
    return jnp.where(e < 0.02, e * (1.0 - e * (0.5 - e * (1.0 / 3 - e * 0.25))), jnp.log(1.0 + e))


def unpack(packs, bw, rb, rows, w_rate, w_entry, vecs, gains):
    total, CH = packs.shape
    n = bw // rb
    prow, o_vec, o_gain = pack_rows(rb)
    m, l = iota2((bw, total))
    _, lane = iota2((bw, CH))
    for dst, off in ((w_rate, 0), (w_entry, rb)):
        pick = jnp.logical_and(l // prow == m // rb, l % prow == m % rb + off)
        block = dot(jnp.where(pick, 1.0, 0.0).astype(BF16), packs[...])
        for h in range(CH // bw):
            dst[h * bw : (h + 1) * bw] = jnp.where(lane // bw == h, block, 0.0).astype(BF16)

    def rows_at(off):
        m, l = iota2((n * 8, total))
        pick = l == (m // 8) * prow + off + m % 8
        return dot(jnp.where(pick, 1.0, 0.0).astype(BF16), packs[...])

    short = rows_at(o_vec)[:, :128].astype(BF16)
    l, m = iota2((128, CH))
    spread = jnp.logical_and(l // rb == m // bw, l % rb == m % rb)
    wide = dot(short, jnp.where(spread, 1.0, 0.0).astype(BF16))
    _, lane = iota2((8, CH))
    vec = jnp.zeros((8, CH), F32)
    for j in range(n):
        vec = vec + jnp.where(lane % bw // rb == j, wide[j * 8 : (j + 1) * 8], 0.0)
    decay = vec[7:8]
    e = jnp.exp(-jnp.abs(decay))
    vecs[0:7] = vec[0:7]
    vecs[SOFT : SOFT + 1] = jnp.maximum(-decay, 0.0) + log1p_small(e)
    vecs[SLOPE : SLOPE + 1] = sigmoid(-decay)
    vecs[SLOPE + 1 :] = jnp.zeros((16 - SLOPE - 1, CH), F32)
    both = rows_at(o_gain)
    if rows % 128 == 0:
        for j in range(n):
            for u in range(2):
                gains[u : u + 1, j * rows : (j + 1) * rows] = both[j * 8 + u : j * 8 + u + 1, :rows]
    else:
        l, m = iota2((128, gains.shape[1]))
        row = jnp.zeros((8, gains.shape[1]), F32)
        for j in range(n):
            place = jnp.logical_and(l < rows, m == l + j * rows)
            row = row + dot(both[j * 8 : (j + 1) * 8, :128].astype(BF16), jnp.where(place, 1.0, 0.0).astype(BF16))
        gains[...] = row[:2]


def mlp_forward_steps(w_gate, w_up, low_two, gate_pre, up_pre, hidden, wg, wu, og, ou, oh, sem_in, sem_out):
    L, tile = og.shape[1], og.shape[2]
    nt = w_gate.shape[1] // tile

    def loads(j):
        cols = pl.ds(j * tile, tile)
        return [pltpu.make_async_copy(w.at[:, cols], b.at[j % 2], sem_in.at[j % 2, i]) for i, (w, b) in enumerate(((w_gate, wg), (w_up, wu)))]

    def stores(j):
        cols = pl.ds(j * tile, tile)
        return [pltpu.make_async_copy(b.at[j % 2], o.at[:, cols], sem_out.at[j % 2, i]) for i, (b, o) in enumerate(((og, gate_pre), (ou, up_pre), (oh, hidden)))]

    for cp in loads(0):
        cp.start()
    for j in range(nt):
        if j + 1 < nt:
            for cp in loads(j + 1):
                cp.start()
        for cp in loads(j):
            cp.wait()
        if j >= 2:
            for cp in stores(j - 2):
                cp.wait()
        gate, up, out = og.at[j % 2], ou.at[j % 2], oh.at[j % 2]
        rows_dot(gate, low_two, wg.at[j % 2])
        rows_dot(up, low_two, wu.at[j % 2])

        def act(i, _):
            r0 = pl.ds(pl.multiple_of(i * 32, 32), 32)
            out[r0] = (gelu_both(gate[r0])[0] * up[r0]).astype(BF16)
            return 0

        lax.fori_loop(0, L // 32, act, 0)
        for cp in stores(j):
            cp.start()
        yield
    for j in range(max(0, nt - 2), nt):
        for cp in stores(j):
            cp.wait()


def front_call(g, pack, rec_shard, branch_shard, out_shard, mlp_shards, x, bw, rb, cid):
    L, width = x.shape
    CH = pack.shape[1]
    half = L // 2
    n = len(mlp_shards)
    rows = out_shard.shape[0]
    wide = jax.ShapeDtypeStruct((L, CH), F32)
    dense = jax.ShapeDtypeStruct((CH, CH), BF16)

    def whole(s):
        return jax.ShapeDtypeStruct((g.N * s.shape[0], s.shape[1]), s.dtype)

    low = jax.ShapeDtypeStruct((L, width), BF16)
    outs = [low, wide, wide, jax.ShapeDtypeStruct((L, CH), BF16), wide, wide, wide, wide, jax.ShapeDtypeStruct((8, CH), F32),
            low, jax.ShapeDtypeStruct((half, width), F32), dense, dense, jax.ShapeDtypeStruct((16, CH), F32),
            jax.ShapeDtypeStruct((2, width), F32), whole(rec_shard), whole(branch_shard), whole(out_shard)]
    outs += [whole(s) for s in mlp_shards]
    F = mlp_shards[0].shape[1]
    tile = tile_of(F)
    outs += [jax.ShapeDtypeStruct((L, F), F32), jax.ShapeDtypeStruct((L, F), F32), jax.ShapeDtypeStruct((L, F), BF16)]
    count = 2 * g.Q + tp_count(g, L) + (n + 4) * gather_count(g)

    def kernel(pack, rec_shard, branch_shard, out_shard, *refs, send_out):
        shards, x = refs[:n], refs[n]
        (low_one, branch, rec, mixed, conv, rate, entry, state, edge, low_two, middle, w_rate, w_entry, vecs, gains,
         w_rec, w_branch, w_out) = refs[n + 1 : n + 19]
        full = refs[n + 19 : 2 * n + 19]
        made = refs[2 * n + 19 : 2 * n + 22]
        (packs, x_edge, a_edge, ext, acum, bcum, tot, gath, term, sendbuf, recvbuf, send, recv, here, *tiles) = refs[2 * n + 22 :]
        q = lax.axis_index("ctx")
        greet(ctx_peers(g) + plane_peers(g) + tp_peers(g))
        wire = Wire(send, recv)
        slots = iter(range(n + 4))

        def gather(srcs, dsts):
            at = [next(slots) for _ in srcs]
            return gather_steps(g, wire, here.at[pl.ds(at[0], len(at))], srcs, dsts)

        small = gather([pack], [packs])
        next(small)
        edge_copy = None
        if g.Q > 1:
            edge_copy = wire.copy(x.at[pl.ds(L - 16, 16)], x_edge, {"ctx": (q + 1) % g.Q})
            edge_copy.start()
        of_rec = gather([rec_shard], [w_rec])
        of_branch = gather([branch_shard], [w_branch])
        of_out = gather([out_shard], [w_out])
        of_gate, of_up, of_down = (gather([s], [d]) for s, d in zip(shards, full))
        next(of_rec)
        next(of_branch)
        run(small)
        unpack(packs, bw, rb, rows, w_rate, w_entry, vecs, gains)

        def norm_rows(i, _):
            r0 = pl.ds(pl.multiple_of(i * ROWS, ROWS), ROWS)
            v = x[r0].astype(F32)
            low_one[r0] = (v * lax.rsqrt(mean_square(v) + EPS) * gains[0:1]).astype(BF16)
            return 0

        lax.fori_loop(0, L // ROWS, norm_rows, 0)
        next(of_rec)
        next(of_branch)
        next(of_out)
        next(of_rec)
        next(of_branch)
        if g.Q > 1:
            edge_copy.wait()
            v = x_edge[...].astype(F32)
            a_edge[...] = (v * lax.rsqrt(mean_square(v) + EPS) * gains[0:1]).astype(BF16)
        run(of_rec)
        rows_dot(rec, low_one, w_rec)
        ext[8:] = rec[...]
        if g.Q > 1:
            ext[0:8] = jnp.where(q > 0, dot(a_edge[...], w_rec[...])[8:], 0.0)
        else:
            ext[0:8] = jnp.zeros((8, CH), F32)
        fwd = forward_steps(g, wire, branch, w_rate, w_entry, vecs, mixed, conv, rate, entry, state, edge,
                            ext, acum, bcum, tot, gath)
        for k in range(L // ROWS):
            next(fwd)
            if k == 2:
                next(of_out)
            if k == 6:
                next(of_out)
        if g.Q > 1:
            next(fwd)
        next(of_gate)
        next(of_up)
        run(of_branch)
        rows_dot(branch, low_one, w_branch)
        send_out(low_one, rec, conv, rate, entry, w_rate, w_entry, w_rec, w_branch, branch)
        run(fwd, of_out)
        send_out(mixed, state, w_out)
        partial, finish = mix_out_body((mixed, w_out, x, gains.at[pl.ds(1, 1)]), (low_two, middle))
        braid(
            tp_steps(g, wire, L, low_two, partial, finish, (term, sendbuf, recvbuf)),
            (of_gate, MIX_GATE),
            (of_up, MIX_UP),
            (only(of_down, 1), MIX_DOWN),
        )
        for _ in mlp_forward_steps(full[0], full[1], low_two, *made, *tiles):
            next(of_down, None)
        run(of_down)

    return call(
        kernel,
        [pack, rec_shard, branch_shard, out_shard, *mlp_shards, x],
        outs,
        [
            pltpu.VMEM((g.N * pack.shape[0], CH), BF16),
            pltpu.VMEM((16, width), BF16),
            pltpu.VMEM((16, width), BF16),
            pltpu.VMEM((L + 8, CH), F32),
            pltpu.VMEM((L, CH), F32),
            pltpu.VMEM((L, CH), F32),
            pltpu.VMEM((8, CH), F32),
            pltpu.VMEM((g.Q, 8, CH), F32),
        ]
        + tp_bufs(g, L, width)
        + sems(count)
        + [pltpu.SemaphoreType.DMA((n + 4,))]
        + [pltpu.VMEM((2, width, tile), BF16)] * 2
        + [pltpu.VMEM((2, L, tile), F32)] * 2
        + [pltpu.VMEM((2, L, tile), BF16), pltpu.SemaphoreType.DMA((2, 2)), pltpu.SemaphoreType.DMA((2, 3))],
        cid,
        "front",
        [VM] * (n + 5),
        [VM] * 18 + [ANY] * (n + 3),
        early=(0, 1, 2, 3, 4, 5, 6, 7, 11, 12, 15, 16, 17),
    )


def backward_steps(g, wire, mid_low, w_out, branch, rec, conv, rate, entry, state, edge, w_rate, w_entry, vecs,
                    branch_low, rec_low, g_small,
                    sgrad, acum, bcum, conv_h, conv_l, rb_h, rb_l, eb_h, eb_l, tot, gath, halo, prevx, slow, bw, rb):
    L, CH = rec.shape
    gconv = sgrad
    q = lax.axis_index("ctx")
    tail = None
    rows_dot(sgrad.at[pl.ds(0, L)], mid_low, w_out)
    for v in slow:
        v.ref()
    if g.Q > 1:
        tail = wire.copy(rec.at[pl.ds(L - 8, 8)], prevx, {"ctx": (q + 1) % g.Q})
        tail.start()
    sub = lax.broadcasted_iota(jnp.int32, (GROUP, 1), 0)
    chunks = L // ROWS

    def chunk(j, carry):
        ua, ub = carry
        r0 = (chunks - 1 - j) * ROWS
        gm = sgrad[pl.ds(r0, ROWS)]
        act, slope = gelu_both(branch[pl.ds(r0, ROWS)])
        branch_low[pl.ds(r0, ROWS)] = (gm * state[pl.ds(r0, ROWS)] * slope).astype(BF16)
        sg = gm * act
        sgrad[pl.ds(r0, ROWS)] = sg
        dec = jnp.exp(-DECAY_SCALE * rate[pl.ds(r0, ROWS)] * vecs[SOFT : SOFT + 1])
        sg = dec * sg
        for n in reversed(range(ROWS // GROUP)):
            A = dec[n * GROUP : (n + 1) * GROUP]
            B = sg[n * GROUP : (n + 1) * GROUP]
            for step in (1, 2, 4):
                keep = sub < GROUP - step
                As = jnp.where(keep, row_shift(A, -step), 1.0)
                Bs = jnp.where(keep, row_shift(B, -step), 0.0)
                B = B + A * Bs
                A = A * As
            B = B + A * ub
            A = A * ua
            acum[pl.ds(r0 + n * GROUP, GROUP)] = A
            bcum[pl.ds(r0 + n * GROUP, GROUP)] = B
            ua = A[0:1]
            ub = B[0:1]
        return ua, ub

    yield
    ua, ub = jnp.ones((1, CH), F32), jnp.zeros((1, CH), F32)
    for i in range(chunks):
        ua, ub = chunk(i, (ua, ub))
        yield
    tot[0:1] = ua
    tot[1:2] = ub
    arriving = jnp.zeros((1, CH), F32)
    if g.Q > 1:
        swap = swap_edges(g, wire, tot, gath)
        next(swap)
        for _ in range(3):
            yield
        run(swap)
        for d in reversed(range(1, g.Q)):
            new = gath[d, 0:1] * arriving + gath[d, 1:2]
            arriving = jnp.where(d > q, new, arriving)
        tail.wait()
    acum[L:] = jnp.ones((8, CH), F32)
    bcum[L:] = jnp.zeros((8, CH), F32)
    zero = jnp.zeros((1, CH), F32)
    if g.Q > 1:
        prev_rows = jnp.where(q > 0, prevx[...], 0.0)
    else:
        prev_rows = jnp.zeros((8, CH), F32)

    def back(i, carry):
        gdec, gbr, gbe, gshift, gt0, gt1, gt2, gt3, last_state, last_rec = carry
        r0 = i * ROWS
        aw = row_shift(acum[pl.ds(r0, ROWS + 8)], -1)[:ROWS]
        bw = row_shift(bcum[pl.ds(r0, ROWS + 8)], -1)[:ROWS]
        car = sgrad[pl.ds(r0, ROWS)] + bw + aw * arriving
        st = state[pl.ds(r0, ROWS)]
        prev = row_shift(jnp.concatenate([last_state, st], axis=0), 1)[8:]
        gr = rate[pl.ds(r0, ROWS)]
        ge = entry[pl.ds(r0, ROWS)]
        c = conv[pl.ds(r0, ROWS)]
        soft = vecs[SOFT : SOFT + 1]
        log = -DECAY_SCALE * gr * soft
        dec = jnp.exp(log)
        scale = jnp.sqrt(minus_expm1(2.0 * log))
        ec = ge * c
        glog = car * prev * dec - car * ec * dec * dec / scale
        glr = 8.0 * glog * gr
        gdec = gdec + jnp.sum(glr, axis=0, keepdims=True)
        rb = -glr * soft * (1.0 - gr)
        cs = car * scale
        eb = cs * ec * (1.0 - ge)
        gbr = gbr + jnp.sum(rb, axis=0, keepdims=True)
        gbe = gbe + jnp.sum(eb, axis=0, keepdims=True)
        rh, rl = halves(rb)
        eh, el = halves(eb)
        ch, cl = halves(c)
        rb_h[pl.ds(r0, ROWS)] = rh
        rb_l[pl.ds(r0, ROWS)] = rl
        eb_h[pl.ds(r0, ROWS)] = eh
        eb_l[pl.ds(r0, ROWS)] = el
        conv_h[pl.ds(r0, ROWS)] = ch
        conv_l[pl.ds(r0, ROWS)] = cl
        wr, we = w_rate[...], w_entry[...]
        gc = cs * ge + dot_rows(rh, wr) + dot_rows(rl, wr) + dot_rows(eh, we) + dot_rows(el, we)
        gconv[pl.ds(r0, ROWS)] = gc
        gshift = gshift + jnp.sum(gc, axis=0, keepdims=True)
        x = rec[pl.ds(r0, ROWS)]
        wide = jnp.concatenate([last_rec, x], axis=0)
        gts = [gt0, gt1, gt2, gt3]
        for k in range(4):
            xk = x if k == 0 else row_shift(wide, k)[8:]
            gts[k] = gts[k] + jnp.sum(gc * xk, axis=0, keepdims=True)
        return (gdec, gbr, gbe, gshift, *gts, st[ROWS - 8 :], x[ROWS - 8 :])

    yield
    carry = (zero,) * 8 + (edge[...], prev_rows)
    for i in range(chunks):
        carry = back(i, carry)
        yield
    gdec, gbr, gbe, gshift, gt0, gt1, gt2, gt3 = carry[:8]
    if g.Q > 1:
        cp = wire.copy(gconv.at[pl.ds(0, 8)], halo, {"ctx": (q + g.Q - 1) % g.Q})
        cp.start()
    gdec = gdec * vecs[SLOPE : SLOPE + 1]
    srows = small_rows(rb)
    for k, v in enumerate((gt0, gt1, gt2, gt3, gshift, gbr, gbe, gdec)):
        tot[k : k + 1] = v
    for j in range(bw // rb):
        g_small[j * srows + 2 * rb : j * srows + 2 * rb + 8] = tot[...]
        g_small[j * srows + 2 * rb + 8 : (j + 1) * srows] = jnp.zeros((srows - 2 * rb - 8, CH), F32)
    yield

    def product(h, l):
        return dot_tokens(conv_h[...], h[...]) + dot_tokens(conv_l[...], h[...]) + dot_tokens(conv_h[...], l[...])

    head = lax.broadcasted_iota(jnp.int32, (bw, CH), 1) // bw

    def diagonal(dense):
        total = jnp.zeros((bw, CH), F32)
        for h in range(CH // bw):
            total = total + jnp.where(head == h, dense[h * bw : (h + 1) * bw], 0.0)
        return total

    for off, (h, l) in ((0, (rb_h, rb_l)), (rb, (eb_h, eb_l))):
        block = diagonal(product(h, l))
        for j in range(bw // rb):
            g_small[j * srows + off : j * srows + off + rb] = block[j * rb : (j + 1) * rb]
        yield
    if g.Q > 1:
        cp.wait()
        gconv[L:] = jnp.where(q < g.Q - 1, halo[...], 0.0)
    else:
        gconv[L:] = jnp.zeros((8, CH), F32)

    def last(i, _):
        r0 = pl.multiple_of(i * ROWS, ROWS)
        wide = gconv[pl.ds(r0, ROWS + 8)]
        total = vecs[TAPS : TAPS + 1] * wide[:ROWS]
        for k in range(1, 4):
            total = total + vecs[TAPS + k : TAPS + k + 1] * row_shift(wide, -k)[:ROWS]
        rec_low[pl.ds(r0, ROWS)] = total.astype(BF16)
        return 0

    lax.fori_loop(0, chunks, last, 0)
    yield


def back_call(g, mid_low, w_out, branch, rec, conv, rate, entry, state, edge, w_rate, w_entry, vecs, bw, rb, middle,
              cot, live, hidden, w_down, mixed, cid):
    L, CH = rec.shape
    half, width = middle.shape
    low = jax.ShapeDtypeStruct((L, CH), BF16)
    F = hidden.shape[1]
    rows = width // g.N
    count = g.Q + 2 + tp_count(g, L) + 2 * reduce_count(g)
    operands = [mid_low, w_out, branch, rec, conv, rate, entry, state, edge, w_rate, w_entry, vecs,
                middle, cot, live, hidden, w_down, mixed]

    def kernel(*refs):
        ins, (middle, cot, live, hidden, w_down, mixed) = refs[:12], refs[12:18]
        slow = [v for v in ins if isinstance(v, Later)]
        outs, (output, g_down, g_out) = refs[18:21], refs[21:24]
        bufs = refs[24:37]
        cot_t, term, sendbuf, recvbuf, *more = refs[37:]
        mid_t = cot_t
        send, recv = more[-2:]
        greet(ctx_peers(g) + tp_peers(g) + plane_peers(g))
        wire = Wire(send, recv)
        ins = [v.dst if isinstance(v, Later) else v for v in ins]

        def z():
            yield
            body = mlp_out_body((hidden.ref(), w_down.ref(), middle, live), (output,))
            yield from tp_steps(g, wire, L, output, *body, (term, sendbuf, recvbuf))

        def down():
            yield from turn_steps(rows, cot_t, cot, live)
            hidden.ref()
            yield from reduce_steps(g, wire, [(product_term(cot.dst, cot_t, hidden.dst, rows, live), g_down, more[0:3])])

        down_steps = down()
        if needs_turn(rows):
            for _ in range(len(range(0, width, 512)) + g.C * g.A * g.B):
                next(down_steps)

        def out():
            yield from turn_steps(rows, mid_t, ins[0])
            mixed.ref()
            yield from reduce_steps(g, wire, [(product_term(ins[0], mid_t, mixed.dst, rows), g_out, more[3:6])])

        braid(
            chain(backward_steps(g, wire, *ins, *outs, *bufs, slow, bw, rb), iter(range(4))),
            (z(), BACK_Z),
            (down_steps, BACK_DOWN),
            (out(), BACK_OUT),
        )

    return call(
        kernel,
        operands,
        [low, low, jax.ShapeDtypeStruct((bw // rb * small_rows(rb), CH), F32), jax.ShapeDtypeStruct((L, width), BF16),
         jax.ShapeDtypeStruct((rows, F), F32), jax.ShapeDtypeStruct((rows, CH), F32)],
        [
            pltpu.VMEM((L + 8, CH), F32),
            pltpu.VMEM((L + 8, CH), F32),
            pltpu.VMEM((L + 8, CH), F32),
        ]
        + [pltpu.VMEM((L, CH), BF16)] * 6
        + [
            pltpu.VMEM((8, CH), F32),
            pltpu.VMEM((g.Q, 8, CH), F32),
            pltpu.VMEM((8, CH), F32),
            pltpu.VMEM((8, CH), F32),
        ]
        + turn_scratch(rows, width, L)
        + tp_bufs(g, L, width)
        + reduce_bufs(g, rows, F)
        + reduce_bufs(g, rows, CH)
        + sems(count),
        cid,
        "rec_backward",
        later=(15, 16, 13, 17, 3, 4, 6),
    )


def reduce_count(g):
    ring = 0
    for nf, ng in ((g.A, g.B), (g.B, g.A)):
        ring += (nf - 1) * ng + (ng - 1)
    return ring + (g.C - 1) * g.A * g.B


def reduce_bufs(g, rows, width):
    nb = g.A * g.B
    arrivals = reduce_count(g) - (g.C - 1) * nb
    return [
        pltpu.VMEM((nb, rows, width), BF16),
        pltpu.VMEM((nb, rows, width), BF16),
        pltpu.VMEM((max(1, arrivals), rows // 2, width), BF16),
    ]


def reduce_steps(g, wire, items):
    a, b, c = g.me()
    sends = []

    def start(src, dst, dev):
        cp = wire.copy(src, dst, dev)
        cp.start()
        sends.append(cp)
        return cp

    nb = g.A * g.B

    def owner(k, core):
        return g.block((a + g.A - k // g.B) % g.A, (b + g.B - k % g.B) % g.B, core)

    def each_tile(width, fn):
        fn(slice(None))

    rings = [(g.A, g.B), (g.B, g.A)]
    devs = [
        (g.dev((a + 1) % g.A, b, c), g.dev(a, (b + 1) % g.B, c)),
        (g.dev(a, (b + 1) % g.B, c), g.dev((a + 1) % g.A, b, c)),
    ]

    def slot(h, df, dg):
        return df * g.B + dg if h == 0 else dg * g.B + df

    bases = []
    state = []
    for term, out, (to_sib, sums, land) in items:
        half = out.shape[0] // 2
        base = wire.used
        bases.append(base)
        if g.C == 2:
            wire.used += nb
            for k in [(i + 1) % nb for i in range(nb)]:

                def tile(cols):
                    to_sib[k, :, cols] = term(owner(k, 1 - c), cols).astype(BF16)

                each_tile(out.shape[1], tile)
                wire.at(base + k, to_sib.at[k], sums.at[k], g.dev(a, b, 1 - c)).start()
                yield
        used = 0
        first = ({}, {})
        for k in [(i + 1) % nb for i in range(nb)]:
            if g.C == 2:
                wire.at(base + k, to_sib.at[k], sums.at[k], g.dev(a, b, 1 - c)).wait_recv()

            def tile(cols):
                s = term(owner(k, c), cols)
                if g.C == 2:
                    s = s + sums[k, :, cols].astype(F32)
                if k == 0:
                    out[:, cols] = s
                else:
                    sums[k, :, cols] = s.astype(BF16)

            each_tile(out.shape[1], tile)
            for h in (0, 1):
                nf, ng = rings[h]
                df, dg = (k // g.B, k % g.B) if h == 0 else (k % g.B, k // g.B)
                if nf > 1 and df == 1:
                    first[h][dg] = (start(sums.at[k, pl.ds(h * half, half)], land.at[used], devs[h][0]), used)
                    used += 1
            yield
        state.append([first, used])

    def add(out, sums, k, h, half, arrived):
        at = slice(h * half, (h + 1) * half)
        if k == 0:
            out[at] = out[at] + arrived.astype(F32)
        else:
            sums[k, at] = (sums[k, at].astype(F32) + arrived.astype(F32)).astype(BF16)

    seconds = []
    for (term, out, (to_sib, sums, land)), st in zip(items, state):
        half = out.shape[0] // 2
        first, used = st
        second = [None, None]
        for h in (0, 1):
            nf, ng = rings[h]
            for i in range(1, nf):
                df = (i + 1) % nf
                for dg in [d % ng for d in range(1, ng + 1)]:
                    cp, at = first[h][dg]
                    cp.wait_recv()
                    k = slot(h, df, dg)
                    add(out, sums, k, h, half, land[at])
                    if i < nf - 1:
                        first[h][dg] = (start(sums.at[k, pl.ds(h * half, half)], land.at[used], devs[h][0]), used)
                        used += 1
                    elif dg == 1 and ng > 1:
                        second[h] = (start(sums.at[k, pl.ds(h * half, half)], land.at[used], devs[h][1]), used)
                        used += 1
            if nf == 1 and ng > 1:
                k = slot(h, 0, 1)
                second[h] = (start(sums.at[k, pl.ds(h * half, half)], land.at[used], devs[h][1]), used)
                used += 1
        seconds.append([second, used])
        yield
    for (term, out, (to_sib, sums, land)), (second, used) in zip(items, seconds):
        half = out.shape[0] // 2
        for h in (0, 1):
            nf, ng = rings[h]
            for j in range(1, ng):
                cp, at = second[h]
                cp.wait_recv()
                k = slot(h, 0, (j + 1) % ng)
                add(out, sums, k, h, half, land[at])
                if j < ng - 1:
                    second[h] = (start(sums.at[k, pl.ds(h * half, half)], land.at[used], devs[h][1]), used)
                    used += 1
        yield
    for cp in sends:
        cp.wait_send()
    if g.C == 2:
        for (term, out, (to_sib, sums, land)), base in zip(items, bases):
            for k in range(nb):
                wire.at(base + k, to_sib.at[k], sums.at[k], g.dev(a, b, 1 - c)).wait_send()


def needs_turn(rows):
    return rows % 128 != 0


def turn_scratch(rows, width, L):
    return [pltpu.VMEM((width, L) if needs_turn(rows) else (16, 128), BF16)]


def product_term(left, turned, right, rows, mask=None):
    def term(block, cols):
        at = pl.ds(pl.multiple_of(block * rows, rows), rows)
        if needs_turn(rows):
            return dot(turned[at], right[:, cols])
        v = left[:, at]
        if mask is not None:
            v = (v.astype(F32) * mask[...]).astype(BF16)
        return dot_tokens(v, right[:, cols])

    return term


def turn_steps(rows, turned, left, mask=None):
    if isinstance(left, Later):
        left = left.ref()
    if needs_turn(rows):
        yield from transpose_steps(turned, left, mask)


def given_term(part, rows):
    def term(block, cols):
        return part[pl.ds(pl.multiple_of(block * rows, rows), rows), cols]

    return term


def mlp_back_call(g, low_two, gate_low, up_low, w_gate, w_up, middle, cot, live, gain, cid):
    L, width = low_two.shape
    F = gate_low.shape[1]
    half = L // 2
    rows = width // g.N
    count = tp_count(g, L) + 2 * reduce_count(g)
    grad = jax.ShapeDtypeStruct((rows, F), F32)

    def kernel(low_two, gate_low, up_low, w_gate, w_up, middle, cot, live, gain,
               mid_low, grad_middle, grad_gain, g_gate, g_up,
               two_t, term, sendbuf, recvbuf, *refs):
        send, recv = refs[-2:]
        bufs = refs[:-2]
        greet(plane_peers(g) + tp_peers(g))
        wire = Wire(send, recv)
        gate_low, up_low, w_gate, w_up, middle, cot = (v.ref() for v in (gate_low, up_low, w_gate, w_up, middle, cot))
        back = mlp_back_body((gate_low, up_low, w_gate, w_up, middle, cot, live, gain), (mid_low, grad_middle, grad_gain))

        def gate():
            yield from turn_steps(rows, two_t, low_two)
            yield from reduce_steps(g, wire, [(product_term(low_two.dst, two_t, gate_low, rows), g_gate, bufs[0:3])])

        def up():
            yield from reduce_steps(g, wire, [(product_term(low_two.dst, two_t, up_low, rows), g_up, bufs[3:6])])

        braid(
            tp_steps(g, wire, L, mid_low, *back, (term, sendbuf, recvbuf)),
            (gate(), MLP_GATE),
            (up(), MLP_UP),
        )

    scratch = turn_scratch(rows, width, L) + tp_bufs(g, L, width)
    for _ in range(2):
        scratch += reduce_bufs(g, rows, F)
    return call(
        kernel,
        [low_two, gate_low, up_low, w_gate, w_up, middle, cot, live, gain],
        [jax.ShapeDtypeStruct((L, width), BF16), jax.ShapeDtypeStruct((half, width), F32),
         jax.ShapeDtypeStruct((1, width), F32), grad, grad],
        scratch + sems(count),
        cid,
        "mlp_back",
        later=(1, 3, 2, 4, 0, 5, 6),
    )


def plane_others(g):
    s, q = lax.axis_index("shard"), lax.axis_index("ctx")
    me = s * g.Q + q
    out = []
    for k in range(1, g.N):
        d = (me + k) % g.N
        out.append({"shard": d // g.Q, "ctx": d % g.Q})
    return me, out


def total_steps(g, wire, mine, land_t, land_p, out):
    t = lax.axis_index("tp")
    me, others = plane_others(g)
    land_t[t] = mine[...]
    cps = [wire.copy(mine, land_t.at[t], {"tp": (t + k) % g.T}) for k in range(1, g.T)]
    for cp in cps:
        cp.start()
    yield
    for cp in cps:
        cp.wait()
    total = land_t[0]
    for d in range(1, g.T):
        total = total + land_t[d]
    mine[...] = total
    land_p[me] = total
    cps = [wire.copy(mine, land_p.at[me], d) for d in others]
    for cp in cps:
        cp.start()
    yield
    for cp in cps:
        cp.wait()
    total = land_p[0]
    for d in range(1, g.N):
        total = total + land_p[d]
    out[...] = total


def rec_back_call(g, branch_low, rec_low, w_branch, w_rec, x, grad_middle, gain, part_two, low_one, small, cid):
    L, width = x.shape
    CH = branch_low.shape[1]
    rows = width // g.N
    srows = small.shape[0] // g.N
    shapes = [(rows, CH), (rows, CH), (srows, small.shape[1])]
    count = tp_count(g, L) + len(shapes) * reduce_count(g) + g.T + g.N

    def kernel(branch_low, rec_low, w_branch, w_rec, x, grad_middle, gain, part_two, low_one, small,
               input_grad, gains, g_branch, g_rec, g_small,
               part_one, one_t, both, land_t, land_p, term, sendbuf, recvbuf, *refs):
        send, recv = refs[-2:]
        bufs = refs[:-2]
        t = lax.axis_index("tp")
        greet(plane_others(g)[1] + [{"tp": (t + k) % g.T} for k in range(1, g.T)])
        wire = Wire(send, recv)
        branch_low, rec_low, w_branch, w_rec, x, grad_middle = (
            v.ref() for v in (branch_low, rec_low, w_branch, w_rec, x, grad_middle)
        )
        back = rec_back_body((branch_low, rec_low, w_branch, w_rec, x, grad_middle, gain), (input_grad, part_one))

        def one(term, out, bufs):
            yield from reduce_steps(g, wire, [(term, out, bufs)])

        def branch():
            yield from turn_steps(rows, one_t, low_one)
            yield from one(product_term(low_one.dst, one_t, branch_low, rows), g_branch, bufs[0:3])

        def main():
            steps = tp_steps(g, wire, L, input_grad, *back, (term, sendbuf, recvbuf))
            for _ in range(L // 2 // PIECE + END["take_far"]):
                next(steps)
                yield
            both[:, :width] = part_one[...]
            both[:, width:] = part_two[...]
            totals = total_steps(g, wire, both, land_t, land_p, gains)
            next(totals)
            for _ in steps:
                next(totals, None)
                yield
            run(totals)

        braid(
            main(),
            (branch(), REC_BRANCH),
            (one(product_term(low_one.dst, one_t, rec_low, rows), g_rec, bufs[3:6]), REC_REC),
            (one(given_term(small, srows), g_small, bufs[6:9]), REC_SMALL),
        )

    scratch = [pltpu.VMEM((1, width), F32)] + turn_scratch(rows, width, L)
    scratch += [pltpu.VMEM((1, 2 * width), F32), pltpu.VMEM((g.T, 1, 2 * width), F32), pltpu.VMEM((g.N, 1, 2 * width), F32)]
    scratch += tp_bufs(g, L, width)
    for s in shapes:
        scratch += reduce_bufs(g, *s)
    return call(
        kernel,
        [branch_low, rec_low, w_branch, w_rec, x, grad_middle, gain, part_two, low_one, small],
        [jax.ShapeDtypeStruct((L, width), BF16), jax.ShapeDtypeStruct((1, 2 * width), F32)]
        + [jax.ShapeDtypeStruct(s, F32) for s in shapes],
        scratch + sems(count),
        cid,
        "rec_back",
        later=(0, 2, 1, 3, 8, 4, 5),
    )


def settle(arrays):
    n = len(arrays)

    def kernel(*refs):
        ins, outs, kept, sem = refs[:n], refs[n : 2 * n], refs[2 * n : 3 * n], refs[3 * n]
        cps = [pltpu.make_async_copy(ins[k], kept[k], sem.at[k]) for k in range(n)]
        back = [pltpu.make_async_copy(kept[k], outs[k], sem.at[n + k]) for k in range(n)]
        for cp in cps:
            cp.start()
        for k in range(n):
            cps[k].wait()
            back[k].start()
        for cp in back:
            cp.wait()

    return pl.pallas_call(
        kernel,
        out_shape=[jax.ShapeDtypeStruct(v.shape, v.dtype) for v in arrays],
        in_specs=[ANY] * n,
        out_specs=[ANY] * n,
        scratch_shapes=[pltpu.VMEM(v.shape, v.dtype) for v in arrays] + [pltpu.SemaphoreType.DMA((2 * n,))],
        compiler_params=pltpu.CompilerParams(vmem_limit_bytes=VMEM_LIMIT),
        name="settle",
    )(*arrays)


def up_to(n, k):
    return -(-n // k) * k


def local(g, inputs, lengths, cotangent, norm1_gain, branch_weight, rec_in_weight, conv_weight, conv_bias,
          rgate_weight, rgate_bias, igate_weight, igate_bias, decay_param, out_weight, norm2_gain,
          mlp_gate_weight, mlp_up_weight, mlp_down_weight):
    slots, block_len, width = inputs.shape
    L = slots * block_len
    N = g.N
    heads, rb, bw = rgate_weight.shape
    ch = heads * bw
    taps = conv_weight.shape[0]
    prow = pack_rows(rb)[0]

    def across(v):
        return jnp.pad(v, ((0, 0), (0, ch - v.shape[1])))

    vectors = jnp.concatenate([conv_weight] + [p[None] for p in (conv_bias, rgate_bias, igate_bias, decay_param)], axis=0)
    gates, vectors, gains = lax.optimization_barrier(
        (jnp.stack([rgate_weight, igate_weight]), vectors, jnp.concatenate([norm1_gain, norm2_gain]))
    )
    pack = jnp.concatenate(
        [gates.transpose(0, 2, 1, 3).reshape(2 * rb, ch), across(vectors.reshape(2 * taps, -1)), across(gains.reshape(2, -1))],
        axis=0,
    )
    pack = jnp.pad(pack, ((0, prow - pack.shape[0]), (0, 0)))
    x_low = inputs.reshape(L, width)
    cot = cotangent.reshape(L, width)
    positions = lax.axis_index("ctx") * block_len + jnp.arange(block_len, dtype=jnp.int32)
    live = (positions[None, :] < lengths[:, None]).astype(F32).reshape(L, 1)
    (low_one, branch_pre, rec_pre, mixed, conv, rate, entry, state, edge, low_two, middle, w_rate, w_entry, vecs, gains,
     w_rec, w_branch, w_out, w_gate, w_up, w_down, gate_pre, up_pre, hidden) = front_call(
        g, pack, rec_in_weight, branch_weight, out_weight, [mlp_gate_weight, mlp_up_weight, mlp_down_weight], x_low, bw, rb, 0
    )
    gain_one, gain_two = gains[0:1], gains[1:2]
    act, slope = gelu_both(gate_pre)
    grad_low = (cot.astype(F32) * live).astype(BF16)
    grad_hidden = dot(grad_low, w_down)
    gate_low = (grad_hidden * up_pre * slope).astype(BF16)
    up_low = (grad_hidden * act).astype(BF16)
    mid_low, grad_middle, part_two, g_gate, g_up = mlp_back_call(
        g, low_two, gate_low, up_low, w_gate, w_up, middle, cot, live, gain_two, 2
    )
    branch_low, rec_low, flat, output, g_down, g_out = back_call(
        g, mid_low, w_out, branch_pre, rec_pre, conv, rate, entry, state, edge, w_rate, w_entry, vecs, bw, rb, middle,
        cot, live, hidden, w_down, mixed, 3
    )
    input_grad, gains, g_branch, g_rec, g_small = rec_back_call(
        g, branch_low, rec_low, w_branch, w_rec, x_low, grad_middle, gain_one, part_two, low_one, flat, 4
    )
    gains = lax.dynamic_slice(
        gains.reshape(2, N, -1), (0, lax.axis_index("shard") * g.Q + lax.axis_index("ctx"), 0), (2, 1, width // N)
    )[:, 0]
    me = lax.axis_index("shard") * g.Q + lax.axis_index("ctx")
    g_rate = g_small[:rb].reshape(rb, heads, bw).transpose(1, 0, 2)
    g_entry = g_small[rb : 2 * rb].reshape(rb, heads, bw).transpose(1, 0, 2)
    rest = lax.dynamic_slice(g_small[2 * rb : 2 * rb + 8].reshape(8, heads, bw), (0, 0, me * rb), (8, heads, rb))
    shape = (slots, block_len, width)
    output, input_grad, g_branch, g_rec, g_out, g_gate, g_up, g_down = settle(
        [output, input_grad, g_branch, g_rec, g_out, g_gate, g_up, g_down]
    )
    return (
        output.reshape(shape), input_grad.reshape(shape), gains[0], g_branch, g_rec, rest[:taps], rest[4],
        g_rate, rest[5], g_entry, rest[6], rest[7], g_out, gains[1], g_gate, g_up, g_down,
    )


def solution(mesh):
    plane = ("shard", "ctx")
    rows, cols = P(plane), P(plane, "tp")
    tok, gate, chan = P("shard", "ctx", None), P("tp", plane, None), P("tp", plane)
    taps = P(None, "tp", plane)
    params = (rows, cols, cols, taps, chan, gate, chan, gate, chan, chan, cols, rows, cols, cols, cols)
    return jax.shard_map(
        functools.partial(local, Grid(mesh)),
        mesh=mesh,
        in_specs=(tok, P("shard"), tok) + params,
        out_specs=(tok, tok) + params,
        check_vma=False,
    )
```

```python
import functools

import jax
import jax.numpy as jnp
from jax import lax
from jax.experimental import pallas as pl
from jax.experimental.pallas import tpu as pltpu
from jax.sharding import PartitionSpec as P

EPS = 1e-06
DECAY_SCALE = 8.0
F32 = jnp.float32
BF16 = jnp.bfloat16
MESH = pl.DeviceIdType.MESH
ANY = pl.BlockSpec(memory_space=pl.ANY)
VM = pl.BlockSpec(memory_space=pltpu.VMEM)
VMEM_LIMIT = 63 * 1024 * 1024


def dot(a, b):
    return jnp.dot(a, b, preferred_element_type=F32)


def dot_rows(a, b):
    return lax.dot_general(a, b, (((1,), (1,)), ((), ())), preferred_element_type=F32)


def dot_tokens(a, b):
    return lax.dot_general(a, b, (((0,), (0,)), ((), ())), preferred_element_type=F32)


def halves(v):
    hi = v.astype(BF16)
    return hi, (v - hi.astype(F32)).astype(BF16)


def gelu(v):
    return jax.nn.gelu(v)


def gelu_both(v):
    c = 0.7978845608028654
    th = jnp.tanh(c * (v + 0.044715 * v * v * v))
    half = 0.5 * (1.0 + th)
    return v * half, half + 0.5 * v * (1.0 - th * th) * c * (1.0 + 3 * 0.044715 * v * v)


def sigmoid(v):
    return 1.0 / (1.0 + jnp.exp(-v))


def minus_expm1(v):
    near = -v * (1.0 + v / 2 * (1.0 + v / 3 * (1.0 + v / 4 * (1.0 + v / 5 * (1.0 + v / 6)))))
    return jnp.where(v > -0.25, near, 1.0 - jnp.exp(v))


class Grid:
    def __init__(self, mesh):
        self.S, self.Q, self.T = (mesh.shape[n] for n in ("shard", "ctx", "tp"))
        dev = mesh.devices

        def chip(d):
            return tuple(getattr(d, "coords", None) or ())

        def paired(one, two):
            return bool(chip(one)) and chip(one) == chip(two)

        self.core_in = None
        if self.Q % 2 == 0 and paired(dev[0, 0, 0], dev[0, 1, 0]):
            self.core_in = "ctx"
        elif self.S % 2 == 0 and paired(dev[0, 0, 0], dev[1, 0, 0]):
            self.core_in = "shard"
        self.C = 1 if self.core_in is None else 2
        self.A = self.S // 2 if self.core_in == "shard" else self.S
        self.B = self.Q // 2 if self.core_in == "ctx" else self.Q
        self.N = self.S * self.Q

    def me(self):
        s, q = lax.axis_index("shard"), lax.axis_index("ctx")
        if self.core_in == "ctx":
            return s, q // 2, q % 2
        if self.core_in == "shard":
            return s // 2, q, s % 2
        return s, q, 0

    def shard_ctx(self, a, b, c):
        if self.core_in == "ctx":
            return a, b * 2 + c
        if self.core_in == "shard":
            return a * 2 + c, b
        return a, b

    def block(self, a, b, c):
        s, q = self.shard_ctx(a, b, c)
        return s * self.Q + q

    def dev(self, a, b, c):
        s, q = self.shard_ctx(a, b, c)
        return {"shard": s, "ctx": q}


class Wire:
    def __init__(self, send, recv, base=0):
        self.send, self.recv, self.used = send, recv, base

    def copy(self, src, dst, dev):
        self.used += 1
        return self.at(self.used - 1, src, dst, dev)

    def at(self, k, src, dst, dev):
        return pltpu.make_async_remote_copy(
            src_ref=src,
            dst_ref=dst,
            send_sem=self.send.at[k],
            recv_sem=self.recv.at[k],
            device_id=dev,
            device_id_type=MESH,
        )


def greet(devs):
    bar = pltpu.get_barrier_semaphore()
    for d in devs:
        pl.semaphore_signal(bar, inc=1, device_id=d, device_id_type=MESH)
    pl.semaphore_wait(bar, len(devs))


def ring_peers(size, at, place):
    if size == 1:
        return []
    if size == 2:
        return [place((at + 1) % 2)]
    return [place((at + 1) % size), place((at + size - 1) % size)]


def plane_peers(g):
    a, b, c = g.me()
    out = ring_peers(g.A, a, lambda k: g.dev(k, b, c))
    out += ring_peers(g.B, b, lambda k: g.dev(a, k, c))
    if g.C == 2:
        out.append(g.dev(a, b, 1 - c))
    return out


def braid(main, *sides):
    k = 0
    for _ in main:
        for steps, plan in sides:
            for _ in range(plan[k] if k < len(plan) else 0):
                next(steps, None)
        k += 1
    left = [s[0] for s in sides]
    while left:
        left = [s for s in left if next(s, left) is not left]


def only(steps, n):
    for _ in range(n):
        next(steps)
        yield


def at_steps(*pairs):
    plan = [0] * (1 + max(last for _, last, _ in pairs))
    for first, last, each in pairs:
        for k in range(first, last + 1):
            plan[k] += each
    return tuple(plan)


ALWAYS = (1,) * 64


def run(*steps):
    for s in steps:
        for _ in s:
            pass


class Later:
    def __init__(self, src, dst, sem):
        self.copy, self.dst, self.here = pltpu.make_async_copy(src, dst, sem), dst, False
        self.copy.start()

    def ref(self):
        if not self.here:
            self.copy.wait()
            self.here = True
        return self.dst


def call(kernel, operands, out_shape, scratch, cid, name, in_specs=None, out_specs=None, later=(), early=()):
    in_specs = list(in_specs or [VM] * len(operands))
    out_specs = list(out_specs or [VM] * len(out_shape))
    for k in later:
        in_specs[k] = ANY
    for k in early:
        out_specs[k] = ANY
    n, m = len(later), len(early)
    n_in = len(operands)

    def body(*refs):
        refs = list(refs)
        if m:
            kept, sem = refs[-m - 1 : -1], refs[-1]
            refs = refs[: -m - 1]
            copies = {}
            for j, k in enumerate(early):
                copies[id(kept[j])] = pltpu.make_async_copy(kept[j], refs[n_in + k], sem.at[j])
                refs[n_in + k] = kept[j]
        if n:
            held, sem_in = refs[-n - 1 : -1], refs[-1]
            refs = refs[: -n - 1]
            for j, k in enumerate(later):
                refs[k] = Later(refs[k], held[j], sem_in.at[j])
        if not m:
            kernel(*refs)
            return
        kernel(*refs, send_out=lambda *which: [copies[id(r)].start() for r in which])
        for cp in copies.values():
            cp.wait()

    extra = [pltpu.VMEM(operands[k].shape, operands[k].dtype) for k in later]
    if n:
        extra.append(pltpu.SemaphoreType.DMA((n,)))
    extra += [pltpu.VMEM(out_shape[k].shape, out_shape[k].dtype) for k in early]
    if m:
        extra.append(pltpu.SemaphoreType.DMA((m,)))
    return pl.pallas_call(
        body,
        out_shape=out_shape,
        in_specs=in_specs,
        out_specs=out_specs,
        scratch_shapes=list(scratch) + extra,
        compiler_params=pltpu.CompilerParams(
            collective_id=cid, has_side_effects=True, vmem_limit_bytes=VMEM_LIMIT
        ),
        name=name,
    )(*operands)


def sems(n):
    return [pltpu.SemaphoreType.DMA((max(1, n),)), pltpu.SemaphoreType.DMA((max(1, n),))]


def gather_count(g):
    ring = 0
    for nf, ng in ((g.A, g.B), (g.B, g.A)):
        ring += (nf - 1) + (ng - 1) * nf
    return ring + (g.C - 1) * (1 + ring)


def gather_steps(g, wire, here, srcs, dsts):
    a, b, c = g.me()
    sib = None if g.C == 1 else g.dev(a, b, 1 - c)
    sends, sib_copies = [], []

    def ring(h):
        if h == 0:
            return g.A, a, (lambda k: g.dev(k, b, c)), g.B, b, (lambda k: g.dev(a, k, c)), (lambda f, s: g.block(f, s, c))
        return g.B, b, (lambda k: g.dev(a, k, c)), g.A, a, (lambda k: g.dev(k, b, c)), (lambda f, s: g.block(s, f, c))

    def start(src, dst, dev):
        cp = wire.copy(src, dst, dev)
        cp.start()
        sends.append(cp)
        return cp

    def rows_of(dst, blk, h, rows):
        half = rows // 2
        return dst.at[pl.ds(pl.multiple_of(blk * rows + h * half, half), half)]

    state = []
    mine = g.block(a, b, c)
    local_copies = []
    for src, dst in zip(srcs, dsts):
        rows = src.shape[0]
        half = rows // 2
        cp = pltpu.make_async_copy(src, dst.at[pl.ds(pl.multiple_of(mine * rows, rows), rows)], here.at[len(local_copies)])
        cp.start()
        local_copies.append(cp)
        per = []
        for h in (0, 1):
            nf, f, fdev, ng, s, sdev, blk = ring(h)
            own = src.at[pl.ds(h * half, half)]
            land = rows_of(dst, mine, h, rows)
            first = start(own, land, fdev((f + 1) % nf)) if nf > 1 else None
            per.append([first, None, own, land])
        for h in (0, 1):
            nf, f, fdev, ng, s, sdev, blk = ring(h)
            _, _, own, land = per[h]
            second = {}
            if ng > 1:
                second[(0, 0)] = start(own, land, sdev((s + 1) % ng))
            per[h][1] = second
        if sib is not None:
            whole = dst.at[pl.ds(pl.multiple_of(mine * rows, rows), rows)]
            sib_copies.append(start(src, whole, sib))
        state.append(per)
        yield
    for (src, dst), per in zip(zip(srcs, dsts), state):
        rows = src.shape[0]
        for h in (0, 1):
            nf, f, fdev, ng, s, sdev, blk = ring(h)
            cp = per[h][0]
            for i in range(1, nf):
                cp.wait_recv()
                at = rows_of(dst, blk((f - i) % nf, s), h, rows)
                if i < nf - 1:
                    cp = start(at, at, fdev((f + 1) % nf))
                if ng > 1:
                    per[h][1][(0, i)] = start(at, at, sdev((s + 1) % ng))
                if sib is not None:
                    sib_copies.append(start(at, at, sib))
        yield
    for (src, dst), per in zip(zip(srcs, dsts), state):
        rows = src.shape[0]
        for h in (0, 1):
            nf, f, fdev, ng, s, sdev, blk = ring(h)
            second = per[h][1]
            for j in range(1, ng):
                for i in range(nf):
                    second[(j - 1, i)].wait_recv()
                    at = rows_of(dst, blk((f - i) % nf, (s - j) % ng), h, rows)
                    if j < ng - 1:
                        second[(j, i)] = start(at, at, sdev((s + 1) % ng))
                    if sib is not None:
                        sib_copies.append(start(at, at, sib))
        yield
    for cp in local_copies:
        cp.wait()
    for cp in sib_copies:
        cp.wait_recv()
    for cp in sends:
        cp.wait_send()


def tp_peers(g):
    t = lax.axis_index("tp")
    return ring_peers(g.T, t, lambda k: {"tp": k})


MIX_GATE = at_steps((6, 6, 1), (15, 15, 1))
MIX_UP = at_steps((11, 11, 1), (19, 19, 1))
MIX_DOWN = at_steps((11, 11, 1))
BACK_Z = ALWAYS
BACK_DOWN = at_steps((2, 2, 1), (4, 4, 1), (6, 6, 1), (8, 8, 1), (9, 10, 2), (17, 17, 1))
BACK_OUT = at_steps((11, 12, 2), (13, 16, 1), (21, 21, 1))
MLP_GATE = at_steps((0, 3, 2), (8, 8, 1), (14, 14, 1))
MLP_UP = at_steps((4, 7, 2), (14, 14, 1), (21, 21, 1))
REC_BRANCH = at_steps((0, 3, 2), (9, 9, 1), (17, 17, 1))
REC_REC = at_steps((4, 7, 2), (13, 13, 1), (19, 19, 1))
REC_SMALL = at_steps((8, 11, 2), (15, 15, 1), (20, 20, 1))
PIECE = 32
CHUNK = 256


def tp_count(g, rows):
    return 4 * (rows // 2 // PIECE)


def tp_place(g):
    t = lax.axis_index("tp")
    side = jnp.where(t >= (g.T + 1) // 2, 1, 0)
    return side, jnp.where(side == 1, g.T - 1 - t, t)


END = {"send_near": 0, "take_far": 8, "take_near": 14}
INNER = {"send_near": 0, "take_far": 4, "pass_far": 10, "take_near": 12}


def tp_steps(g, wire, rows, out, partial=None, finish=None, bufs=None, gather=True):
    T = g.T
    t = lax.axis_index("tp")
    half = rows // 2
    pieces = half // PIECE
    side, pos = tp_place(g)
    end, inner = pos == 0, pos > 0
    near, far = side, 1 - side
    away = {"tp": jnp.where(side == 1, t - 1, t + 1)}
    home = {"tp": jnp.where(side == 1, (t + 1) % T, (t + T - 1) % T)}
    k_rs = wire.used
    if partial is not None:
        wire.used += 2 * pieces
    k_ag = wire.used
    if gather:
        wire.used += 2 * pieces

    def row(d, p):
        return pl.multiple_of(half * (1 - d) + p * PIECE, PIECE)

    def rs(d, p, dev):
        return wire.at(k_rs + d * pieces + p, bufs[1].at[d, p], bufs[2].at[d, p], dev)

    def ag(d, p, dev):
        at = out.at[pl.ds(row(d, p), PIECE)]
        return wire.at(k_ag + d * pieces + p, at, at, dev)

    step = chunk_rows(g, rows, out.shape[1])
    per = step // PIECE

    def ready(d, p, which):
        term = bufs[0].at[which]
        if p % per == 0:
            partial(pl.multiple_of(half * (1 - d) + p * PIECE, step), step, term)
        return term.at[pl.ds(p % per * PIECE, PIECE)]

    def send_near(p, at_end):
        part = ready(near, p, 0)[...]
        if not at_end:
            rs(near, p, away).wait_recv()
            part = part + bufs[2][near, p].astype(F32)
        bufs[1][near, p] = part.astype(BF16)
        rs(near, p, away).start()

    def take_far(p, at_end):
        part = ready(far, p, 1)
        rs(far, p, home).wait_recv()
        total = part[...] + bufs[2][far, p].astype(F32)
        if not at_end:
            bufs[1][far, p] = total.astype(BF16)
            rs(far, p, home).start()
            return
        done = finish(total, p * PIECE, row(far, p), PIECE)
        if gather:
            out[pl.ds(row(far, p), PIECE)] = done
            ag(far, p, away).start()
        else:
            out[p * PIECE : (p + 1) * PIECE] = done

    def pass_far(p, at_end):
        ag(far, p, away).wait_recv()
        ag(far, p, away).start()

    def take_near(p, at_end):
        ag(near, p, home).wait_recv()
        if not at_end:
            ag(near, p, home).start()

    acts = {"send_near": send_near, "take_far": take_far, "pass_far": pass_far, "take_near": take_near}
    if partial is None:

        @pl.when(end)
        def _():
            for p in range(pieces):
                ag(far, p, away).start()

        acts = {"pass_far": pass_far, "take_near": take_near}
        yield
    elif not gather:
        acts = {"send_near": send_near, "take_far": take_far}

    def schedule(lates):
        lates = {k: v for k, v in lates.items() if k in acts}
        least = min(lates.values())
        return [(acts[k], v - least) for k, v in lates.items()]

    plans = [(end, True, schedule(END)), (inner, False, schedule(INNER))]
    for i in range(pieces + max(late for _, _, plan in plans for _, late in plan)):
        for where, at_end, plan in plans:

            @pl.when(where)
            def _():
                for act, late in plan:
                    if 0 <= i - late < pieces:
                        act(i - late, at_end)

        yield
    if partial is not None:
        for p in range(pieces):
            rs(near, p, away).wait_send()
    if gather:
        for p in range(pieces):
            ag(far, p, away).wait_send()

    @pl.when(inner)
    def _():
        for p in range(pieces):
            if partial is not None:
                rs(far, p, home).wait_send()
            if gather:
                ag(near, p, home).wait_send()


def chunk_rows(g, rows, width):
    return min(CHUNK // 4 if needs_turn(width // g.N) else CHUNK, rows // 2)


def tp_bufs(g, rows, width):
    pieces = rows // 2 // PIECE
    return [
        pltpu.VMEM((2, chunk_rows(g, rows, width), width), F32),
        pltpu.VMEM((2, pieces, PIECE, width), BF16),
        pltpu.VMEM((2, pieces, PIECE, width), BF16),
    ]


def transpose_steps(dst, src, scale=None):
    if isinstance(src, Later):
        src = src.ref()
    width = src.shape[1]
    part = 512
    assert width % part == 0

    for at in range(0, width, part):

        def body(j, _):
            c0 = pl.multiple_of(at + j * 128, 128)
            v = src[:, pl.ds(c0, 128)]
            if scale is not None:
                v = (v.astype(F32) * scale[...]).astype(BF16)
            dst[pl.ds(c0, 128), :] = v.T
            return 0

        lax.fori_loop(0, part // 128, body, 0)
        yield


def chain(*steps):
    for s in steps:
        yield from s


def tile_of(width):
    return 512 if width % 512 == 0 else width


def rows_product(term, at, n, pairs):
    width = term.shape[1]
    tile = tile_of(width)

    def body(j, _):
        c0 = pl.multiple_of(j * tile, tile)
        total = None
        for l, r in pairs:
            p = dot_rows(l[pl.ds(at, n)], r[pl.ds(c0, tile)])
            total = p if total is None else total + p
        term[:, pl.ds(c0, tile)] = total
        return 0

    lax.fori_loop(0, width // tile, body, 0)


def rows_dot(dst, left, right):
    step = 256 if left.shape[0] % 256 == 0 else left.shape[0]

    def body(i, _):
        r0 = pl.ds(pl.multiple_of(i * step, step), step)
        dst[r0] = dot(left[r0], right[...])
        return 0

    lax.fori_loop(0, left.shape[0] // step, body, 0)


def mean_square(v):
    return jnp.mean(v * v, axis=-1, keepdims=True)


def mix_out_body(ins, outs):
    mixed, w_out, x, gain = ins
    _, middle = outs

    def partial(at, n, term):
        rows_product(term, at, n, [(mixed, w_out)])

    def finish(total, near, at, n):
        m = x[pl.ds(at, n)].astype(F32) + total
        middle[near : near + n] = m
        return (m * lax.rsqrt(mean_square(m) + EPS) * gain[...]).astype(BF16)

    return partial, finish


def mlp_out_body(ins, outs):
    hidden, w_down, middle, live = ins

    def partial(at, n, term):
        rows_product(term, at, n, [(hidden, w_down)])

    def finish(total, near, at, n):
        return ((middle[near : near + n] + total) * live[pl.ds(at, n)]).astype(BF16)

    return partial, finish


def norm_back(grad_normed, rows, gain):
    inv = lax.rsqrt(mean_square(rows) + EPS)
    gg = grad_normed * gain
    back = inv * gg - rows * (inv * inv * inv) * jnp.mean(gg * rows, axis=-1, keepdims=True)
    return back, jnp.sum(grad_normed * rows * inv, axis=0, keepdims=True)


def mlp_back_body(ins, outs):
    gate_low, up_low, w_gate, w_up, middle, cot, live, gain = ins
    _, grad_middle, grad_gain = outs
    grad_gain[...] = jnp.zeros_like(grad_gain)

    def partial(at, n, term):
        rows_product(term, at, n, [(gate_low, w_gate), (up_low, w_up)])

    def finish(total, near, at, n):
        back, gain_sum = norm_back(total, middle[near : near + n], gain[...])
        gm = cot[pl.ds(at, n)].astype(F32) * live[pl.ds(at, n)] + back
        grad_middle[near : near + n] = gm
        grad_gain[...] = grad_gain[...] + gain_sum
        return gm.astype(BF16)

    return partial, finish


def rec_back_body(ins, outs):
    branch_low, rec_low, w_branch, w_rec, x, grad_middle, gain = ins
    _, grad_gain = outs
    grad_gain[...] = jnp.zeros_like(grad_gain)

    def partial(at, n, term):
        rows_product(term, at, n, [(branch_low, w_branch), (rec_low, w_rec)])

    def finish(total, near, at, n):
        back, gain_sum = norm_back(total, x[pl.ds(at, n)].astype(F32), gain[...])
        grad_gain[...] = grad_gain[...] + gain_sum
        return (grad_middle[near : near + n] + back).astype(BF16)

    return partial, finish


TAPS, SHIFT, RBIAS, EBIAS, SOFT, SLOPE = 0, 4, 5, 6, 7, 8
ROWS = 64
GROUP = 8


def ctx_peers(g):
    q = lax.axis_index("ctx")
    return [{"ctx": (q + k) % g.Q} for k in range(1, g.Q)]


def swap_edges(g, wire, src, land):
    q = lax.axis_index("ctx")
    cps = []
    for k in range(1, g.Q):
        cp = wire.copy(src, land.at[q], {"ctx": (q + k) % g.Q})
        cp.start()
        cps.append(cp)
    yield
    for cp in cps:
        cp.wait_recv()
    for cp in cps:
        cp.wait_send()


def row_shift(v, n):
    return pltpu.roll(v, n % v.shape[0], 0)


def forward_steps(g, wire, branch, w_rate, w_entry, vecs, mixed, conv, rate, entry, state, edge,
                  ext, acum, bcum, tot, gath):
    L, CH = branch.shape
    q = lax.axis_index("ctx")
    sub = lax.broadcasted_iota(jnp.int32, (GROUP, 1), 0)

    def chunk(i, carry):
        ca, cb = carry
        r0 = i * ROWS
        wide = ext[pl.ds(r0, ROWS + 8)]
        c = vecs[SHIFT : SHIFT + 1] + vecs[TAPS : TAPS + 1] * wide[8:]
        for k in range(1, 4):
            c = c + vecs[TAPS + k : TAPS + k + 1] * row_shift(wide, k)[8:]
        conv[pl.ds(r0, ROWS)] = c
        hi, lo = halves(c)
        gr = sigmoid(dot(hi, w_rate[...]) + dot(lo, w_rate[...]) + vecs[RBIAS : RBIAS + 1])
        ge = sigmoid(dot(hi, w_entry[...]) + dot(lo, w_entry[...]) + vecs[EBIAS : EBIAS + 1])
        rate[pl.ds(r0, ROWS)] = gr
        entry[pl.ds(r0, ROWS)] = ge
        log = -DECAY_SCALE * gr * vecs[SOFT : SOFT + 1]
        dec = jnp.exp(log)
        drive = jnp.sqrt(minus_expm1(2.0 * log)) * ge * c
        for n in range(ROWS // GROUP):
            A = dec[n * GROUP : (n + 1) * GROUP]
            B = drive[n * GROUP : (n + 1) * GROUP]
            for step in (1, 2, 4):
                keep = sub >= step
                As = jnp.where(keep, row_shift(A, step), 1.0)
                Bs = jnp.where(keep, row_shift(B, step), 0.0)
                B = B + A * Bs
                A = A * As
            B = B + A * cb
            A = A * ca
            acum[pl.ds(r0 + n * GROUP, GROUP)] = A
            bcum[pl.ds(r0 + n * GROUP, GROUP)] = B
            ca = A[GROUP - 1 : GROUP]
            cb = B[GROUP - 1 : GROUP]
        return ca, cb

    ca, cb = jnp.ones((1, CH), F32), jnp.zeros((1, CH), F32)
    for i in range(L // ROWS):
        ca, cb = chunk(i, (ca, cb))
        yield
    tot[0:1] = ca
    tot[1:2] = cb
    start = jnp.zeros((1, CH), F32)
    if g.Q > 1:
        yield from swap_edges(g, wire, tot, gath)
        for d in range(g.Q - 1):
            new = gath[d, 0:1] * start + gath[d, 1:2]
            start = jnp.where(d < q, new, start)
    edge[...] = jnp.broadcast_to(start, (8, CH))
    yield

    def fix(i, _):
        r0 = pl.multiple_of(i * ROWS, ROWS)
        s = bcum[pl.ds(r0, ROWS)] + acum[pl.ds(r0, ROWS)] * start
        state[pl.ds(r0, ROWS)] = s
        mixed[pl.ds(r0, ROWS)] = (gelu_both(branch[pl.ds(r0, ROWS)])[0] * s).astype(BF16)
        return 0

    lax.fori_loop(0, L // ROWS, fix, 0)
    yield


def small_rows(rb):
    return up_to(2 * rb + 8, 32)


def pack_rows(rb):
    return up_to(2 * rb + 10, 32), 2 * rb, 2 * rb + 8


def iota2(shape):
    return lax.broadcasted_iota(jnp.int32, shape, 0), lax.broadcasted_iota(jnp.int32, shape, 1)


def log1p_small(e):
    return jnp.where(e < 0.02, e * (1.0 - e * (0.5 - e * (1.0 / 3 - e * 0.25))), jnp.log(1.0 + e))


def unpack(packs, bw, rb, rows, w_rate, w_entry, vecs, gains):
    total, CH = packs.shape
    n = bw // rb
    prow, o_vec, o_gain = pack_rows(rb)
    m, l = iota2((bw, total))
    _, lane = iota2((bw, CH))
    for dst, off in ((w_rate, 0), (w_entry, rb)):
        pick = jnp.logical_and(l // prow == m // rb, l % prow == m % rb + off)
        block = dot(jnp.where(pick, 1.0, 0.0).astype(BF16), packs[...])
        for h in range(CH // bw):
            dst[h * bw : (h + 1) * bw] = jnp.where(lane // bw == h, block, 0.0).astype(BF16)

    def rows_at(off):
        m, l = iota2((n * 8, total))
        pick = l == (m // 8) * prow + off + m % 8
        return dot(jnp.where(pick, 1.0, 0.0).astype(BF16), packs[...])

    short = rows_at(o_vec)[:, :128].astype(BF16)
    l, m = iota2((128, CH))
    spread = jnp.logical_and(l // rb == m // bw, l % rb == m % rb)
    wide = dot(short, jnp.where(spread, 1.0, 0.0).astype(BF16))
    _, lane = iota2((8, CH))
    vec = jnp.zeros((8, CH), F32)
    for j in range(n):
        vec = vec + jnp.where(lane % bw // rb == j, wide[j * 8 : (j + 1) * 8], 0.0)
    decay = vec[7:8]
    e = jnp.exp(-jnp.abs(decay))
    vecs[0:7] = vec[0:7]
    vecs[SOFT : SOFT + 1] = jnp.maximum(-decay, 0.0) + log1p_small(e)
    vecs[SLOPE : SLOPE + 1] = sigmoid(-decay)
    vecs[SLOPE + 1 :] = jnp.zeros((16 - SLOPE - 1, CH), F32)
    both = rows_at(o_gain)
    if rows % 128 == 0:
        for j in range(n):
            for u in range(2):
                gains[u : u + 1, j * rows : (j + 1) * rows] = both[j * 8 + u : j * 8 + u + 1, :rows]
    else:
        l, m = iota2((128, gains.shape[1]))
        row = jnp.zeros((8, gains.shape[1]), F32)
        for j in range(n):
            place = jnp.logical_and(l < rows, m == l + j * rows)
            row = row + dot(both[j * 8 : (j + 1) * 8, :128].astype(BF16), jnp.where(place, 1.0, 0.0).astype(BF16))
        gains[...] = row[:2]


def mlp_forward_steps(w_gate, w_up, low_two, gate_pre, up_pre, hidden, wg, wu, og, ou, oh, sem_in, sem_out):
    L, tile = og.shape[1], og.shape[2]
    nt = w_gate.shape[1] // tile

    def loads(j):
        cols = pl.ds(j * tile, tile)
        return [pltpu.make_async_copy(w.at[:, cols], b.at[j % 2], sem_in.at[j % 2, i]) for i, (w, b) in enumerate(((w_gate, wg), (w_up, wu)))]

    def stores(j):
        cols = pl.ds(j * tile, tile)
        return [pltpu.make_async_copy(b.at[j % 2], o.at[:, cols], sem_out.at[j % 2, i]) for i, (b, o) in enumerate(((og, gate_pre), (ou, up_pre), (oh, hidden)))]

    for cp in loads(0):
        cp.start()
    for j in range(nt):
        if j + 1 < nt:
            for cp in loads(j + 1):
                cp.start()
        for cp in loads(j):
            cp.wait()
        if j >= 2:
            for cp in stores(j - 2):
                cp.wait()
        gate, up, out = og.at[j % 2], ou.at[j % 2], oh.at[j % 2]
        rows_dot(gate, low_two, wg.at[j % 2])
        rows_dot(up, low_two, wu.at[j % 2])

        def act(i, _):
            r0 = pl.ds(pl.multiple_of(i * 32, 32), 32)
            out[r0] = (gelu_both(gate[r0])[0] * up[r0]).astype(BF16)
            return 0

        lax.fori_loop(0, L // 32, act, 0)
        for cp in stores(j):
            cp.start()
        yield
    for j in range(max(0, nt - 2), nt):
        for cp in stores(j):
            cp.wait()


def front_call(g, pack, rec_shard, branch_shard, out_shard, mlp_shards, x, bw, rb, cid):
    L, width = x.shape
    CH = pack.shape[1]
    half = L // 2
    n = len(mlp_shards)
    rows = out_shard.shape[0]
    wide = jax.ShapeDtypeStruct((L, CH), F32)
    dense = jax.ShapeDtypeStruct((CH, CH), BF16)

    def whole(s):
        return jax.ShapeDtypeStruct((g.N * s.shape[0], s.shape[1]), s.dtype)

    low = jax.ShapeDtypeStruct((L, width), BF16)
    outs = [low, wide, wide, jax.ShapeDtypeStruct((L, CH), BF16), wide, wide, wide, wide, jax.ShapeDtypeStruct((8, CH), F32),
            low, jax.ShapeDtypeStruct((half, width), F32), dense, dense, jax.ShapeDtypeStruct((16, CH), F32),
            jax.ShapeDtypeStruct((2, width), F32), whole(rec_shard), whole(branch_shard), whole(out_shard)]
    outs += [whole(s) for s in mlp_shards]
    F = mlp_shards[0].shape[1]
    tile = tile_of(F)
    outs += [jax.ShapeDtypeStruct((L, F), F32), jax.ShapeDtypeStruct((L, F), F32), jax.ShapeDtypeStruct((L, F), BF16)]
    count = 2 * g.Q + tp_count(g, L) + (n + 4) * gather_count(g)

    def kernel(pack, rec_shard, branch_shard, out_shard, *refs, send_out):
        shards, x = refs[:n], refs[n]
        (low_one, branch, rec, mixed, conv, rate, entry, state, edge, low_two, middle, w_rate, w_entry, vecs, gains,
         w_rec, w_branch, w_out) = refs[n + 1 : n + 19]
        full = refs[n + 19 : 2 * n + 19]
        made = refs[2 * n + 19 : 2 * n + 22]
        (packs, x_edge, a_edge, ext, acum, bcum, tot, gath, term, sendbuf, recvbuf, send, recv, here, *tiles) = refs[2 * n + 22 :]
        q = lax.axis_index("ctx")
        greet(ctx_peers(g) + plane_peers(g) + tp_peers(g))
        wire = Wire(send, recv)
        slots = iter(range(n + 4))

        def gather(srcs, dsts):
            at = [next(slots) for _ in srcs]
            return gather_steps(g, wire, here.at[pl.ds(at[0], len(at))], srcs, dsts)

        small = gather([pack], [packs])
        next(small)
        edge_copy = None
        if g.Q > 1:
            edge_copy = wire.copy(x.at[pl.ds(L - 16, 16)], x_edge, {"ctx": (q + 1) % g.Q})
            edge_copy.start()
        of_rec = gather([rec_shard], [w_rec])
        of_branch = gather([branch_shard], [w_branch])
        of_out = gather([out_shard], [w_out])
        of_gate, of_up, of_down = (gather([s], [d]) for s, d in zip(shards, full))
        next(of_rec)
        next(of_branch)
        run(small)
        unpack(packs, bw, rb, rows, w_rate, w_entry, vecs, gains)

        def norm_rows(i, _):
            r0 = pl.ds(pl.multiple_of(i * ROWS, ROWS), ROWS)
            v = x[r0].astype(F32)
            low_one[r0] = (v * lax.rsqrt(mean_square(v) + EPS) * gains[0:1]).astype(BF16)
            return 0

        lax.fori_loop(0, L // ROWS, norm_rows, 0)
        next(of_rec)
        next(of_branch)
        next(of_out)
        next(of_rec)
        next(of_branch)
        if g.Q > 1:
            edge_copy.wait()
            v = x_edge[...].astype(F32)
            a_edge[...] = (v * lax.rsqrt(mean_square(v) + EPS) * gains[0:1]).astype(BF16)
        run(of_rec)
        rows_dot(rec, low_one, w_rec)
        ext[8:] = rec[...]
        if g.Q > 1:
            ext[0:8] = jnp.where(q > 0, dot(a_edge[...], w_rec[...])[8:], 0.0)
        else:
            ext[0:8] = jnp.zeros((8, CH), F32)
        fwd = forward_steps(g, wire, branch, w_rate, w_entry, vecs, mixed, conv, rate, entry, state, edge,
                            ext, acum, bcum, tot, gath)
        for k in range(L // ROWS):
            next(fwd)
            if k == 2:
                next(of_out)
            if k == 6:
                next(of_out)
        if g.Q > 1:
            next(fwd)
        next(of_gate)
        next(of_up)
        run(of_branch)
        rows_dot(branch, low_one, w_branch)
        send_out(low_one, rec, conv, rate, entry, w_rate, w_entry, w_rec, w_branch, branch)
        run(fwd, of_out)
        send_out(mixed, state, w_out)
        partial, finish = mix_out_body((mixed, w_out, x, gains.at[pl.ds(1, 1)]), (low_two, middle))
        braid(
            tp_steps(g, wire, L, low_two, partial, finish, (term, sendbuf, recvbuf)),
            (of_gate, MIX_GATE),
            (of_up, MIX_UP),
            (only(of_down, 1), MIX_DOWN),
        )
        for _ in mlp_forward_steps(full[0], full[1], low_two, *made, *tiles):
            next(of_down, None)
        run(of_down)

    return call(
        kernel,
        [pack, rec_shard, branch_shard, out_shard, *mlp_shards, x],
        outs,
        [
            pltpu.VMEM((g.N * pack.shape[0], CH), BF16),
            pltpu.VMEM((16, width), BF16),
            pltpu.VMEM((16, width), BF16),
            pltpu.VMEM((L + 8, CH), F32),
            pltpu.VMEM((L, CH), F32),
            pltpu.VMEM((L, CH), F32),
            pltpu.VMEM((8, CH), F32),
            pltpu.VMEM((g.Q, 8, CH), F32),
        ]
        + tp_bufs(g, L, width)
        + sems(count)
        + [pltpu.SemaphoreType.DMA((n + 4,))]
        + [pltpu.VMEM((2, width, tile), BF16)] * 2
        + [pltpu.VMEM((2, L, tile), F32)] * 2
        + [pltpu.VMEM((2, L, tile), BF16), pltpu.SemaphoreType.DMA((2, 2)), pltpu.SemaphoreType.DMA((2, 3))],
        cid,
        "front",
        [VM] * (n + 5),
        [VM] * 18 + [ANY] * (n + 3),
        early=(0, 1, 2, 3, 4, 5, 6, 7, 11, 12, 15, 16, 17),
    )


def backward_steps(g, wire, mid_low, w_out, branch, rec, conv, rate, entry, state, edge, w_rate, w_entry, vecs,
                    branch_low, rec_low, g_small,
                    sgrad, acum, bcum, conv_h, conv_l, rb_h, rb_l, eb_h, eb_l, tot, gath, halo, prevx, slow, bw, rb):
    L, CH = rec.shape
    gconv = sgrad
    q = lax.axis_index("ctx")
    tail = None
    rows_dot(sgrad.at[pl.ds(0, L)], mid_low, w_out)
    for v in slow:
        v.ref()
    if g.Q > 1:
        tail = wire.copy(rec.at[pl.ds(L - 8, 8)], prevx, {"ctx": (q + 1) % g.Q})
        tail.start()
    sub = lax.broadcasted_iota(jnp.int32, (GROUP, 1), 0)
    chunks = L // ROWS

    def chunk(j, carry):
        ua, ub = carry
        r0 = (chunks - 1 - j) * ROWS
        gm = sgrad[pl.ds(r0, ROWS)]
        act, slope = gelu_both(branch[pl.ds(r0, ROWS)])
        branch_low[pl.ds(r0, ROWS)] = (gm * state[pl.ds(r0, ROWS)] * slope).astype(BF16)
        sg = gm * act
        sgrad[pl.ds(r0, ROWS)] = sg
        dec = jnp.exp(-DECAY_SCALE * rate[pl.ds(r0, ROWS)] * vecs[SOFT : SOFT + 1])
        sg = dec * sg
        for n in reversed(range(ROWS // GROUP)):
            A = dec[n * GROUP : (n + 1) * GROUP]
            B = sg[n * GROUP : (n + 1) * GROUP]
            for step in (1, 2, 4):
                keep = sub < GROUP - step
                As = jnp.where(keep, row_shift(A, -step), 1.0)
                Bs = jnp.where(keep, row_shift(B, -step), 0.0)
                B = B + A * Bs
                A = A * As
            B = B + A * ub
            A = A * ua
            acum[pl.ds(r0 + n * GROUP, GROUP)] = A
            bcum[pl.ds(r0 + n * GROUP, GROUP)] = B
            ua = A[0:1]
            ub = B[0:1]
        return ua, ub

    yield
    ua, ub = jnp.ones((1, CH), F32), jnp.zeros((1, CH), F32)
    for i in range(chunks):
        ua, ub = chunk(i, (ua, ub))
        yield
    tot[0:1] = ua
    tot[1:2] = ub
    arriving = jnp.zeros((1, CH), F32)
    if g.Q > 1:
        swap = swap_edges(g, wire, tot, gath)
        next(swap)
        for _ in range(3):
            yield
        run(swap)
        for d in reversed(range(1, g.Q)):
            new = gath[d, 0:1] * arriving + gath[d, 1:2]
            arriving = jnp.where(d > q, new, arriving)
        tail.wait()
    acum[L:] = jnp.ones((8, CH), F32)
    bcum[L:] = jnp.zeros((8, CH), F32)
    zero = jnp.zeros((1, CH), F32)
    if g.Q > 1:
        prev_rows = jnp.where(q > 0, prevx[...], 0.0)
    else:
        prev_rows = jnp.zeros((8, CH), F32)

    def back(i, carry):
        gdec, gbr, gbe, gshift, gt0, gt1, gt2, gt3, last_state, last_rec = carry
        r0 = i * ROWS
        aw = row_shift(acum[pl.ds(r0, ROWS + 8)], -1)[:ROWS]
        bw = row_shift(bcum[pl.ds(r0, ROWS + 8)], -1)[:ROWS]
        car = sgrad[pl.ds(r0, ROWS)] + bw + aw * arriving
        st = state[pl.ds(r0, ROWS)]
        prev = row_shift(jnp.concatenate([last_state, st], axis=0), 1)[8:]
        gr = rate[pl.ds(r0, ROWS)]
        ge = entry[pl.ds(r0, ROWS)]
        c = conv[pl.ds(r0, ROWS)]
        soft = vecs[SOFT : SOFT + 1]
        log = -DECAY_SCALE * gr * soft
        dec = jnp.exp(log)
        scale = jnp.sqrt(minus_expm1(2.0 * log))
        ec = ge * c
        glog = car * prev * dec - car * ec * dec * dec / scale
        glr = 8.0 * glog * gr
        gdec = gdec + jnp.sum(glr, axis=0, keepdims=True)
        rb = -glr * soft * (1.0 - gr)
        cs = car * scale
        eb = cs * ec * (1.0 - ge)
        gbr = gbr + jnp.sum(rb, axis=0, keepdims=True)
        gbe = gbe + jnp.sum(eb, axis=0, keepdims=True)
        rh, rl = halves(rb)
        eh, el = halves(eb)
        ch, cl = halves(c)
        rb_h[pl.ds(r0, ROWS)] = rh
        rb_l[pl.ds(r0, ROWS)] = rl
        eb_h[pl.ds(r0, ROWS)] = eh
        eb_l[pl.ds(r0, ROWS)] = el
        conv_h[pl.ds(r0, ROWS)] = ch
        conv_l[pl.ds(r0, ROWS)] = cl
        wr, we = w_rate[...], w_entry[...]
        gc = cs * ge + dot_rows(rh, wr) + dot_rows(rl, wr) + dot_rows(eh, we) + dot_rows(el, we)
        gconv[pl.ds(r0, ROWS)] = gc
        gshift = gshift + jnp.sum(gc, axis=0, keepdims=True)
        x = rec[pl.ds(r0, ROWS)]
        wide = jnp.concatenate([last_rec, x], axis=0)
        gts = [gt0, gt1, gt2, gt3]
        for k in range(4):
            xk = x if k == 0 else row_shift(wide, k)[8:]
            gts[k] = gts[k] + jnp.sum(gc * xk, axis=0, keepdims=True)
        return (gdec, gbr, gbe, gshift, *gts, st[ROWS - 8 :], x[ROWS - 8 :])

    yield
    carry = (zero,) * 8 + (edge[...], prev_rows)
    for i in range(chunks):
        carry = back(i, carry)
        yield
    gdec, gbr, gbe, gshift, gt0, gt1, gt2, gt3 = carry[:8]
    if g.Q > 1:
        cp = wire.copy(gconv.at[pl.ds(0, 8)], halo, {"ctx": (q + g.Q - 1) % g.Q})
        cp.start()
    gdec = gdec * vecs[SLOPE : SLOPE + 1]
    srows = small_rows(rb)
    for k, v in enumerate((gt0, gt1, gt2, gt3, gshift, gbr, gbe, gdec)):
        tot[k : k + 1] = v
    for j in range(bw // rb):
        g_small[j * srows + 2 * rb : j * srows + 2 * rb + 8] = tot[...]
        g_small[j * srows + 2 * rb + 8 : (j + 1) * srows] = jnp.zeros((srows - 2 * rb - 8, CH), F32)
    yield

    def product(h, l):
        return dot_tokens(conv_h[...], h[...]) + dot_tokens(conv_l[...], h[...]) + dot_tokens(conv_h[...], l[...])

    head = lax.broadcasted_iota(jnp.int32, (bw, CH), 1) // bw

    def diagonal(dense):
        total = jnp.zeros((bw, CH), F32)
        for h in range(CH // bw):
            total = total + jnp.where(head == h, dense[h * bw : (h + 1) * bw], 0.0)
        return total

    for off, (h, l) in ((0, (rb_h, rb_l)), (rb, (eb_h, eb_l))):
        block = diagonal(product(h, l))
        for j in range(bw // rb):
            g_small[j * srows + off : j * srows + off + rb] = block[j * rb : (j + 1) * rb]
        yield
    if g.Q > 1:
        cp.wait()
        gconv[L:] = jnp.where(q < g.Q - 1, halo[...], 0.0)
    else:
        gconv[L:] = jnp.zeros((8, CH), F32)

    def last(i, _):
        r0 = pl.multiple_of(i * ROWS, ROWS)
        wide = gconv[pl.ds(r0, ROWS + 8)]
        total = vecs[TAPS : TAPS + 1] * wide[:ROWS]
        for k in range(1, 4):
            total = total + vecs[TAPS + k : TAPS + k + 1] * row_shift(wide, -k)[:ROWS]
        rec_low[pl.ds(r0, ROWS)] = total.astype(BF16)
        return 0

    lax.fori_loop(0, chunks, last, 0)
    yield


def back_call(g, mid_low, w_out, branch, rec, conv, rate, entry, state, edge, w_rate, w_entry, vecs, bw, rb, middle,
              cot, live, hidden, w_down, mixed, cid):
    L, CH = rec.shape
    half, width = middle.shape
    low = jax.ShapeDtypeStruct((L, CH), BF16)
    F = hidden.shape[1]
    rows = width // g.N
    count = g.Q + 2 + tp_count(g, L) + 2 * reduce_count(g)
    operands = [mid_low, w_out, branch, rec, conv, rate, entry, state, edge, w_rate, w_entry, vecs,
                middle, cot, live, hidden, w_down, mixed]

    def kernel(*refs):
        ins, (middle, cot, live, hidden, w_down, mixed) = refs[:12], refs[12:18]
        slow = [v for v in ins if isinstance(v, Later)]
        outs, (output, g_down, g_out) = refs[18:21], refs[21:24]
        bufs = refs[24:37]
        cot_t, term, sendbuf, recvbuf, *more = refs[37:]
        mid_t = cot_t
        send, recv = more[-2:]
        greet(ctx_peers(g) + tp_peers(g) + plane_peers(g))
        wire = Wire(send, recv)
        ins = [v.dst if isinstance(v, Later) else v for v in ins]

        def z():
            yield
            body = mlp_out_body((hidden.ref(), w_down.ref(), middle, live), (output,))
            yield from tp_steps(g, wire, L, output, *body, (term, sendbuf, recvbuf))

        def down():
            yield from turn_steps(rows, cot_t, cot, live)
            hidden.ref()
            yield from reduce_steps(g, wire, [(product_term(cot.dst, cot_t, hidden.dst, rows, live), g_down, more[0:3])])

        down_steps = down()
        if needs_turn(rows):
            for _ in range(len(range(0, width, 512)) + g.C * g.A * g.B):
                next(down_steps)

        def out():
            yield from turn_steps(rows, mid_t, ins[0])
            mixed.ref()
            yield from reduce_steps(g, wire, [(product_term(ins[0], mid_t, mixed.dst, rows), g_out, more[3:6])])

        braid(
            chain(backward_steps(g, wire, *ins, *outs, *bufs, slow, bw, rb), iter(range(4))),
            (z(), BACK_Z),
            (down_steps, BACK_DOWN),
            (out(), BACK_OUT),
        )

    return call(
        kernel,
        operands,
        [low, low, jax.ShapeDtypeStruct((bw // rb * small_rows(rb), CH), F32), jax.ShapeDtypeStruct((L, width), BF16),
         jax.ShapeDtypeStruct((rows, F), F32), jax.ShapeDtypeStruct((rows, CH), F32)],
        [
            pltpu.VMEM((L + 8, CH), F32),
            pltpu.VMEM((L + 8, CH), F32),
            pltpu.VMEM((L + 8, CH), F32),
        ]
        + [pltpu.VMEM((L, CH), BF16)] * 6
        + [
            pltpu.VMEM((8, CH), F32),
            pltpu.VMEM((g.Q, 8, CH), F32),
            pltpu.VMEM((8, CH), F32),
            pltpu.VMEM((8, CH), F32),
        ]
        + turn_scratch(rows, width, L)
        + tp_bufs(g, L, width)
        + reduce_bufs(g, rows, F)
        + reduce_bufs(g, rows, CH)
        + sems(count),
        cid,
        "rec_backward",
        later=(15, 16, 13, 17, 3, 4, 6),
    )


def reduce_count(g):
    ring = 0
    for nf, ng in ((g.A, g.B), (g.B, g.A)):
        ring += (nf - 1) * ng + (ng - 1)
    return ring + (g.C - 1) * g.A * g.B


def reduce_bufs(g, rows, width):
    nb = g.A * g.B
    arrivals = reduce_count(g) - (g.C - 1) * nb
    return [
        pltpu.VMEM((nb, rows, width), BF16),
        pltpu.VMEM((nb, rows, width), BF16),
        pltpu.VMEM((max(1, arrivals), rows // 2, width), BF16),
    ]


def reduce_steps(g, wire, items):
    a, b, c = g.me()
    sends = []

    def start(src, dst, dev):
        cp = wire.copy(src, dst, dev)
        cp.start()
        sends.append(cp)
        return cp

    nb = g.A * g.B

    def owner(k, core):
        return g.block((a + g.A - k // g.B) % g.A, (b + g.B - k % g.B) % g.B, core)

    def each_tile(width, fn):
        fn(slice(None))

    rings = [(g.A, g.B), (g.B, g.A)]
    devs = [
        (g.dev((a + 1) % g.A, b, c), g.dev(a, (b + 1) % g.B, c)),
        (g.dev(a, (b + 1) % g.B, c), g.dev((a + 1) % g.A, b, c)),
    ]

    def slot(h, df, dg):
        return df * g.B + dg if h == 0 else dg * g.B + df

    bases = []
    state = []
    for term, out, (to_sib, sums, land) in items:
        half = out.shape[0] // 2
        base = wire.used
        bases.append(base)
        if g.C == 2:
            wire.used += nb
            for k in [(i + 1) % nb for i in range(nb)]:

                def tile(cols):
                    to_sib[k, :, cols] = term(owner(k, 1 - c), cols).astype(BF16)

                each_tile(out.shape[1], tile)
                wire.at(base + k, to_sib.at[k], sums.at[k], g.dev(a, b, 1 - c)).start()
                yield
        used = 0
        first = ({}, {})
        for k in [(i + 1) % nb for i in range(nb)]:
            if g.C == 2:
                wire.at(base + k, to_sib.at[k], sums.at[k], g.dev(a, b, 1 - c)).wait_recv()

            def tile(cols):
                s = term(owner(k, c), cols)
                if g.C == 2:
                    s = s + sums[k, :, cols].astype(F32)
                if k == 0:
                    out[:, cols] = s
                else:
                    sums[k, :, cols] = s.astype(BF16)

            each_tile(out.shape[1], tile)
            for h in (0, 1):
                nf, ng = rings[h]
                df, dg = (k // g.B, k % g.B) if h == 0 else (k % g.B, k // g.B)
                if nf > 1 and df == 1:
                    first[h][dg] = (start(sums.at[k, pl.ds(h * half, half)], land.at[used], devs[h][0]), used)
                    used += 1
            yield
        state.append([first, used])

    def add(out, sums, k, h, half, arrived):
        at = slice(h * half, (h + 1) * half)
        if k == 0:
            out[at] = out[at] + arrived.astype(F32)
        else:
            sums[k, at] = (sums[k, at].astype(F32) + arrived.astype(F32)).astype(BF16)

    seconds = []
    for (term, out, (to_sib, sums, land)), st in zip(items, state):
        half = out.shape[0] // 2
        first, used = st
        second = [None, None]
        for h in (0, 1):
            nf, ng = rings[h]
            for i in range(1, nf):
                df = (i + 1) % nf
                for dg in [d % ng for d in range(1, ng + 1)]:
                    cp, at = first[h][dg]
                    cp.wait_recv()
                    k = slot(h, df, dg)
                    add(out, sums, k, h, half, land[at])
                    if i < nf - 1:
                        first[h][dg] = (start(sums.at[k, pl.ds(h * half, half)], land.at[used], devs[h][0]), used)
                        used += 1
                    elif dg == 1 and ng > 1:
                        second[h] = (start(sums.at[k, pl.ds(h * half, half)], land.at[used], devs[h][1]), used)
                        used += 1
            if nf == 1 and ng > 1:
                k = slot(h, 0, 1)
                second[h] = (start(sums.at[k, pl.ds(h * half, half)], land.at[used], devs[h][1]), used)
                used += 1
        seconds.append([second, used])
        yield
    for (term, out, (to_sib, sums, land)), (second, used) in zip(items, seconds):
        half = out.shape[0] // 2
        for h in (0, 1):
            nf, ng = rings[h]
            for j in range(1, ng):
                cp, at = second[h]
                cp.wait_recv()
                k = slot(h, 0, (j + 1) % ng)
                add(out, sums, k, h, half, land[at])
                if j < ng - 1:
                    second[h] = (start(sums.at[k, pl.ds(h * half, half)], land.at[used], devs[h][1]), used)
                    used += 1
        yield
    for cp in sends:
        cp.wait_send()
    if g.C == 2:
        for (term, out, (to_sib, sums, land)), base in zip(items, bases):
            for k in range(nb):
                wire.at(base + k, to_sib.at[k], sums.at[k], g.dev(a, b, 1 - c)).wait_send()


def needs_turn(rows):
    return rows % 128 != 0


def turn_scratch(rows, width, L):
    return [pltpu.VMEM((width, L) if needs_turn(rows) else (16, 128), BF16)]


def product_term(left, turned, right, rows, mask=None):
    def term(block, cols):
        at = pl.ds(pl.multiple_of(block * rows, rows), rows)
        if needs_turn(rows):
            return dot(turned[at], right[:, cols])
        v = left[:, at]
        if mask is not None:
            v = (v.astype(F32) * mask[...]).astype(BF16)
        return dot_tokens(v, right[:, cols])

    return term


def turn_steps(rows, turned, left, mask=None):
    if isinstance(left, Later):
        left = left.ref()
    if needs_turn(rows):
        yield from transpose_steps(turned, left, mask)


def given_term(part, rows):
    def term(block, cols):
        return part[pl.ds(pl.multiple_of(block * rows, rows), rows), cols]

    return term


def mlp_back_call(g, low_two, gate_low, up_low, w_gate, w_up, middle, cot, live, gain, cid):
    L, width = low_two.shape
    F = gate_low.shape[1]
    half = L // 2
    rows = width // g.N
    count = tp_count(g, L) + 2 * reduce_count(g)
    grad = jax.ShapeDtypeStruct((rows, F), F32)

    def kernel(low_two, gate_low, up_low, w_gate, w_up, middle, cot, live, gain,
               mid_low, grad_middle, grad_gain, g_gate, g_up,
               two_t, term, sendbuf, recvbuf, *refs):
        send, recv = refs[-2:]
        bufs = refs[:-2]
        greet(plane_peers(g) + tp_peers(g))
        wire = Wire(send, recv)
        gate_low, up_low, w_gate, w_up, middle, cot = (v.ref() for v in (gate_low, up_low, w_gate, w_up, middle, cot))
        back = mlp_back_body((gate_low, up_low, w_gate, w_up, middle, cot, live, gain), (mid_low, grad_middle, grad_gain))

        def gate():
            yield from turn_steps(rows, two_t, low_two)
            yield from reduce_steps(g, wire, [(product_term(low_two.dst, two_t, gate_low, rows), g_gate, bufs[0:3])])

        def up():
            yield from reduce_steps(g, wire, [(product_term(low_two.dst, two_t, up_low, rows), g_up, bufs[3:6])])

        braid(
            tp_steps(g, wire, L, mid_low, *back, (term, sendbuf, recvbuf)),
            (gate(), MLP_GATE),
            (up(), MLP_UP),
        )

    scratch = turn_scratch(rows, width, L) + tp_bufs(g, L, width)
    for _ in range(2):
        scratch += reduce_bufs(g, rows, F)
    return call(
        kernel,
        [low_two, gate_low, up_low, w_gate, w_up, middle, cot, live, gain],
        [jax.ShapeDtypeStruct((L, width), BF16), jax.ShapeDtypeStruct((half, width), F32),
         jax.ShapeDtypeStruct((1, width), F32), grad, grad],
        scratch + sems(count),
        cid,
        "mlp_back",
        later=(1, 3, 2, 4, 0, 5, 6),
    )


def plane_others(g):
    s, q = lax.axis_index("shard"), lax.axis_index("ctx")
    me = s * g.Q + q
    out = []
    for k in range(1, g.N):
        d = (me + k) % g.N
        out.append({"shard": d // g.Q, "ctx": d % g.Q})
    return me, out


def total_steps(g, wire, mine, land_t, land_p, out):
    t = lax.axis_index("tp")
    me, others = plane_others(g)
    land_t[t] = mine[...]
    cps = [wire.copy(mine, land_t.at[t], {"tp": (t + k) % g.T}) for k in range(1, g.T)]
    for cp in cps:
        cp.start()
    yield
    for cp in cps:
        cp.wait()
    total = land_t[0]
    for d in range(1, g.T):
        total = total + land_t[d]
    mine[...] = total
    land_p[me] = total
    cps = [wire.copy(mine, land_p.at[me], d) for d in others]
    for cp in cps:
        cp.start()
    yield
    for cp in cps:
        cp.wait()
    total = land_p[0]
    for d in range(1, g.N):
        total = total + land_p[d]
    out[...] = total


def rec_back_call(g, branch_low, rec_low, w_branch, w_rec, x, grad_middle, gain, part_two, low_one, small, cid):
    L, width = x.shape
    CH = branch_low.shape[1]
    rows = width // g.N
    srows = small.shape[0] // g.N
    shapes = [(rows, CH), (rows, CH), (srows, small.shape[1])]
    count = tp_count(g, L) + len(shapes) * reduce_count(g) + g.T + g.N

    def kernel(branch_low, rec_low, w_branch, w_rec, x, grad_middle, gain, part_two, low_one, small,
               input_grad, gains, g_branch, g_rec, g_small,
               part_one, one_t, both, land_t, land_p, term, sendbuf, recvbuf, *refs):
        send, recv = refs[-2:]
        bufs = refs[:-2]
        t = lax.axis_index("tp")
        greet(plane_others(g)[1] + [{"tp": (t + k) % g.T} for k in range(1, g.T)])
        wire = Wire(send, recv)
        branch_low, rec_low, w_branch, w_rec, x, grad_middle = (
            v.ref() for v in (branch_low, rec_low, w_branch, w_rec, x, grad_middle)
        )
        back = rec_back_body((branch_low, rec_low, w_branch, w_rec, x, grad_middle, gain), (input_grad, part_one))

        def one(term, out, bufs):
            yield from reduce_steps(g, wire, [(term, out, bufs)])

        def branch():
            yield from turn_steps(rows, one_t, low_one)
            yield from one(product_term(low_one.dst, one_t, branch_low, rows), g_branch, bufs[0:3])

        def main():
            steps = tp_steps(g, wire, L, input_grad, *back, (term, sendbuf, recvbuf))
            for _ in range(L // 2 // PIECE + END["take_far"]):
                next(steps)
                yield
            both[:, :width] = part_one[...]
            both[:, width:] = part_two[...]
            totals = total_steps(g, wire, both, land_t, land_p, gains)
            next(totals)
            for _ in steps:
                next(totals, None)
                yield
            run(totals)

        braid(
            main(),
            (branch(), REC_BRANCH),
            (one(product_term(low_one.dst, one_t, rec_low, rows), g_rec, bufs[3:6]), REC_REC),
            (one(given_term(small, srows), g_small, bufs[6:9]), REC_SMALL),
        )

    scratch = [pltpu.VMEM((1, width), F32)] + turn_scratch(rows, width, L)
    scratch += [pltpu.VMEM((1, 2 * width), F32), pltpu.VMEM((g.T, 1, 2 * width), F32), pltpu.VMEM((g.N, 1, 2 * width), F32)]
    scratch += tp_bufs(g, L, width)
    for s in shapes:
        scratch += reduce_bufs(g, *s)
    return call(
        kernel,
        [branch_low, rec_low, w_branch, w_rec, x, grad_middle, gain, part_two, low_one, small],
        [jax.ShapeDtypeStruct((L, width), BF16), jax.ShapeDtypeStruct((1, 2 * width), F32)]
        + [jax.ShapeDtypeStruct(s, F32) for s in shapes],
        scratch + sems(count),
        cid,
        "rec_back",
        later=(0, 2, 1, 3, 8, 4, 5),
    )


def settle(arrays):
    n = len(arrays)

    def kernel(*refs):
        ins, outs, kept, sem = refs[:n], refs[n : 2 * n], refs[2 * n : 3 * n], refs[3 * n]
        cps = [pltpu.make_async_copy(ins[k], kept[k], sem.at[k]) for k in range(n)]
        back = [pltpu.make_async_copy(kept[k], outs[k], sem.at[n + k]) for k in range(n)]
        for cp in cps:
            cp.start()
        for k in range(n):
            cps[k].wait()
            back[k].start()
        for cp in back:
            cp.wait()

    return pl.pallas_call(
        kernel,
        out_shape=[jax.ShapeDtypeStruct(v.shape, v.dtype) for v in arrays],
        in_specs=[ANY] * n,
        out_specs=[ANY] * n,
        scratch_shapes=[pltpu.VMEM(v.shape, v.dtype) for v in arrays] + [pltpu.SemaphoreType.DMA((2 * n,))],
        compiler_params=pltpu.CompilerParams(vmem_limit_bytes=VMEM_LIMIT),
        name="settle",
    )(*arrays)


def up_to(n, k):
    return -(-n // k) * k


def local(g, inputs, lengths, cotangent, norm1_gain, branch_weight, rec_in_weight, conv_weight, conv_bias,
          rgate_weight, rgate_bias, igate_weight, igate_bias, decay_param, out_weight, norm2_gain,
          mlp_gate_weight, mlp_up_weight, mlp_down_weight):
    slots, block_len, width = inputs.shape
    L = slots * block_len
    N = g.N
    heads, rb, bw = rgate_weight.shape
    ch = heads * bw
    taps = conv_weight.shape[0]
    prow = pack_rows(rb)[0]

    def across(v):
        return jnp.pad(v, ((0, 0), (0, ch - v.shape[1])))

    vectors = jnp.concatenate([conv_weight] + [p[None] for p in (conv_bias, rgate_bias, igate_bias, decay_param)], axis=0)
    gates, vectors, gains = lax.optimization_barrier(
        (jnp.stack([rgate_weight, igate_weight]), vectors, jnp.concatenate([norm1_gain, norm2_gain]))
    )
    pack = jnp.concatenate(
        [gates.transpose(0, 2, 1, 3).reshape(2 * rb, ch), across(vectors.reshape(2 * taps, -1)), across(gains.reshape(2, -1))],
        axis=0,
    )
    pack = jnp.pad(pack, ((0, prow - pack.shape[0]), (0, 0)))
    x_low = inputs.reshape(L, width)
    cot = cotangent.reshape(L, width)
    positions = lax.axis_index("ctx") * block_len + jnp.arange(block_len, dtype=jnp.int32)
    live = (positions[None, :] < lengths[:, None]).astype(F32).reshape(L, 1)
    (low_one, branch_pre, rec_pre, mixed, conv, rate, entry, state, edge, low_two, middle, w_rate, w_entry, vecs, gains,
     w_rec, w_branch, w_out, w_gate, w_up, w_down, gate_pre, up_pre, hidden) = front_call(
        g, pack, rec_in_weight, branch_weight, out_weight, [mlp_gate_weight, mlp_up_weight, mlp_down_weight], x_low, bw, rb, 0
    )
    gain_one, gain_two = gains[0:1], gains[1:2]
    act, slope = gelu_both(gate_pre)
    grad_low = (cot.astype(F32) * live).astype(BF16)
    grad_hidden = dot(grad_low, w_down)
    gate_low = (grad_hidden * up_pre * slope).astype(BF16)
    up_low = (grad_hidden * act).astype(BF16)
    mid_low, grad_middle, part_two, g_gate, g_up = mlp_back_call(
        g, low_two, gate_low, up_low, w_gate, w_up, middle, cot, live, gain_two, 2
    )
    branch_low, rec_low, flat, output, g_down, g_out = back_call(
        g, mid_low, w_out, branch_pre, rec_pre, conv, rate, entry, state, edge, w_rate, w_entry, vecs, bw, rb, middle,
        cot, live, hidden, w_down, mixed, 3
    )
    input_grad, gains, g_branch, g_rec, g_small = rec_back_call(
        g, branch_low, rec_low, w_branch, w_rec, x_low, grad_middle, gain_one, part_two, low_one, flat, 4
    )
    me = lax.axis_index("shard") * g.Q + lax.axis_index("ctx")
    m = width // N
    gains = [lax.dynamic_slice(gains, (0, k * width + me * m), (1, m)).reshape(m) for k in range(2)]
    g_rate = g_small[:rb].reshape(rb, heads, bw).transpose(1, 0, 2)
    g_entry = g_small[rb : 2 * rb].reshape(rb, heads, bw).transpose(1, 0, 2)
    rest = lax.dynamic_slice(g_small[2 * rb : 2 * rb + 8].reshape(8, heads, bw), (0, 0, me * rb), (8, heads, rb))
    shape = (slots, block_len, width)
    output, input_grad, g_branch, g_rec, g_out, g_gate, g_up, g_down = settle(
        [output, input_grad, g_branch, g_rec, g_out, g_gate, g_up, g_down]
    )
    return (
        output.reshape(shape), input_grad.reshape(shape), gains[0], g_branch, g_rec, rest[:taps], rest[4],
        g_rate, rest[5], g_entry, rest[6], rest[7], g_out, gains[1], g_gate, g_up, g_down,
    )


def solution(mesh):
    plane = ("shard", "ctx")
    rows, cols = P(plane), P(plane, "tp")
    tok, gate, chan = P("shard", "ctx", None), P("tp", plane, None), P("tp", plane)
    taps = P(None, "tp", plane)
    params = (rows, cols, cols, taps, chan, gate, chan, gate, chan, chan, cols, rows, cols, cols, cols)
    return jax.shard_map(
        functools.partial(local, Grid(mesh)),
        mesh=mesh,
        in_specs=(tok, P("shard"), tok) + params,
        out_specs=(tok, tok) + params,
        check_vma=False,
    )
```
